32 devices in a mesh: dp: 8 (over y, x, core), stream: 4 (over z).
Axes of the slice: x: 2, y: 2, z: 4, core: 2. Of those that a mesh axis runs over, the one named last changes fastest.
Arguments:
- history: bfloat16 [11, 8192, 2048], P(None, 'dp', 'stream'), may hold values from -6 to 6
- mix_in: bfloat16 [2048, 44], replicated, may hold values from -0.125 to 0.125
- mix_out: bfloat16 [44, 44], replicated, may hold values from -0.875 to 0.875
- mix_static: float32 [4, 11], replicated, may hold values from 0.05 to 0.6
- stream_gain: float32 [3, 2048], P(None, 'stream'), may hold values from 0.1 to 1.9
- qkv_weight: bfloat16 [2048, 3, 2048], P(None, None, 'stream'), may hold values from -0.125 to 0.125
- out_weight: bfloat16 [2048, 2048], P(None, 'stream'), may hold values from -2 to 2
- mlp_gain: float32 [2048], replicated, may hold values from 0.1 to 1.9
- up_weight: bfloat16 [2048, 8192], P(None, 'stream'), may hold values from -0.125 to 0.125
- down_weight: bfloat16 [2048, 8192], P(None, 'stream'), may hold values from -0.0625 to 0.0625
- out_grad: bfloat16 [8192, 2048], P('dp', 'stream'), may hold values from -6 to 6
- seq_group: int32 [8], P('dp'), may hold values from 0 to 21
- group_weight: int32 [22], replicated, may hold values from 1 to 4
Outputs:
- output: bfloat16 [8192, 2048], P('dp', 'stream')
- history_grad: bfloat16 [11, 8192, 2048], P(None, 'dp', 'stream')
- mix_in_grad: float32 [2048, 44], P('stream')
- mix_out_grad: float32 [44, 44], replicated
- mix_static_grad: float32 [4, 11], replicated
- stream_gain_grad: float32 [3, 2048], P(None, 'stream')
- qkv_grad: float32 [2048, 3, 2048], P('dp', None, 'stream')
- out_weight_grad: float32 [2048, 2048], P('dp', 'stream')
- mlp_gain_grad: float32 [2048], replicated
- up_grad: float32 [2048, 8192], P('dp', 'stream')
- down_grad: float32 [2048, 8192], P('dp', 'stream')
The draws below stay inside these ranges and needn't reach their ends.
All inputs are finite; a program needn't handle non-finite values.
Results may differ from the reference program's by a relative error of at most 0.014.
The reference program's roundings to bfloat16 on the way count: a program that leaves them out, or rounds other values in their place, can miss the bound.
Values may be sent and summed in bfloat16 or wider, within the bound.
No kernel may reach another device: no remote copies, remote signals or barrier semaphores. Data moves between devices by JAX's collectives and lax.ppermute only.
A program may use at most 320 MiB of HBM per device.

```python
import jax
import jax.numpy as jnp
from jax import lax

D = 2048
HEADS = 16
HEAD_DIM = 128
FF = 8192
HIST = 11
MIXH = 44
GROUPS = 22
SEQ = 1024
SEQS = 8
TOKENS = 8192


def with_ends(drawn, key, least, top_value):
    shape = drawn.shape
    spot = [jax.random.randint(jax.random.fold_in(key, axis), (), 0, shape[axis]) for axis in range(len(shape))]
    drawn = drawn.at[tuple(spot)].set(least)
    longest = shape.index(max(shape))
    spot[longest] = (spot[longest] + 1) % shape[longest]
    return drawn.at[tuple(spot)].set(top_value)


def block_levels(key, shape, cuts, smallest, largest):
    factor_of = 1.0
    for position, blocks in cuts:
        heights = jax.random.uniform(jax.random.fold_in(jax.random.fold_in(key, 6), position), (blocks,), jnp.float32, smallest / len(cuts), largest / len(cuts))
        factor_of = factor_of * jnp.repeat(jnp.exp(heights), shape[position] // blocks).reshape((-1,) + (1,) * (len(shape) - 1 - position))
    return factor_of


def gaussian(stream_key, dims, width, bound, pieces=(), held_as=jnp.bfloat16):
    array = jax.random.normal(stream_key, dims, jnp.float32) * width
    if len(pieces) > 0:
        array = block_levels(stream_key, dims, pieces, -0.22, 0.18) * array
    return jnp.clip(array, min=-bound, max=bound).astype(held_as)


def setup_inputs(seed: int = 0) -> dict:
    key_list = jax.random.split(jax.random.key(seed), 14)
    history = gaussian(key_list[0], (HIST, TOKENS, D), 1.0, 6.0, ((1, 8), (2, 4)))
    mix_in = gaussian(key_list[1], (D, MIXH), D ** -0.5, 0.125)
    mix_out = gaussian(key_list[2], (MIXH, 4 * HIST), MIXH ** -0.5, 0.875)
    mix_static = jnp.clip(jax.random.uniform(key_list[3], (4, HIST), jnp.float32, 0.05, 0.6), 0.05, 0.6)
    stream_gain = jnp.clip(1.0 + 0.18 * jax.random.normal(key_list[4], (3, D), jnp.float32), 0.1, 1.9)
    qkv_weight = gaussian(key_list[5], (D, 3, D), D ** -0.5, 0.125, ((2, 4),))
    out_weight = gaussian(key_list[6], (D, D), (4 * D // SEQ) ** -0.5, 2.0, ((1, 4),))
    mlp_gain = jnp.clip(1.0 + 0.18 * jax.random.normal(key_list[7], (D,), jnp.float32), 0.1, 1.9)
    up_weight = gaussian(key_list[8], (D, FF), D ** -0.5, 0.125, ((1, 4),))
    down_weight = gaussian(key_list[9], (D, FF), FF ** -0.5, 0.0625, ((1, 4),))
    out_grad = gaussian(key_list[10], (TOKENS, D), 1.0, 6.0, ((0, 8), (1, 4)))
    seq_group = with_ends(jax.random.randint(key_list[11], (SEQS,), 0, GROUPS), jax.random.fold_in(key_list[11], 1), 0, GROUPS - 1).astype(jnp.int32)
    group_weight = with_ends(jax.random.randint(key_list[12], (GROUPS,), 1, 5), jax.random.fold_in(key_list[12], 1), 1, 4).astype(jnp.int32)
    return dict(history=history, mix_in=mix_in, mix_out=mix_out, mix_static=mix_static, stream_gain=stream_gain, qkv_weight=qkv_weight, out_weight=out_weight, mlp_gain=mlp_gain, up_weight=up_weight, down_weight=down_weight, out_grad=out_grad, seq_group=seq_group, group_weight=group_weight)


HIGH = lax.Precision.HIGHEST
EPS_NORM = 1e-05
EPS_MIX = 1e-06
COT_SCALE = 0.4

@jax.custom_vjp
def low(v):
    return lax.optimization_barrier(v.astype(jnp.bfloat16)).astype(jnp.float32)

@jax.custom_vjp
def low_back(v):
    return v

def low_keep(v):
    return (low(v), None)

def low_pass(kept, grad):
    return (grad,)

def back_keep(v):
    return (v, None)

def back_low(kept, grad):
    return (low(grad),)
low.defvjp(low_keep, low_pass)
low_back.defvjp(back_keep, back_low)

def product(former, latter):
    return jnp.dot(former, latter, precision=HIGH, preferred_element_type=jnp.float32)

def product_t(former, latter):
    return lax.dot_general(former, latter, (((1,), (1,)), ((), ())), precision=HIGH, preferred_element_type=jnp.float32)

def layer_norm(values, norm_gain):
    center = values - lax.optimization_barrier(jnp.mean(values, axis=-1, keepdims=True))
    variance = lax.optimization_barrier(jnp.mean(jnp.square(center), axis=-1, keepdims=True))
    return center * lax.rsqrt(variance + EPS_NORM) * norm_gain

def attend_head(operands):
    queries, keys_head, values = operands
    scores = low_back(product_t(queries, keys_head) * HEAD_DIM ** (-0.5))
    row_index = lax.broadcasted_iota(jnp.int32, (SEQ, SEQ), 0)
    key_index = lax.broadcasted_iota(jnp.int32, (SEQ, SEQ), 1)
    scores = jnp.where(key_index <= row_index, scores, -1e+30)
    attn_probs = jax.nn.softmax(scores, axis=-1)
    return product(low(attn_probs), values)

def forward(history, mix_in, mix_out, mix_static, stream_gain, qkv_weight, out_weight, mlp_gain, up_weight, down_weight):
    last_layer = history[HIST - 1]
    mix_scale = lax.rsqrt(lax.optimization_barrier(jnp.mean(jnp.square(last_layer), axis=-1, keepdims=True)) + EPS_MIX)
    mix_pre = mix_scale * product(last_layer, mix_in)
    mix_act = jax.nn.gelu(mix_pre, approximate=False)
    mix_coef = (product(mix_act, mix_out) + mix_static.reshape(1, -1)).reshape(SEQ, 4, HIST)
    streams = jnp.einsum('tsj,jtd->std', mix_coef, history, precision=HIGH)
    head_list = []
    for stream_idx in range(3):
        normed = low(layer_norm(streams[stream_idx], stream_gain[stream_idx]))
        projected = low(low_back(product(normed, qkv_weight[:, stream_idx, :])))
        head_list.append(projected.reshape(SEQ, HEADS, HEAD_DIM).transpose(1, 0, 2))
    attended = lax.map(jax.checkpoint(attend_head), (head_list[0], head_list[1], head_list[2]))
    heads_out = low(low_back(attended.transpose(1, 0, 2).reshape(SEQ, D)))
    residual = streams[3] + low_back(product_t(heads_out, out_weight))
    normed_mlp = low(layer_norm(residual, mlp_gain))
    hidden_pre = low_back(product(normed_mlp, up_weight))
    hidden = low(jax.nn.gelu(hidden_pre, approximate=False))
    return residual + low_back(product_t(hidden, down_weight))

def reference(history, mix_in, mix_out, mix_static, stream_gain, qkv_weight, out_weight, mlp_gain, up_weight, down_weight, out_grad, seq_group, group_weight):
    params = (mix_in.astype(jnp.float32), mix_out.astype(jnp.float32), mix_static.astype(jnp.float32), stream_gain.astype(jnp.float32), qkv_weight.astype(jnp.float32), out_weight.astype(jnp.float32), mlp_gain.astype(jnp.float32), up_weight.astype(jnp.float32), down_weight.astype(jnp.float32))
    seq_weight = group_weight[seq_group].astype(jnp.float32) * COT_SCALE
    history_seqs = jnp.moveaxis(history.reshape(HIST, SEQS, SEQ, D), 1, 0)
    grad_seqs = out_grad.reshape(SEQS, SEQ, D)

    def one_sequence(totals, inputs):
        hist_seq, grad_seq, weight = inputs
        out_seq, pullback = jax.vjp(forward, hist_seq.astype(jnp.float32), *params)
        grad_list = pullback(grad_seq.astype(jnp.float32) * weight)
        totals = tuple((former + latter for former, latter in zip(totals, grad_list[1:])))
        return (totals, (out_seq.astype(jnp.bfloat16), grad_list[0].astype(jnp.bfloat16)))
    zero_grads = tuple((jnp.zeros_like(param) for param in params))
    totals, seq_results = lax.scan(one_sequence, zero_grads, (history_seqs, grad_seqs, seq_weight))
    seq_outputs, hist_grads = seq_results
    output = seq_outputs.reshape(TOKENS, D)
    history_grad = jnp.moveaxis(hist_grads, 0, 1).reshape(HIST, TOKENS, D)
    mix_in_grad, mix_out_grad, mix_static_grad, stream_gain_grad, qkv_grad, out_weight_grad, mlp_gain_grad, up_grad, down_grad = totals
    return (output, history_grad, mix_in_grad, mix_out_grad, mix_static_grad, stream_gain_grad, qkv_grad, out_weight_grad, mlp_gain_grad, up_grad, down_grad)
```

```python
import functools
import math

import jax
import jax.numpy as jnp
from jax import lax
from jax.experimental import pallas as pl
from jax.experimental.pallas import tpu as pltpu
from jax.sharding import PartitionSpec as P

HEAD_DIM = 128
SEQ = 1024
CHUNKS = 2
SUB = 256

HIGH = lax.Precision.HIGHEST
EPS_NORM = 1e-05
EPS_MIX = 1e-06
COT_SCALE = 0.4
F32 = jnp.float32
BF16 = jnp.bfloat16


def gelu_both(values):
    cdf = 0.5 * (1.0 + lax.erf(values * math.sqrt(0.5)))
    density = jnp.exp(-0.5 * jnp.square(values)) * (1.0 / math.sqrt(2.0 * math.pi))
    return values * cdf, cdf + values * density


def dot_tt(former, latter, dims, precision=None):
    return lax.dot_general(
        former, latter, (dims, ((), ())), precision=precision, preferred_element_type=F32
    )


def contract_rows(former, latter):
    return dot_tt(former, latter, ((0,), (0,)))


def times_transpose(former, latter):
    return dot_tt(former, latter, ((1,), (1,)))


def line_gather(piece, member):
    n = lax.axis_size("stream")
    from_low, from_high = [piece], [piece]
    for step in range(1, n):
        up = [(i, i + 1) for i in range(step - 1, n - 1)]
        down = [(i, i - 1) for i in range(1, n - step + 1)]
        from_low.append(lax.ppermute(from_low[-1], "stream", up))
        from_high.append(lax.ppermute(from_high[-1], "stream", down))
    slots = []
    for slot in range(n):
        value = piece
        for at in range(n):
            if at > slot:
                value = jnp.where(member == at, from_low[at - slot], value)
            elif at < slot:
                value = jnp.where(member == at, from_high[slot - at], value)
        slots.append(value)
    return jnp.concatenate(slots, axis=-1)


def line_scatter(block):
    n = lax.axis_size("stream")
    parts = {}

    def part(idx):
        if idx not in parts:
            parts[idx] = block(idx)
        return parts[idx]

    up = down = None
    for step in range(n - 1):
        up_value, down_value = part(n - 1 - step), part(1 + step)
        if up is not None:
            if n - 1 - step == 1 + step:
                up_value = down_value = up_value + up.astype(F32) + down.astype(F32)
            else:
                up_value = up_value + up.astype(F32)
                down_value = down_value + down.astype(F32)
        up = lax.ppermute(up_value.astype(BF16), "stream", [(i, i + 1) for i in range(step + 1)])
        down = lax.ppermute(
            down_value.astype(BF16), "stream", [(i, i - 1) for i in range(n - 1 - step, n)]
        )
    return part(0) + up.astype(F32) + down.astype(F32)


def butterfly(value, axis, merge=jnp.add):
    n = lax.axis_size(axis)
    span = 1
    while span < n:
        other = lax.ppermute(value, axis, [(i, i ^ span) for i in range(n)])
        value = merge(value, other)
        span *= 2
    return value


def merge_moments(width):
    def start(value):
        state = {"count": width}

        def merge(mine, other):
            half = mine.shape[0] // 2
            gap = mine[:half] - other[:half]
            mean = 0.5 * (mine[:half] + other[:half])
            square = mine[half:] + other[half:] + jnp.square(gap) * (0.5 * state["count"])
            state["count"] *= 2
            return jnp.concatenate([mean, square], axis=0)

        return butterfly(value, "stream", merge)

    return start


def attend_forward_kernel(chunk, q_ref, *refs):
    k_refs, v_refs = refs[: chunk + 1], refs[chunk + 1 : 2 * chunk + 2]
    o_ref, lse_ref = refs[2 * chunk + 2 :]
    rows = q_ref.shape[0]
    keys = jnp.concatenate([ref[...] for ref in k_refs], axis=0)
    values = jnp.concatenate([ref[...] for ref in v_refs], axis=0)
    for sub in range(rows // SUB):
        count = chunk * rows + (sub + 1) * SUB
        span = pl.ds(sub * SUB, SUB)
        scores = times_transpose(keys[:count], q_ref[span, :]) * HEAD_DIM ** (-0.5)
        allowed = lax.broadcasted_iota(jnp.int32, (SUB, SUB), 0) <= lax.broadcasted_iota(
            jnp.int32, (SUB, SUB), 1
        )
        tail = jnp.where(allowed, scores[count - SUB :], -1e30)
        scores = jnp.concatenate([scores[: count - SUB], tail], axis=0) if count > SUB else tail
        top = jnp.max(scores, axis=0, keepdims=True)
        weights = jnp.exp(scores - top)
        total = jnp.sum(weights, axis=0, keepdims=True)
        probs = (weights * (1.0 / total)).astype(BF16)
        lse_ref[0, :, span] = top + jnp.log(total)
        out = contract_rows(values[:count], probs)
        o_ref[span, :] = out.T.astype(BF16)


def attend_forward(queries, keys, values):
    rows, width = queries.shape
    heads = width // HEAD_DIM
    chunk = len(keys) - 1
    spec = pl.BlockSpec((rows, HEAD_DIM), lambda h: (0, h))
    return pl.pallas_call(
        functools.partial(attend_forward_kernel, chunk),
        grid=(heads,),
        in_specs=[spec] * (2 * chunk + 3),
        out_specs=[spec, pl.BlockSpec((1, 1, rows), lambda h: (h, 0, 0))],
        out_shape=[
            jax.ShapeDtypeStruct((rows, width), BF16),
            jax.ShapeDtypeStruct((heads, 1, rows), F32),
        ],
        compiler_params=pltpu.CompilerParams(vmem_limit_bytes=48 * 2**20),
        name="attend_forward",
    )(queries, *keys, *values)


def attend_backward_kernel(chunk, last, q_ref, do_ref, lse_ref, *refs):
    n = chunk + 1
    k_refs, v_refs, refs = refs[:n], refs[n : 2 * n], refs[2 * n :]
    if not last:
        dk_in, dv_in, refs = refs[:n], refs[n : 2 * n], refs[2 * n :]
    dq_ref, dk_refs, dv_refs, (dk_acc, dv_acc) = refs[0], refs[1 : 1 + n], refs[1 + n : 1 + 2 * n], refs[1 + 2 * n :]
    rows = q_ref.shape[0]
    keys = jnp.concatenate([ref[...] for ref in k_refs], axis=0)
    values = jnp.concatenate([ref[...] for ref in v_refs], axis=0)
    if last:
        dk_acc[...] = jnp.zeros_like(dk_acc)
        dv_acc[...] = jnp.zeros_like(dv_acc)
    else:
        for i in range(n):
            dk_acc[pl.ds(i * rows, rows), :] = dk_in[i][...]
            dv_acc[pl.ds(i * rows, rows), :] = dv_in[i][...]
    scale = HEAD_DIM ** (-0.5)
    for sub in range(rows // SUB):
        count = chunk * rows + (sub + 1) * SUB
        span = pl.ds(sub * SUB, SUB)
        query, grad = q_ref[span, :], do_ref[span, :]
        scores = times_transpose(keys[:count], query) * scale
        probs = jnp.exp(scores - lse_ref[0, :, span])
        allowed = lax.broadcasted_iota(jnp.int32, (SUB, SUB), 0) <= lax.broadcasted_iota(
            jnp.int32, (SUB, SUB), 1
        )
        tail = jnp.where(allowed, probs[count - SUB :], 0.0)
        probs = jnp.concatenate([probs[: count - SUB], tail], axis=0) if count > SUB else tail
        prob_grad = times_transpose(values[:count], grad)
        row_dot = jnp.sum(probs * prob_grad, axis=0, keepdims=True)
        score_grad = (probs * (prob_grad - row_dot)).astype(BF16)
        dq_ref[span, :] = (contract_rows(keys[:count], score_grad) * scale).T.astype(BF16)
        dk_acc[pl.ds(0, count), :] += jnp.dot(score_grad, query, preferred_element_type=F32) * scale
        dv_acc[pl.ds(0, count), :] += jnp.dot(
            probs.astype(BF16), grad, preferred_element_type=F32
        )
    for i in range(n):
        dk_refs[i][...] = dk_acc[pl.ds(i * rows, rows), :].astype(dk_refs[i].dtype)
        dv_refs[i][...] = dv_acc[pl.ds(i * rows, rows), :].astype(dv_refs[i].dtype)


def attend_backward(queries, grad, lse, keys, values, sums):
    rows, width = queries.shape
    heads = width // HEAD_DIM
    chunk = len(keys) - 1
    n = chunk + 1
    spec = pl.BlockSpec((rows, HEAD_DIM), lambda h: (0, h))
    kinds = [F32] * chunk + [BF16]
    dk_dv = [jax.ShapeDtypeStruct((rows, width), kind) for kind in kinds]
    carried = [] if sums is None else [*sums[0], *sums[1]]
    outs = pl.pallas_call(
        functools.partial(attend_backward_kernel, chunk, sums is None),
        grid=(heads,),
        in_specs=[spec, spec, pl.BlockSpec((1, 1, rows), lambda h: (h, 0, 0))]
        + [spec] * (2 * n + len(carried)),
        out_specs=[spec] * (1 + 2 * n),
        out_shape=[jax.ShapeDtypeStruct((rows, width), BF16), *dk_dv, *dk_dv],
        scratch_shapes=[pltpu.VMEM((n * rows, HEAD_DIM), F32)] * 2,
        compiler_params=pltpu.CompilerParams(vmem_limit_bytes=48 * 2**20),
        name="attend_backward",
    )(queries, grad, lse, *keys, *values, *carried)
    return outs[0], outs[1 : 1 + n], outs[1 + n :]


def local(
    history,
    mix_in,
    mix_out,
    mix_static,
    stream_gain,
    qkv_weight,
    out_weight,
    mlp_gain,
    up_weight,
    down_weight,
    out_grad,
    seq_group,
    group_weight,
):
    n_stream = lax.axis_size("stream")
    member = lax.axis_index("stream")
    n_hist, tokens, width = history.shape
    assert tokens == SEQ
    full_width = width * n_stream
    rows = tokens // CHUNKS
    order = list(reversed(range(CHUNKS)))
    spans = [slice(c * rows, (c + 1) * rows) for c in range(CHUNKS)]
    first_col = member * width

    def rows_of(weight, idx):
        begin = lax.rem(member + idx, n_stream) * width
        return lax.dynamic_slice_in_dim(weight, begin, width, 0)

    moments_of = merge_moments(width)

    def moments(parts):
        means = jnp.stack([jnp.mean(part, axis=1) for part in parts])
        squares = jnp.stack(
            [jnp.sum(jnp.square(part - mean[:, None]), axis=1) for part, mean in zip(parts, means)]
        )
        both = moments_of(jnp.concatenate([means, squares], axis=0))
        count = len(parts)
        inv = lax.rsqrt(both[count:] / full_width + EPS_NORM)
        return [both[i][:, None] for i in range(count)], [inv[i][:, None] for i in range(count)]

    qkv_slices = [qkv_weight[:, s, :] for s in range(3)]
    mix_in_rows = lax.dynamic_slice_in_dim(mix_in, first_col, width, 0)
    mix_out_float = mix_out.astype(F32)
    mlp_gain_cols = lax.dynamic_slice_in_dim(mlp_gain, first_col, width, 0)

    group_pick = (
        seq_group[:, None] == jnp.arange(group_weight.shape[0], dtype=jnp.int32)[None, :]
    ).astype(F32)
    seq_weight = jnp.sum(group_pick * group_weight.astype(F32)[None, :]) * COT_SCALE
    cot_cols = out_grad.astype(F32) * seq_weight
    cot_low_cols = cot_cols.astype(BF16)

    scale_t, raw_t, pre_t, act_t, slope_t, coef_t, coef = {}, {}, {}, {}, {}, {}, {}
    for c in order:
        last = history[n_hist - 1, spans[c]]
        square_part = jnp.sum(jnp.square(last.astype(F32)), axis=1)[None]
        raw_part = dot_tt(mix_in_rows, last, ((0,), (1,)))
        both = butterfly(jnp.concatenate([raw_part, square_part], axis=0), "stream")
        raw_t[c] = both[:-1]
        scale_t[c] = lax.rsqrt(both[-1:] / full_width + EPS_MIX)
        pre_t[c] = scale_t[c] * raw_t[c]
        act_t[c], slope_t[c] = gelu_both(pre_t[c])
        coef_t[c] = dot_tt(mix_out_float, act_t[c], ((0,), (0,)), HIGH) + mix_static.reshape(-1, 1)
        coef[c] = coef_t[c].T

    streams, hat, inv_std, normed = {}, {}, {}, {}
    for c in order:
        mixed = []
        for s in range(4):
            total = coef[c][:, s * n_hist][:, None] * history[0, spans[c]].astype(F32)
            for j in range(1, n_hist):
                total = total + coef[c][:, s * n_hist + j][:, None] * history[j, spans[c]].astype(F32)
            mixed.append(total)
        streams[c] = mixed
        mean, inv_std[c] = moments(mixed[:3])
        hat[c] = [(mixed[s] - mean[s]) * inv_std[c][s] for s in range(3)]
        cols = jnp.stack([(hat[c][s] * stream_gain[s][None, :]).astype(BF16) for s in range(3)])
        normed[c] = line_gather(cols, member)

    cot_low = {c: line_gather(cot_low_cols[spans[c]], member) for c in order}

    proj = {
        c: [
            jnp.dot(normed[c][s], qkv_slices[s], preferred_element_type=F32).astype(BF16)
            for s in range(3)
        ]
        for c in order
    }
    query = {c: proj[c][0] for c in order}
    key = {c: proj[c][1] for c in order}
    value = {c: proj[c][2] for c in order}

    heads_out, lse, residual, hat_mlp, inv_mlp, normed_mlp = {}, {}, {}, {}, {}, {}
    for c in order:
        heads_out[c], lse[c] = attend_forward(
            query[c], [key[i] for i in range(c + 1)], [value[i] for i in range(c + 1)]
        )
        branch = line_scatter(lambda idx: times_transpose(heads_out[c], rows_of(out_weight, idx)))
        residual[c] = streams[c][3] + branch
        (mean,), (inv_mlp[c],) = moments([residual[c]])
        hat_mlp[c] = (residual[c] - mean) * inv_mlp[c]
        normed_mlp[c] = line_gather((hat_mlp[c] * mlp_gain_cols[None, :]).astype(BF16), member)

    hidden, d_hpre, d_normed_mlp = {}, {}, {}
    for c in order:
        d_hidden = jnp.dot(cot_low[c], down_weight, preferred_element_type=F32)
        hidden_pre = jnp.dot(normed_mlp[c], up_weight, preferred_element_type=F32)
        act, slope = gelu_both(hidden_pre)
        hidden[c] = act.astype(BF16)
        d_hpre[c] = (d_hidden * slope).astype(BF16)
        d_normed_mlp[c] = line_scatter(
            lambda idx: times_transpose(d_hpre[c], rows_of(up_weight, idx))
        )

    resid_grad, d_branch, d_heads = {}, {}, {}
    gain_part = 0.0
    for c in order:
        gain_part = gain_part + jnp.sum(d_normed_mlp[c] * hat_mlp[c], axis=0)
        scaled = d_normed_mlp[c] * mlp_gain_cols[None, :]
        sums = butterfly(
            jnp.stack([jnp.sum(scaled, axis=1), jnp.sum(scaled * hat_mlp[c], axis=1)]), "stream"
        )
        sums = sums / full_width
        resid_grad[c] = cot_cols[spans[c]] + inv_mlp[c] * (
            scaled - sums[0][:, None] - hat_mlp[c] * sums[1][:, None]
        )
        d_branch[c] = line_gather(resid_grad[c].astype(BF16), member)
        d_heads[c] = jnp.dot(d_branch[c], out_weight, preferred_element_type=F32).astype(BF16)
    d_proj = {}
    carried = None
    for c in order:
        dq, dk, dv = attend_backward(
            query[c],
            d_heads[c],
            lse[c],
            [key[i] for i in range(c + 1)],
            [value[i] for i in range(c + 1)],
            carried,
        )
        carried = (dk[:c], dv[:c])
        d_proj[c] = [dq, dk[c], dv[c]]

    d_normed = {}
    for c in order:
        d_normed[c] = [
            line_scatter(lambda idx: times_transpose(d_proj[c][s], rows_of(qkv_slices[s], idx)))
            for s in range(3)
        ]

    output = {}
    for c in order:
        output[c] = (
            residual[c]
            + line_scatter(lambda idx: times_transpose(hidden[c], rows_of(down_weight, idx)))
        ).astype(BF16)
    output_cols = jnp.concatenate([output[c] for c in range(CHUNKS)], axis=0)

    def whole(parts, axis=0):
        return jnp.concatenate([parts[c] for c in range(CHUNKS)], axis=axis)

    def weight_grad(former, latter):
        part = contract_rows(whole(former), whole(latter)).astype(BF16)
        return lax.psum_scatter(part, "dp", scatter_dimension=0, tiled=True).astype(F32)

    down_grad = weight_grad(cot_low, hidden)
    up_grad = weight_grad(normed_mlp, d_hpre)
    out_weight_grad = weight_grad(d_branch, heads_out)
    qkv_part = jnp.concatenate(
        [
            contract_rows(
                whole({c: normed[c][s] for c in order}), whole({c: d_proj[c][s] for c in order})
            ).astype(BF16)
            for s in range(3)
        ],
        axis=1,
    )
    qkv_grad = lax.psum_scatter(qkv_part, "dp", scatter_dimension=0, tiled=True).astype(F32)
    qkv_grad = qkv_grad.reshape(qkv_grad.shape[0], 3, width)

    placed = jnp.where(
        jnp.arange(n_stream)[:, None] == member, gain_part[None, :], jnp.zeros((n_stream, width), F32)
    )
    gain_mlp_grad = butterfly(butterfly(placed, "stream"), "dp").reshape(full_width)

    gain_grad = [0.0] * 3
    static_part = 0.0
    mix_out_part = 0.0
    mix_in_part = 0.0
    history_grad = []
    for c in order:
        layers = [history[j, spans[c]].astype(F32) for j in range(n_hist)]
        plain = jnp.stack([jnp.sum(layer, axis=1) for layer in layers])
        hat_dot = [jnp.stack([jnp.sum(hat[c][s] * layer, axis=1) for layer in layers]) for s in range(3)]
        resid_dot = jnp.stack([jnp.sum(resid_grad[c] * layer, axis=1) for layer in layers])
        early = butterfly(jnp.concatenate([plain, *hat_dot, resid_dot], axis=0), "stream")
        plain = early[:n_hist]
        hat_dot = [early[(s + 1) * n_hist : (s + 2) * n_hist] for s in range(3)]
        resid_dot = early[4 * n_hist :]

        grad_norm = [d_normed[c][s] * stream_gain[s][None, :] for s in range(3)]
        for s in range(3):
            gain_grad[s] = gain_grad[s] + jnp.sum(d_normed[c][s] * hat[c][s], axis=0)
        grad_sum = jnp.stack([jnp.sum(g, axis=1) for g in grad_norm])
        grad_hat = jnp.stack([jnp.sum(g * h, axis=1) for g, h in zip(grad_norm, hat[c])])
        grad_dot = [
            jnp.stack([jnp.sum(g * layer, axis=1) for layer in layers]) for g in grad_norm
        ]
        late = butterfly(jnp.concatenate([grad_sum, grad_hat, *grad_dot], axis=0), "stream")
        mean_grad = late[:3] / full_width
        mean_hat = late[3:6] / full_width
        grad_dot = [late[6 + s * n_hist : 6 + (s + 1) * n_hist] for s in range(3)]
        d_coef = jnp.concatenate(
            [
                inv_std[c][s].T
                * (grad_dot[s] - mean_grad[s][None] * plain - mean_hat[s][None] * hat_dot[s])
                for s in range(3)
            ]
            + [resid_dot],
            axis=0,
        )
        d_streams = [
            inv_std[c][s]
            * (grad_norm[s] - mean_grad[s][:, None] - hat[c][s] * mean_hat[s][:, None])
            for s in range(3)
        ] + [resid_grad[c]]
        static_part = static_part + jnp.sum(d_coef, axis=1)
        mix_out_part = mix_out_part + dot_tt(act_t[c], d_coef, ((1,), (1,)), HIGH)
        d_pre = dot_tt(mix_out_float, d_coef, ((1,), (0,)), HIGH) * slope_t[c]
        d_raw = d_pre * scale_t[c]
        last = layers[n_hist - 1]
        mix_in_part = mix_in_part + dot_tt(d_raw, last, ((1,), (0,)), HIGH)
        scale_term = (
            scale_t[c] * scale_t[c] * scale_t[c] / full_width
            * jnp.sum(d_pre * raw_t[c], axis=0, keepdims=True)
        ).T
        mix_back = dot_tt(d_raw, mix_in_rows.astype(F32), ((0,), (1,)), HIGH) - scale_term * last
        grads = []
        for j in range(n_hist):
            total = coef[c][:, 3 * n_hist + j][:, None] * d_streams[3]
            for s in range(3):
                total = total + coef[c][:, s * n_hist + j][:, None] * d_streams[s]
            if j == n_hist - 1:
                total = total + mix_back
            grads.append(total.astype(BF16))
        history_grad.append(jnp.stack(grads))
    history_grad = jnp.concatenate(list(reversed(history_grad)), axis=1)

    stream_gain_grad = butterfly(jnp.stack(gain_grad), "dp")
    small = jnp.concatenate(
        [mix_in_part, mix_out_part, static_part[:, None]], axis=1
    )
    small = butterfly(small, "dp")
    mixh = mix_in.shape[1]
    mix_in_grad = small[:, :width].T
    mix_out_grad = small[:, width : width + 4 * n_hist]
    static_grad = small[:, width + 4 * n_hist].reshape(4, n_hist)
    return (
        output_cols,
        history_grad,
        mix_in_grad,
        mix_out_grad,
        static_grad,
        stream_gain_grad,
        qkv_grad,
        out_weight_grad,
        gain_mlp_grad,
        up_grad,
        down_grad,
    )


def solution(mesh):
    in_specs = (
        P(None, "dp", "stream"),
        P(),
        P(),
        P(),
        P(None, "stream"),
        P(None, None, "stream"),
        P(None, "stream"),
        P(),
        P(None, "stream"),
        P(None, "stream"),
        P("dp", "stream"),
        P("dp"),
        P(),
    )
    out_specs = (
        P("dp", "stream"),
        P(None, "dp", "stream"),
        P("stream", None),
        P(),
        P(),
        P(None, "stream"),
        P("dp", None, "stream"),
        P("dp", "stream"),
        P(),
        P("dp", "stream"),
        P("dp", "stream"),
    )
    return jax.shard_map(local, mesh=mesh, in_specs=in_specs, out_specs=out_specs, check_vma=False)
```

```python
import functools
import math

import jax
import jax.numpy as jnp
from jax import lax
from jax.experimental import pallas as pl
from jax.experimental.pallas import tpu as pltpu
from jax.sharding import PartitionSpec as P

HEAD_DIM = 128
SEQ = 1024
CHUNKS = 2
SUB = 256

HIGH = lax.Precision.HIGHEST
EPS_NORM = 1e-05
EPS_MIX = 1e-06
COT_SCALE = 0.4
F32 = jnp.float32
BF16 = jnp.bfloat16


def gelu_both(values):
    cdf = 0.5 * (1.0 + lax.erf(values * math.sqrt(0.5)))
    density = jnp.exp(-0.5 * jnp.square(values)) * (1.0 / math.sqrt(2.0 * math.pi))
    return values * cdf, cdf + values * density


def dot_tt(former, latter, dims, precision=None):
    return lax.dot_general(
        former, latter, (dims, ((), ())), precision=precision, preferred_element_type=F32
    )


def contract_rows(former, latter):
    return dot_tt(former, latter, ((0,), (0,)))


def times_transpose(former, latter):
    return dot_tt(former, latter, ((1,), (1,)))


def after(value, *others):
    return lax.optimization_barrier((value, *others))[0]


class Order:
    def __init__(self):
        self.tick = ()

    def hold(self, value):
        return after(value, *self.tick) if self.tick else value

    def did(self, *outs):
        self.tick = (*self.tick, *outs)

    def send(self, *chains):
        items = [chain.items() for chain in chains]
        flat = [value for chain_items in items for value, _, _ in chain_items]
        held = lax.optimization_barrier((*flat, *self.tick))[: len(flat)]
        self.tick = tuple(held)
        at = 0
        for chain, chain_items in zip(chains, items):
            got = []
            for _, axis, perm in chain_items:
                got.append(lax.ppermute(held[at], axis, perm))
                at += 1
            chain.take(got)


class LineGather:
    def __init__(self, piece, member):
        self.piece, self.member = piece, member
        self.low, self.high = [piece], [piece]

    def items(self):
        n, step = lax.axis_size("stream"), len(self.low)
        return [
            (self.low[-1], "stream", [(i, i + 1) for i in range(step - 1, n - 1)]),
            (self.high[-1], "stream", [(i, i - 1) for i in range(1, n - step + 1)]),
        ]

    def take(self, got):
        self.low.append(got[0])
        self.high.append(got[1])

    def value(self):
        n, member = lax.axis_size("stream"), self.member
        slots = []
        for slot in range(n):
            value = self.piece
            for at in range(n):
                if at > slot:
                    value = jnp.where(member == at, self.low[at - slot], value)
                elif at < slot:
                    value = jnp.where(member == at, self.high[slot - at], value)
            slots.append(value)
        return jnp.concatenate(slots, axis=-1)


class LineScatter:
    def __init__(self, order, block):
        self.order, self.block = order, block
        self.parts, self.came, self.step = {}, None, 0

    def part(self, idx):
        if idx not in self.parts:
            self.parts[idx] = self.block(idx, lambda value: value)
        return self.parts[idx]

    def items(self):
        n, step = lax.axis_size("stream"), self.step
        up_idx, down_idx = n - 1 - step, 1 + step
        up_value, down_value = self.part(up_idx), self.part(down_idx)
        if self.came is not None:
            up, down = [got.astype(F32) for got in self.came]
            if up_idx == down_idx:
                up_value = down_value = up_value + up + down
            else:
                up_value, down_value = up_value + up, down_value + down
        return [
            (up_value.astype(BF16), "stream", [(i, i + 1) for i in range(step + 1)]),
            (down_value.astype(BF16), "stream", [(i, i - 1) for i in range(n - 1 - step, n)]),
        ]

    def take(self, got):
        self.came = got
        self.step += 1

    def prepare(self):
        n, step = lax.axis_size("stream"), self.step
        for idx in {n - 1 - step, (1 + step) % n}:
            if idx not in self.parts:
                self.parts[idx] = self.block(idx, self.order.hold)
                self.order.did(self.parts[idx])

    def pieces(self):
        return self.part(0), *self.came

    def value(self):
        own, up, down = self.pieces()
        return own + up.astype(F32) + down.astype(F32)


class Butterfly:
    def __init__(self, value, axes=("stream",), merge=jnp.add):
        self.now, self.merge = value, merge
        self.turns = [(axis, 1 << i) for axis in axes for i in range(lax.axis_size(axis).bit_length() - 1)]
        assert all(lax.axis_size(axis) & (lax.axis_size(axis) - 1) == 0 for axis in axes)

    def items(self):
        axis, span = self.turns[0]
        return [(self.now, axis, [(i, i ^ span) for i in range(lax.axis_size(axis))])]

    def take(self, got):
        self.turns = self.turns[1:]
        self.now = self.merge(self.now, got[0])

    def value(self):
        assert not self.turns
        return self.now


def moments_merger(width, half):
    count = [width]

    def merge(mine, other):
        row = lax.broadcasted_iota(jnp.int32, mine.shape, 0)
        total = mine + other
        gap = jnp.roll(mine - other, half, axis=0)
        square = total + jnp.square(gap) * (0.5 * count[0])
        count[0] *= 2
        return jnp.where(row < half, 0.5 * total, square)

    return merge


def attend_forward_kernel(chunk, q_ref, *refs):
    k_refs, v_refs = refs[: chunk + 1], refs[chunk + 1 : 2 * chunk + 2]
    o_ref, lse_ref = refs[2 * chunk + 2 :]
    rows = q_ref.shape[0]
    keys = jnp.concatenate([ref[...] for ref in k_refs], axis=0)
    values = jnp.concatenate([ref[...] for ref in v_refs], axis=0)
    for sub in range(rows // SUB):
        count = chunk * rows + (sub + 1) * SUB
        span = pl.ds(sub * SUB, SUB)
        scores = times_transpose(keys[:count], q_ref[span, :]) * HEAD_DIM ** (-0.5)
        allowed = lax.broadcasted_iota(jnp.int32, (SUB, SUB), 0) <= lax.broadcasted_iota(
            jnp.int32, (SUB, SUB), 1
        )
        tail = jnp.where(allowed, scores[count - SUB :], -1e30)
        scores = jnp.concatenate([scores[: count - SUB], tail], axis=0) if count > SUB else tail
        top = jnp.max(scores, axis=0, keepdims=True)
        weights = jnp.exp(scores - top)
        total = jnp.sum(weights, axis=0, keepdims=True)
        probs = (weights * (1.0 / total)).astype(BF16)
        lse_ref[0, :, span] = top + jnp.log(total)
        out = contract_rows(values[:count], probs)
        o_ref[span, :] = out.T.astype(BF16)


def attend_forward(queries, keys, values):
    rows, width = queries.shape
    heads = width // HEAD_DIM
    chunk = len(keys) - 1
    spec = pl.BlockSpec((rows, HEAD_DIM), lambda h: (0, h))
    return pl.pallas_call(
        functools.partial(attend_forward_kernel, chunk),
        grid=(heads,),
        in_specs=[spec] * (2 * chunk + 3),
        out_specs=[spec, pl.BlockSpec((1, 1, rows), lambda h: (h, 0, 0))],
        out_shape=[
            jax.ShapeDtypeStruct((rows, width), BF16),
            jax.ShapeDtypeStruct((heads, 1, rows), F32),
        ],
        compiler_params=pltpu.CompilerParams(vmem_limit_bytes=48 * 2**20),
        name="attend_forward",
    )(queries, *keys, *values)


def attend_backward_kernel(chunk, q_ref, do_ref, lse_ref, *refs):
    n = chunk + 1
    k_refs, v_refs, refs = refs[:n], refs[n : 2 * n], refs[2 * n :]
    dk_in, dv_in, refs = refs[:chunk], refs[chunk : 2 * chunk], refs[2 * chunk :]
    dq_ref, dk_refs, dv_refs, (dk_acc, dv_acc) = refs[0], refs[1 : 1 + n], refs[1 + n : 1 + 2 * n], refs[1 + 2 * n :]
    rows = q_ref.shape[0]
    keys = jnp.concatenate([ref[...] for ref in k_refs], axis=0)
    values = jnp.concatenate([ref[...] for ref in v_refs], axis=0)
    for i in range(n):
        here = pl.ds(i * rows, rows)
        dk_acc[here, :] = dk_in[i][...] if i < chunk else jnp.zeros((rows, HEAD_DIM), F32)
        dv_acc[here, :] = dv_in[i][...] if i < chunk else jnp.zeros((rows, HEAD_DIM), F32)
    scale = HEAD_DIM ** (-0.5)
    for sub in range(rows // SUB):
        count = chunk * rows + (sub + 1) * SUB
        span = pl.ds(sub * SUB, SUB)
        query, grad = q_ref[span, :], do_ref[span, :]
        scores = times_transpose(keys[:count], query) * scale
        probs = jnp.exp(scores - lse_ref[0, :, span])
        allowed = lax.broadcasted_iota(jnp.int32, (SUB, SUB), 0) <= lax.broadcasted_iota(
            jnp.int32, (SUB, SUB), 1
        )
        tail = jnp.where(allowed, probs[count - SUB :], 0.0)
        probs = jnp.concatenate([probs[: count - SUB], tail], axis=0) if count > SUB else tail
        prob_grad = times_transpose(values[:count], grad)
        row_dot = jnp.sum(probs * prob_grad, axis=0, keepdims=True)
        score_grad = (probs * (prob_grad - row_dot)).astype(BF16)
        dq_ref[span, :] = (contract_rows(keys[:count], score_grad) * scale).T.astype(BF16)
        dk_acc[pl.ds(0, count), :] += jnp.dot(score_grad, query, preferred_element_type=F32) * scale
        dv_acc[pl.ds(0, count), :] += jnp.dot(
            probs.astype(BF16), grad, preferred_element_type=F32
        )
    for i in range(n):
        dk_refs[i][...] = dk_acc[pl.ds(i * rows, rows), :].astype(dk_refs[i].dtype)
        dv_refs[i][...] = dv_acc[pl.ds(i * rows, rows), :].astype(dv_refs[i].dtype)


def attend_backward(queries, grad, lse, keys, values, sums, final):
    rows, width = queries.shape
    heads = width // HEAD_DIM
    chunk = len(keys) - 1
    n = chunk + 1
    spec = pl.BlockSpec((rows, HEAD_DIM), lambda h: (0, h))
    dk_dv = [jax.ShapeDtypeStruct((rows, width), BF16 if final else F32)] * (2 * n)
    carried = [] if sums is None else [*sums[0], *sums[1]]
    outs = pl.pallas_call(
        functools.partial(attend_backward_kernel, chunk),
        grid=(heads,),
        in_specs=[spec, spec, pl.BlockSpec((1, 1, rows), lambda h: (h, 0, 0))]
        + [spec] * (2 * n + len(carried)),
        out_specs=[spec] * (1 + 2 * n),
        out_shape=[jax.ShapeDtypeStruct((rows, width), BF16), *dk_dv],
        scratch_shapes=[pltpu.VMEM((n * rows, HEAD_DIM), F32)] * 2,
        compiler_params=pltpu.CompilerParams(vmem_limit_bytes=48 * 2**20),
        name="attend_backward",
    )(queries, grad, lse, *keys, *values, *carried)
    return outs[0], outs[1 : 1 + n], outs[1 + n :]


GROUP = 64
TILE = 128
SLOT = 16
SCALE_ROW = 48
MEAN_ROW = 56
LANES = 128


def put_lane(acc, idx, column):
    lane = lax.broadcasted_iota(jnp.int32, acc.shape, 1)
    return jnp.where(lane == idx, column, acc)


def row_sum(values):
    return jnp.sum(values, axis=1, keepdims=True)


def spread(values, idx):
    return jnp.broadcast_to(values[:, idx : idx + 1], (values.shape[0], LANES))


def by_groups(tile, body):
    def step(i, carry):
        body(pl.ds(pl.multiple_of(i * GROUP, GROUP), GROUP))
        return carry

    lax.fori_loop(0, tile // GROUP, step, 0)


def mix_kernel(picked, hist_ref, coef_ref, *refs):
    out_refs, stat_ref, stat_acc = refs[: len(picked)], *(refs[len(picked) :] or (None, None))
    n_hist, tile, width = hist_ref.shape

    def group(span):
        coef = coef_ref[span, :]
        cols = {(s, j): spread(coef, s * n_hist + j) for s in picked for j in range(n_hist)}
        pivots, sums, squares = [], [], []
        for w in range(width // LANES):
            lanes = pl.ds(w * LANES, LANES)
            totals = [0.0] * len(picked)
            for j in range(n_hist):
                layer = hist_ref[j, span, lanes].astype(F32)
                for i, s in enumerate(picked):
                    totals[i] = totals[i] + cols[s, j] * layer
            for i, total in enumerate(totals):
                out_refs[i][span, lanes] = total
                if stat_ref is None:
                    continue
                if w == 0:
                    pivots.append(spread(total, 0))
                    sums.append(0.0)
                    squares.append(0.0)
                gap = total - pivots[i]
                sums[i] = sums[i] + gap
                squares[i] = squares[i] + jnp.square(gap)
        if stat_ref is not None:
            stats = jnp.zeros((GROUP, LANES), F32)
            for i in range(len(picked)):
                shift = row_sum(sums[i]) * (1.0 / width)
                stats = put_lane(stats, i, pivots[i] + shift)
                stats = put_lane(stats, len(picked) + i, row_sum(squares[i]) - shift * shift * width)
            stat_acc[span, :] = stats

    by_groups(tile, group)
    if stat_ref is not None:
        stat_ref[...] = stat_acc[...].T[: stat_ref.shape[0]]


def mix_streams(history, coef, chunk, picked, with_stats):
    n_hist, tokens, width = history.shape
    rows = coef.shape[0]
    base = chunk * rows // TILE
    wide = pl.BlockSpec((TILE, width), lambda i: (i, 0))
    n = len(picked)
    return pl.pallas_call(
        functools.partial(mix_kernel, picked),
        grid=(rows // TILE,),
        in_specs=[
            pl.BlockSpec((n_hist, TILE, width), lambda i: (0, base + i, 0)),
            pl.BlockSpec((TILE, 4 * n_hist), lambda i: (i, 0)),
        ],
        out_specs=[wide] * n + ([pl.BlockSpec((8, TILE), lambda i: (0, i))] if with_stats else []),
        out_shape=[jax.ShapeDtypeStruct((rows, width), F32)] * n
        + ([jax.ShapeDtypeStruct((8, rows), F32)] if with_stats else []),
        scratch_shapes=[pltpu.VMEM((TILE, LANES), F32)] if with_stats else [],
        compiler_params=pltpu.CompilerParams(vmem_limit_bytes=32 * 2**20),
        name="mix_streams",
    )(history, coef)


def hat_of(stream, stat, s):
    return (stream - spread(stat, s)) * spread(stat, 3 + s)


def early_kernel(hist_ref, x0, x1, x2, stat_ref, resid_ref, sums_ref, acc_ref):
    n_hist, tile, width = hist_ref.shape

    def group(span):
        stat = stat_ref[span, :]
        sums = jnp.zeros((GROUP, LANES), F32)
        pieces = [pl.ds(w * LANES, LANES) for w in range(width // LANES)]
        others = [[hat_of(x[span, p], stat, s) for p in pieces] for s, x in enumerate((x0, x1, x2))]
        others.append([resid_ref[span, p] for p in pieces])
        for j in range(n_hist):
            layer = [hist_ref[j, span, p].astype(F32) for p in pieces]
            sums = put_lane(sums, j, row_sum(sum(layer[1:], layer[0])))
            for s in range(4):
                terms = [x * y for x, y in zip(others[s], layer)]
                sums = put_lane(sums, (s + 1) * SLOT + j, row_sum(sum(terms[1:], terms[0])))
        acc_ref[span, :] = sums

    by_groups(tile, group)
    sums_ref[...] = acc_ref[...].T[: sums_ref.shape[0]]


def early_dots(history, streams, stat, resid_grad, chunk):
    n_hist, tokens, width = history.shape
    rows = resid_grad.shape[0]
    base = chunk * rows // TILE
    wide = pl.BlockSpec((TILE, width), lambda i: (i, 0))
    return pl.pallas_call(
        early_kernel,
        grid=(rows // TILE,),
        in_specs=[
            pl.BlockSpec((n_hist, TILE, width), lambda i: (0, base + i, 0)),
            wide,
            wide,
            wide,
            pl.BlockSpec((TILE, LANES), lambda i: (i, 0)),
            wide,
        ],
        out_specs=pl.BlockSpec((5 * SLOT, TILE), lambda i: (0, i)),
        out_shape=jax.ShapeDtypeStruct((5 * SLOT, rows), F32),
        scratch_shapes=[pltpu.VMEM((TILE, LANES), F32)],
        compiler_params=pltpu.CompilerParams(vmem_limit_bytes=32 * 2**20),
        name="early_dots",
    )(history, *streams, stat, resid_grad)


def late_kernel(hist_ref, x0, x1, x2, stat_ref, gain_ref, d0, d1, d2, *refs):
    sums_ref, gain_grad_ref, acc_ref = refs[-3:]
    n_hist, tile, width = hist_ref.shape

    @pl.when(pl.program_id(0) == 0)
    def _():
        gain_grad_ref[...] = jnp.zeros_like(gain_grad_ref)

    def group(span):
        stat = stat_ref[span, :]
        sums = jnp.zeros((GROUP, LANES), F32)
        pieces = [pl.ds(w * LANES, LANES) for w in range(width // LANES)]
        grads = []
        for s, (x, d) in enumerate(((x0, d0), (x1, d1), (x2, d2))):
            scaled, dots = [], []
            for p in pieces:
                product = d[span, p] * hat_of(x[span, p], stat, s)
                gain = gain_ref[pl.ds(s, 1), p]
                gain_grad_ref[s, :, p] += jnp.sum(product.reshape(GROUP // 8, 8, LANES), axis=0)
                scaled.append(d[span, p] * gain)
                dots.append(product * gain)
            sums = put_lane(sums, s * SLOT + n_hist, row_sum(sum(scaled[1:], scaled[0])))
            sums = put_lane(sums, s * SLOT + n_hist + 1, row_sum(sum(dots[1:], dots[0])))
            grads.append(scaled)
        for j in range(n_hist):
            layer = [hist_ref[j, span, p].astype(F32) for p in pieces]
            for s in range(3):
                terms = [x * y for x, y in zip(grads[s], layer)]
                sums = put_lane(sums, s * SLOT + j, row_sum(sum(terms[1:], terms[0])))
        acc_ref[span, :] = sums

    by_groups(tile, group)
    sums_ref[...] = acc_ref[...].T[: sums_ref.shape[0]]


def late_dots(history, streams, stat, gain, d_normed, chunk, others):
    n_hist, tokens, width = history.shape
    rows = stat.shape[0]
    base = chunk * rows // TILE
    wide = pl.BlockSpec((TILE, width), lambda i: (i, 0))
    slices = [pl.BlockSpec((None, TILE, width), lambda i, s=s: (s, i, 0)) for s in range(3)]
    return pl.pallas_call(
        late_kernel,
        grid=(rows // TILE,),
        in_specs=[
            pl.BlockSpec((n_hist, TILE, width), lambda i: (0, base + i, 0)),
            wide,
            wide,
            wide,
            pl.BlockSpec((TILE, LANES), lambda i: (i, 0)),
            pl.BlockSpec((3, width), lambda i: (0, 0)),
            *slices,
        ]
        + [pl.BlockSpec(memory_space=pl.ANY)] * len(others),
        out_specs=[
            pl.BlockSpec((3 * SLOT, TILE), lambda i: (0, i)),
            pl.BlockSpec((3, 8, width), lambda i: (0, 0, 0)),
        ],
        out_shape=[
            jax.ShapeDtypeStruct((3 * SLOT, rows), F32),
            jax.ShapeDtypeStruct((3, 8, width), F32),
        ],
        scratch_shapes=[pltpu.VMEM((TILE, LANES), F32)],
        compiler_params=pltpu.CompilerParams(vmem_limit_bytes=32 * 2**20),
        name="late_dots",
    )(history, *streams, stat, gain, d_normed, d_normed, d_normed, *others)


def layers_kernel(coef_ref, x0, x1, x2, stat_ref, gain_ref, mean_ref, d0, d1, d2, resid_ref, extra_ref, *refs):
    out_ref = refs[-1]
    n_hist, tile, width = out_ref.shape

    def group(span):
        stat, coef, means = stat_ref[span, :], coef_ref[span, :], mean_ref[span, :]
        cols = [spread(coef, i) for i in range(4 * n_hist)]
        for w in range(width // LANES):
            p = pl.ds(w * LANES, LANES)
            grads = []
            for s, (x, d) in enumerate(((x0, d0), (x1, d1), (x2, d2))):
                scaled = d[span, p] * gain_ref[pl.ds(s, 1), p]
                hat = hat_of(x[span, p], stat, s)
                grads.append(
                    spread(stat, 3 + s) * (scaled - spread(means, MEAN_ROW + s) - hat * spread(means, MEAN_ROW + 3 + s))
                )
            grads.append(resid_ref[span, p])
            for j in range(n_hist):
                total = extra_ref[span, p] if j == n_hist - 1 else 0.0
                for s in range(4):
                    total = total + cols[s * n_hist + j] * grads[s]
                out_ref[j, span, p] = total.astype(BF16)

    by_groups(tile, group)


def layer_grads(coef, streams, stat, gain, means, d_normed, resid_grad, extra, chunk, held, tokens):
    rows, width = resid_grad.shape
    n_hist = coef.shape[1] // 4
    base = chunk * rows // TILE
    wide = pl.BlockSpec((TILE, width), lambda i: (i, 0))
    slices = [pl.BlockSpec((None, TILE, width), lambda i, s=s: (s, i, 0)) for s in range(3)]
    narrow = pl.BlockSpec((TILE, LANES), lambda i: (i, 0))
    return pl.pallas_call(
        layers_kernel,
        grid=(rows // TILE,),
        in_specs=[
            pl.BlockSpec((TILE, 4 * n_hist), lambda i: (i, 0)),
            wide,
            wide,
            wide,
            narrow,
            pl.BlockSpec((3, width), lambda i: (0, 0)),
            pl.BlockSpec((TILE, LANES), lambda i: (i, 0)),
            *slices,
            wide,
            wide,
        ]
        + ([] if held is None else [pl.BlockSpec(memory_space=pl.ANY)]),
        out_specs=pl.BlockSpec((n_hist, TILE, width), lambda i: (0, base + i, 0)),
        out_shape=jax.ShapeDtypeStruct((n_hist, tokens, width), BF16),
        input_output_aliases={} if held is None else {12: 0},
        compiler_params=pltpu.CompilerParams(vmem_limit_bytes=32 * 2**20),
        name="layer_grads",
    )(coef, *streams, stat, gain, means, d_normed, d_normed, d_normed, resid_grad, extra, *([] if held is None else [held]))


def coef_kernel(full_width, n_hist, early, late, stat, act, slope, raw, scale, mix_out, mix_in, last, out_part, in_part, turned_ref, extra_ref, pack):
    rows = late.shape[1]
    mixh = act.shape[0]
    inside = lax.broadcasted_iota(jnp.int32, (SLOT, rows), 0) < n_hist
    pack[...] = jnp.zeros_like(pack)
    slots = []
    for s in range(3):
        mean = late[pl.ds(s * SLOT + n_hist, 1), :] * (1.0 / full_width)
        mean_hat = late[pl.ds(s * SLOT + n_hist + 1, 1), :] * (1.0 / full_width)
        pack[pl.ds(MEAN_ROW + s, 1), :] = mean
        pack[pl.ds(MEAN_ROW + 3 + s, 1), :] = mean_hat
        slot = inv_std(stat[pl.ds(3 + s, 1), :], full_width) * (
            late[pl.ds(s * SLOT, SLOT), :]
            - mean * early[pl.ds(0, SLOT), :]
            - mean_hat * early[pl.ds((s + 1) * SLOT, SLOT), :]
        )
        slots.append(jnp.where(inside, slot, 0.0))
    slots.append(jnp.where(inside, early[pl.ds(4 * SLOT, SLOT), :], 0.0))
    d_coef = jnp.concatenate(slots, axis=0)
    ones = jnp.ones((8, rows), F32)
    out_part[pl.ds(0, mixh), :] = dot_tt(act[...], d_coef, ((1,), (1,)), HIGH)
    out_part[pl.ds(SCALE_ROW, 8), :] = dot_tt(ones, d_coef, ((1,), (1,)), HIGH)
    d_pre = dot_tt(mix_out[...], d_coef, ((1,), (0,)), HIGH) * slope[...]
    d_raw = d_pre * scale[...]
    in_part[...] = dot_tt(d_raw, last[...].astype(F32), ((1,), (0,)), HIGH)
    pack[pl.ds(0, mixh), :] = d_raw
    pack[pl.ds(SCALE_ROW, 1), :] = (
        scale[...] * scale[...] * scale[...] * (1.0 / full_width)
        * jnp.sum(d_pre * raw[...], axis=0, keepdims=True)
    )
    turned = pack[...].T
    turned_ref[...] = turned
    back = dot_tt(turned, mix_in[...], ((1,), (1,)), HIGH)
    extra_ref[...] = back - turned[:, SCALE_ROW : SCALE_ROW + 1] * last[...].astype(F32)


def coef_grads(full_width, early, late, stat, act, slope, raw, scale, mix_out, mix_in, history, chunk):
    n_hist, tokens, width = history.shape
    rows = late.shape[1]
    mixh = act.shape[0]

    def full(array):
        return pl.BlockSpec(array.shape, lambda i: (0,) * array.ndim)

    arrays = [early, late, stat, act, slope, raw, scale, mix_out, mix_in]
    outs = [
        jax.ShapeDtypeStruct((SCALE_ROW + 8, 4 * SLOT), F32),
        jax.ShapeDtypeStruct((mixh, width), F32),
        jax.ShapeDtypeStruct((rows, LANES), F32),
        jax.ShapeDtypeStruct((rows, width), F32),
    ]
    return pl.pallas_call(
        functools.partial(coef_kernel, full_width, n_hist),
        grid=(1,),
        in_specs=[full(a) for a in arrays]
        + [pl.BlockSpec((None, rows, width), lambda i: (n_hist - 1, chunk, 0))],
        out_specs=[full(a) for a in outs],
        out_shape=outs,
        scratch_shapes=[pltpu.VMEM((LANES, rows), F32)],
        compiler_params=pltpu.CompilerParams(vmem_limit_bytes=32 * 2**20),
        name="coef_grads",
    )(*arrays, history)


def columns(rows_values):
    return jnp.concatenate([rows_values, jnp.zeros((TILE - 8, TILE), F32)], axis=0).T


def inv_std(squares, full_width):
    return lax.rsqrt(squares * (1.0 / full_width) + EPS_NORM)


def norm_kernel(full_width, x0, x1, x2, moment_ref, gain_ref, cols_ref, stat_ref):
    row = lax.broadcasted_iota(jnp.int32, (8, TILE), 0)
    moments = moment_ref[...]
    stat = columns(jnp.where(row < 3, moments, inv_std(moments, full_width)))
    stat_ref[...] = stat
    for s, x in enumerate((x0, x1, x2)):
        hat = (x[...] - stat[:, s : s + 1]) * stat[:, 3 + s : 4 + s]
        cols_ref[s] = (hat * gain_ref[pl.ds(s, 1), :]).astype(BF16)


def norm_streams(full_width, streams, moments, gain):
    rows, width = streams[0].shape
    wide = pl.BlockSpec((TILE, width), lambda i: (i, 0))
    return pl.pallas_call(
        functools.partial(norm_kernel, full_width),
        grid=(rows // TILE,),
        in_specs=[
            wide,
            wide,
            wide,
            pl.BlockSpec((8, TILE), lambda i: (0, i)),
            pl.BlockSpec((3, width), lambda i: (0, 0)),
        ],
        out_specs=[
            pl.BlockSpec((3, TILE, width), lambda i: (0, i, 0)),
            pl.BlockSpec((TILE, LANES), lambda i: (i, 0)),
        ],
        out_shape=[
            jax.ShapeDtypeStruct((3, rows, width), BF16),
            jax.ShapeDtypeStruct((rows, LANES), F32),
        ],
        compiler_params=pltpu.CompilerParams(vmem_limit_bytes=32 * 2**20),
        name="norm_streams",
    )(*streams, moments, gain)


def residual_kernel(own, up, down, base, out_ref, stat_ref):
    width = own.shape[1]
    value = base[...] + own[...] + up[...].astype(F32) + down[...].astype(F32)
    out_ref[...] = value
    pivot = value[:, :1]
    gap = value - pivot
    shift = row_sum(gap) * (1.0 / width)
    acc = put_lane(jnp.zeros((TILE, LANES), F32), 0, pivot + shift)
    acc = put_lane(acc, 1, row_sum(jnp.square(gap)) - shift * shift * width)
    stat_ref[...] = acc.T[:8]


def residual_rows(own, up, down, base):
    rows, width = own.shape
    wide = pl.BlockSpec((TILE, width), lambda i: (i, 0))
    return pl.pallas_call(
        residual_kernel,
        grid=(rows // TILE,),
        in_specs=[wide] * 4,
        out_specs=[wide, pl.BlockSpec((8, TILE), lambda i: (0, i))],
        out_shape=[
            jax.ShapeDtypeStruct((rows, width), F32),
            jax.ShapeDtypeStruct((8, rows), F32),
        ],
        compiler_params=pltpu.CompilerParams(vmem_limit_bytes=32 * 2**20),
        name="residual_rows",
    )(own, up, down, base)


def hat_kernel(full_width, x, stat_ref, gain_ref, out_ref):
    stat = columns(stat_ref[...])
    hat = (x[...] - stat[:, :1]) * inv_std(stat[:, 1:2], full_width)
    out_ref[...] = (hat * gain_ref[...]).astype(BF16)


def mlp_input(full_width, residual, stat, gain):
    rows, width = residual.shape
    wide = pl.BlockSpec((TILE, width), lambda i: (i, 0))
    return pl.pallas_call(
        functools.partial(hat_kernel, full_width),
        grid=(rows // TILE,),
        in_specs=[
            wide,
            pl.BlockSpec((8, TILE), lambda i: (0, i)),
            pl.BlockSpec((1, width), lambda i: (0, 0)),
        ],
        out_specs=wide,
        out_shape=jax.ShapeDtypeStruct((rows, width), BF16),
        compiler_params=pltpu.CompilerParams(vmem_limit_bytes=32 * 2**20),
        name="mlp_input",
    )(residual, stat, gain)


def mlp_back_kernel(full_width, own, up, down, x, stat_ref, gain_ref, out_ref, sums_ref, gain_grad_ref):
    @pl.when(pl.program_id(0) == 0)
    def _():
        gain_grad_ref[...] = jnp.zeros_like(gain_grad_ref)

    stat = columns(stat_ref[...])
    grad = own[...] + up[...].astype(F32) + down[...].astype(F32)
    out_ref[...] = grad
    product = grad * ((x[...] - stat[:, :1]) * inv_std(stat[:, 1:2], full_width))
    gain_grad_ref[...] += jnp.sum(product.reshape(TILE // 8, 8, -1), axis=0)
    acc = put_lane(jnp.zeros((TILE, LANES), F32), 0, row_sum(grad * gain_ref[...]))
    acc = put_lane(acc, 1, row_sum(product * gain_ref[...]))
    sums_ref[...] = acc.T[:8]


def mlp_back_rows(full_width, own, up, down, residual, stat, gain):
    rows, width = residual.shape
    wide = pl.BlockSpec((TILE, width), lambda i: (i, 0))
    narrow = pl.BlockSpec((8, TILE), lambda i: (0, i))
    return pl.pallas_call(
        functools.partial(mlp_back_kernel, full_width),
        grid=(rows // TILE,),
        in_specs=[wide] * 4 + [narrow, pl.BlockSpec((1, width), lambda i: (0, 0))],
        out_specs=[wide, narrow, pl.BlockSpec((8, width), lambda i: (0, 0))],
        out_shape=[
            jax.ShapeDtypeStruct((rows, width), F32),
            jax.ShapeDtypeStruct((8, rows), F32),
            jax.ShapeDtypeStruct((8, width), F32),
        ],
        compiler_params=pltpu.CompilerParams(vmem_limit_bytes=32 * 2**20),
        name="mlp_back_rows",
    )(own, up, down, residual, stat, gain)


def resid_grad_kernel(full_width, grad, x, stat_ref, sums_ref, gain_ref, cot, out_ref, low_ref):
    stat = columns(stat_ref[...])
    sums = columns(sums_ref[...]) * (1.0 / full_width)
    inv = inv_std(stat[:, 1:2], full_width)
    hat = (x[...] - stat[:, :1]) * inv
    value = cot[...] + inv * (grad[...] * gain_ref[...] - sums[:, :1] - hat * sums[:, 1:2])
    out_ref[...] = value
    low_ref[...] = value.astype(BF16)


def resid_grad_rows(full_width, grad, residual, stat, sums, gain, cot):
    rows, width = residual.shape
    wide = pl.BlockSpec((TILE, width), lambda i: (i, 0))
    narrow = pl.BlockSpec((8, TILE), lambda i: (0, i))
    return pl.pallas_call(
        functools.partial(resid_grad_kernel, full_width),
        grid=(rows // TILE,),
        in_specs=[wide, wide, narrow, narrow, pl.BlockSpec((1, width), lambda i: (0, 0)), wide],
        out_specs=[wide, wide],
        out_shape=[
            jax.ShapeDtypeStruct((rows, width), F32),
            jax.ShapeDtypeStruct((rows, width), BF16),
        ],
        compiler_params=pltpu.CompilerParams(vmem_limit_bytes=32 * 2**20),
        name="resid_grad_rows",
    )(grad, residual, stat, sums, gain, cot)


def rows_product_kernel(n, *refs):
    former, latter, out_ref, turned = refs[:n], refs[n : 2 * n], refs[-2], refs[-1]
    rows = former[0].shape[0]

    @pl.when(pl.program_id(1) == 0)
    def _():
        for c in range(n):
            turned[:, pl.ds(c * rows, rows)] = former[c][...].T

    total = 0.0
    for c in range(n):
        total = total + jnp.dot(
            turned[:, pl.ds(c * rows, rows)], latter[c][...], preferred_element_type=F32
        )
    out_ref[...] = total.astype(BF16)


def rows_product(former, latter, out_cols, first, held, others=(), slot=None):
    n = len(former)
    rows, height = former[0].shape[-2:]
    width = latter[0].shape[1]
    tile_m, tile_n = min(512, height), min(1024, width)
    begin = first // tile_n
    free = [*others] + ([] if held is None else [held])
    return pl.pallas_call(
        functools.partial(rows_product_kernel, n),
        grid=(height // tile_m, width // tile_n),
        in_specs=[
            pl.BlockSpec((rows, tile_m), lambda i, j: (0, i))
            if slot is None
            else pl.BlockSpec((None, rows, tile_m), lambda i, j: (slot, 0, i))
        ]
        * n
        + [pl.BlockSpec((rows, tile_n), lambda i, j: (0, j))] * n
        + [pl.BlockSpec(memory_space=pl.ANY)] * len(free),
        out_specs=pl.BlockSpec((tile_m, tile_n), lambda i, j: (i, begin + j)),
        out_shape=jax.ShapeDtypeStruct((height, out_cols), BF16),
        input_output_aliases={} if held is None else {2 * n + len(others): 0},
        scratch_shapes=[pltpu.VMEM((tile_m, n * rows), BF16)],
        compiler_params=pltpu.CompilerParams(vmem_limit_bytes=48 * 2**20),
        name="rows_product",
    )(*former, *latter, *free)


def local(
    history,
    mix_in,
    mix_out,
    mix_static,
    stream_gain,
    qkv_weight,
    out_weight,
    mlp_gain,
    up_weight,
    down_weight,
    out_grad,
    seq_group,
    group_weight,
):
    n_stream = lax.axis_size("stream")
    member = lax.axis_index("stream")
    n_hist, tokens, width = history.shape
    assert tokens == SEQ
    full_width = width * n_stream
    rows = tokens // CHUNKS
    both = range(CHUNKS)
    spans = [slice(c * rows, (c + 1) * rows) for c in both]
    first_col = member * width
    mixh = mix_in.shape[1]
    ff = up_weight.shape[1]
    order = Order()

    def rows_of(weight, idx):
        begin = lax.rem(member + idx, n_stream) * width
        return lax.dynamic_slice_in_dim(weight, begin, width, 0)

    def dp_sum(part):
        return lax.psum_scatter(part, "dp", scatter_dimension=0, tiled=True).astype(F32)

    mix_in_rows = lax.dynamic_slice_in_dim(mix_in, first_col, width, 0)
    mix_out_float = mix_out.astype(F32)

    raw = []
    for c in both:
        last = history[n_hist - 1, spans[c]]
        square_part = jnp.sum(jnp.square(last.astype(F32)), axis=1)[None]
        raw_part = dot_tt(mix_in_rows, last, ((0,), (1,)))
        raw.append(Butterfly(jnp.concatenate([raw_part, square_part], axis=0)))
    order.send(*raw)

    group_pick = (
        seq_group[:, None] == jnp.arange(group_weight.shape[0], dtype=jnp.int32)[None, :]
    ).astype(F32)
    seq_weight = jnp.sum(group_pick * group_weight.astype(F32)[None, :]) * COT_SCALE
    out_grad_held = order.hold(out_grad)
    cot_cols = [out_grad_held[spans[c]].astype(F32) * seq_weight for c in both]
    cot = [LineGather(cot_cols[c].astype(BF16), member) for c in both]
    order.did(cot[0].piece)
    order.send(*raw)
    order.send(cot[0])

    scale_t, raw_t, act_t, slope_t, coef = [], [], [], [], []
    for c in both:
        sums = raw[c].value()
        raw_t.append(sums[:-1])
        scale_t.append(lax.rsqrt(sums[-1:] / full_width + EPS_MIX))
        act, slope = gelu_both(scale_t[c] * raw_t[c])
        act_t.append(act)
        slope_t.append(slope)
        coef_t = dot_tt(mix_out_float, act, ((0,), (0,)), HIGH) + mix_static.reshape(-1, 1)
        coef.append(coef_t.T)

    streams, moments = [None] * 2, [None] * 2
    stat, stat_rows, normed_chain = [None] * 2, [None] * 2, [None] * 2
    resid_streams = [None] * 2

    def mix(c):
        *streams[c], sums = mix_streams(history, coef[c], c, (0, 1, 2), True)
        moments[c] = Butterfly(sums, merge=moments_merger(width, 3))

    def norm(c):
        stat_rows[c] = moments[c].value()
        cols, stat[c] = norm_streams(full_width, streams[c], stat_rows[c], stream_gain)
        normed_chain[c] = LineGather(cols, member)

    def mix_resid(c):
        (resid_streams[c],) = mix_streams(history, order.hold(coef[c]), c, (3,), False)
        order.did(resid_streams[c])

    mix(0)
    order.send(moments[0])
    coef[1] = order.hold(coef[1])
    mix(1)
    order.did(streams[1][0])
    order.send(moments[0])
    norm(0)
    order.send(normed_chain[0])
    order.send(moments[1])
    mix_resid(0)
    mix_resid(1)
    order.send(normed_chain[0])
    order.send(moments[1])
    norm(1)
    order.did(normed_chain[1].piece)
    qkv_slices = [qkv_weight[:, s, :] for s in range(3)]
    order.send(normed_chain[0])
    order.send(normed_chain[1])

    normed, query, key, value, heads_out, lse = [], [], [], [], [], []
    branch = []

    def attend(c):
        normed.append(normed_chain[c].value())
        for held, s in ((query, 0), (key, 1), (value, 2)):
            held.append(
                jnp.dot(normed[c][s], qkv_slices[s], preferred_element_type=F32).astype(BF16)
            )
        out, out_lse = attend_forward(query[c], key[: c + 1], value[: c + 1])
        heads_out.append(out)
        lse.append(out_lse)
        branch.append(
            LineScatter(
                order, lambda idx, hold: times_transpose(hold(out), rows_of(out_weight, idx))
            )
        )

    residual, resid_moments = [], []

    def end_branch(c):
        value, stats = residual_rows(*branch[c].pieces(), resid_streams[c])
        residual.append(value)
        resid_moments.append(Butterfly(stats, merge=moments_merger(width, 1)))

    mlp_gain_cols = lax.dynamic_slice_in_dim(mlp_gain, first_col, width, 0)[None, :]
    mlp_in = []

    def norm_mlp(c):
        cols = mlp_input(full_width, residual[c], resid_moments[c].value(), mlp_gain_cols)
        mlp_in.append(LineGather(cols, member))

    cot_low, d_hidden = [], []

    def down_back(c):
        cot_low.append(cot[c].value())
        d_hidden.append(
            jnp.dot(order.hold(cot_low[c]), down_weight, preferred_element_type=F32)
        )
        order.did(d_hidden[c])

    normed_mlp, hidden, d_hpre, mlp_back, mlp_out = [], [], [], [], []

    def mlp(c):
        normed_mlp.append(mlp_in[c].value())
        hidden_pre = jnp.dot(normed_mlp[c], up_weight, preferred_element_type=F32)
        act, slope = gelu_both(hidden_pre)
        act = act.astype(BF16)
        d_pre = (d_hidden[c] * slope).astype(BF16)
        hidden.append(act)
        d_hpre.append(d_pre)
        mlp_back.append(
            LineScatter(
                order, lambda idx, hold: times_transpose(hold(d_pre), rows_of(up_weight, idx))
            )
        )
        mlp_out.append(
            LineScatter(
                order, lambda idx, hold: times_transpose(hold(act), rows_of(down_weight, idx))
            )
        )

    d_normed_mlp, back_sums, mlp_gain_shares = [], [], []

    def end_mlp_back(c):
        value, sums, share = mlp_back_rows(
            full_width, *mlp_back[c].pieces(), residual[c], resid_moments[c].value(), mlp_gain_cols
        )
        d_normed_mlp.append(value)
        back_sums.append(Butterfly(sums))
        mlp_gain_shares.append(share)

    resid_grad, branch_grad = [], []

    def norm_mlp_back(c):
        value, low = resid_grad_rows(
            full_width, d_normed_mlp[c], residual[c], resid_moments[c].value(),
            back_sums[c].value(), mlp_gain_cols, cot_cols[c],
        )
        resid_grad.append(value)
        branch_grad.append(LineGather(low, member))

    d_branch, d_proj = [], []
    carried = [None]

    def attend_back(c):
        d_branch.append(branch_grad[c].value())
        d_heads = jnp.dot(d_branch[c], out_weight, preferred_element_type=F32).astype(BF16)
        d_query, dk, dv = attend_backward(
            query[c], d_heads, lse[c], key[: c + 1], value[: c + 1], carried[0], c == CHUNKS - 1
        )
        carried[0] = (dk, dv)
        d_proj.append([d_query, None, None])
        if c == CHUNKS - 1:
            for i in both:
                d_proj[i][1:] = [dk[i], dv[i]]

    attend(0)
    order.send(branch[0])
    branch[0].prepare()
    order.send(normed_chain[1])
    order.send(branch[0])
    branch[0].prepare()
    order.send(normed_chain[1])
    order.send(branch[0])
    branch[0].prepare()
    end_branch(0)
    order.send(resid_moments[0], cot[0])
    order.send(resid_moments[0])
    norm_mlp(0)
    order.send(mlp_in[0], cot[0])
    attend(1)
    order.send(branch[1], mlp_in[0])
    branch[1].prepare()
    down_back(0)
    order.send(branch[1], mlp_in[0])
    branch[1].prepare()
    order.send(branch[1], cot[1])
    branch[1].prepare()
    mlp(0)
    end_branch(1)
    order.send(resid_moments[1])
    order.did(hidden[0])
    order.send(resid_moments[1], cot[1])
    norm_mlp(1)
    order.send(mlp_in[1], mlp_back[0])
    mlp_back[0].prepare()
    order.send(cot[1])
    order.send(mlp_in[1], mlp_back[0])
    mlp_back[0].prepare()
    down_back(1)
    order.send(mlp_in[1], mlp_back[0])
    mlp_back[0].prepare()
    end_mlp_back(0)
    order.send(back_sums[0])
    mlp(1)
    order.did(hidden[1])
    order.send(back_sums[0])
    norm_mlp_back(0)
    order.send(mlp_back[1], branch_grad[0])
    mlp_back[1].prepare()
    order.send(mlp_back[1], branch_grad[0])
    mlp_back[1].prepare()
    order.send(mlp_back[1], branch_grad[0])
    mlp_back[1].prepare()
    end_mlp_back(1)
    order.send(back_sums[1])
    attend_back(0)
    order.did(d_proj[0][0])
    order.send(back_sums[1])
    norm_mlp_back(1)
    mlp_out[0].prepare()
    order.send(branch_grad[1], mlp_out[0])
    mlp_out[0].prepare()
    order.send(branch_grad[1], mlp_out[0])
    mlp_out[0].prepare()
    order.send(branch_grad[1], mlp_out[0])
    mlp_out[0].prepare()
    attend_back(1)

    def grad_chain(c):
        return LineScatter(
            order,
            lambda idx, hold: jnp.stack(
                [times_transpose(hold(d_proj[c][s]), rows_of(qkv_slices[s], idx)) for s in range(3)]
            ),
        )

    def weight_part(former, latter, out_cols, first=0, held=None):
        part = rows_product(former, latter, out_cols, first, held, order.tick)
        order.did(part)
        return part

    def early(c):
        sums = early_dots(history, streams[c], stat[c], order.hold(resid_grad[c]), c)
        order.did(sums)
        return Butterfly(sums)

    gain_part = jnp.sum(mlp_gain_shares[0] + mlp_gain_shares[1], axis=0)
    placed = jnp.where(
        jnp.arange(n_stream)[:, None] == member, gain_part[None, :], jnp.zeros((n_stream, width), F32)
    )
    gain_chain = Butterfly(placed)

    grads = [grad_chain(c) for c in both]
    order.send(grads[0])
    order.send(grads[1])
    down_part = weight_part(cot_low, hidden, ff)
    out_part = weight_part(d_branch, heads_out, width)
    down_grad, out_weight_grad = dp_sum(down_part), dp_sum(out_part)
    grads[0].prepare()
    grads[1].prepare()
    order.send(grads[0])
    up_part = weight_part(normed_mlp, d_hpre, ff)
    early_chain = [early(0)]
    up_grad = dp_sum(up_part)
    order.send(grads[1], gain_chain)
    grads[0].prepare()
    order.send(grads[0], gain_chain, early_chain[0])
    qkv_part = None
    for s in range(3):
        qkv_part = rows_product(
            [normed[c] for c in both], [d_proj[c][s] for c in both], 3 * width, s * width, qkv_part,
            order.tick, s,
        )
    order.did(qkv_part)
    qkv_grad = dp_sum(qkv_part)
    qkv_grad = qkv_grad.reshape(qkv_grad.shape[0], 3, width)
    early_chain.append(early(1))
    grads[1].prepare()
    order.send(grads[1], *early_chain)

    mix_out_wide = jnp.pad(
        mix_out_float.reshape(-1, 4, n_hist), ((0, 0), (0, 0), (0, SLOT - n_hist))
    ).reshape(-1, 4 * SLOT)
    mix_in_wide = jnp.pad(mix_in_rows.astype(F32), ((0, 0), (0, LANES - mixh)))
    d_normed, late, gain_shares, shares = [], [], [], []
    history_grad = [None]

    def late_sums(c, others):
        d_normed.append(grads[c].value())
        sums, gain_share = late_dots(
            history, streams[c], stat[c], stream_gain, d_normed[c], c, others
        )
        late.append(Butterfly(sums))
        gain_shares.append(gain_share)

    def coefs(c):
        shares.append(
            coef_grads(
                full_width, early_chain[c].value(), late[c].value(), stat_rows[c], act_t[c],
                slope_t[c], raw_t[c], scale_t[c], mix_out_wide, mix_in_wide, history, c,
            )
        )

    def layers(c):
        _, _, turned, extra = shares[c]
        history_grad[0] = layer_grads(
            coef[c], streams[c], stat[c], stream_gain, order.hold(turned), d_normed[c],
            resid_grad[c], extra, c, history_grad[0], tokens,
        )
        order.did(history_grad[0])

    mlp_out[1].prepare()
    late_sums(0, ())
    order.send(late[0], early_chain[1])
    late_sums(1, (down_grad, up_grad, out_weight_grad))
    order.send(late[0], late[1])
    order.send(late[1])
    order.send(mlp_out[1])
    mlp_out[1].prepare()
    coefs(0)
    coefs(1)
    out_share, in_share = [shares[0][i] + shares[1][i] for i in range(2)]
    gain_share = jnp.sum(gain_shares[0] + gain_shares[1], axis=1)
    out_share = jnp.pad(out_share, ((0, 0), (0, width - 4 * SLOT)))
    small = Butterfly(
        jnp.concatenate([out_share, in_share, gain_share, gain_chain.value()], axis=0), ("dp",)
    )
    order.send(small)
    layers(0)
    order.send(small, mlp_out[1])
    layers(1)
    while small.turns:
        order.send(small, *([mlp_out[1]] if mlp_out[1].step < n_stream - 1 else []))
    output_cols = jnp.concatenate(
        [(residual[c] + mlp_out[c].value()).astype(BF16) for c in both], axis=0
    )
    small = small.value()
    top = out_share.shape[0]
    by_slot = small[:top, : 4 * SLOT].reshape(-1, 4, SLOT)[:, :, :n_hist]
    return (
        output_cols,
        history_grad[0],
        small[top : top + mixh].T,
        by_slot[:mixh].reshape(mixh, 4 * n_hist),
        by_slot[SCALE_ROW],
        small[top + mixh : top + mixh + 3],
        qkv_grad,
        out_weight_grad,
        small[top + mixh + 3 :].reshape(full_width),
        up_grad,
        down_grad,
    )


def solution(mesh):
    in_specs = (
        P(None, "dp", "stream"),
        P(),
        P(),
        P(),
        P(None, "stream"),
        P(None, None, "stream"),
        P(None, "stream"),
        P(),
        P(None, "stream"),
        P(None, "stream"),
        P("dp", "stream"),
        P("dp"),
        P(),
    )
    out_specs = (
        P("dp", "stream"),
        P(None, "dp", "stream"),
        P("stream", None),
        P(),
        P(),
        P(None, "stream"),
        P("dp", None, "stream"),
        P("dp", "stream"),
        P(),
        P("dp", "stream"),
        P("dp", "stream"),
    )
    return jax.shard_map(local, mesh=mesh, in_specs=in_specs, out_specs=out_specs, check_vma=False)
```

```python
import functools
import math

import jax
import jax.numpy as jnp
from jax import lax
from jax.experimental import pallas as pl
from jax.experimental.pallas import tpu as pltpu
from jax.sharding import PartitionSpec as P

HEAD_DIM = 128
SEQ = 1024
CHUNKS = 2
SUB = 256

HIGH = lax.Precision.HIGHEST
EPS_NORM = 1e-05
EPS_MIX = 1e-06
COT_SCALE = 0.4
F32 = jnp.float32
BF16 = jnp.bfloat16


def gelu_both(values):
    cdf = 0.5 * (1.0 + lax.erf(values * math.sqrt(0.5)))
    density = jnp.exp(-0.5 * jnp.square(values)) * (1.0 / math.sqrt(2.0 * math.pi))
    return values * cdf, cdf + values * density


def dot_tt(former, latter, dims, precision=None):
    return lax.dot_general(
        former, latter, (dims, ((), ())), precision=precision, preferred_element_type=F32
    )


def contract_rows(former, latter):
    return dot_tt(former, latter, ((0,), (0,)))


def times_transpose(former, latter):
    return dot_tt(former, latter, ((1,), (1,)))


def after(value, *others):
    return lax.optimization_barrier((value, *others))[0]


class Order:
    def __init__(self):
        self.tick = ()

    def hold(self, value):
        return after(value, *self.tick) if self.tick else value

    def did(self, *outs):
        self.tick = (*self.tick, *outs)

    def send(self, *chains):
        items = [chain.items() for chain in chains]
        flat = [value for chain_items in items for value, _, _ in chain_items]
        held = lax.optimization_barrier((*flat, *self.tick))[: len(flat)]
        self.tick = tuple(held)
        at = 0
        for chain, chain_items in zip(chains, items):
            got = []
            for _, axis, perm in chain_items:
                got.append(lax.ppermute(held[at], axis, perm))
                at += 1
            chain.take(got)


class LineGather:
    def __init__(self, piece, member):
        self.piece, self.member = piece, member
        self.low, self.high = [piece], [piece]

    def items(self):
        n, step = lax.axis_size("stream"), len(self.low)
        return [
            (self.low[-1], "stream", [(i, i + 1) for i in range(step - 1, n - 1)]),
            (self.high[-1], "stream", [(i, i - 1) for i in range(1, n - step + 1)]),
        ]

    def take(self, got):
        self.low.append(got[0])
        self.high.append(got[1])

    def value(self):
        n, member = lax.axis_size("stream"), self.member
        slots = []
        for slot in range(n):
            value = self.piece
            for at in range(n):
                if at > slot:
                    value = jnp.where(member == at, self.low[at - slot], value)
                elif at < slot:
                    value = jnp.where(member == at, self.high[slot - at], value)
            slots.append(value)
        return jnp.concatenate(slots, axis=-1)


class LineScatter:
    def __init__(self, order, block):
        self.order, self.block = order, block
        self.parts, self.came, self.step = {}, None, 0

    def part(self, idx):
        if idx not in self.parts:
            self.parts[idx] = self.block(idx, lambda value: value)
        return self.parts[idx]

    def items(self):
        n, step = lax.axis_size("stream"), self.step
        up_idx, down_idx = n - 1 - step, 1 + step
        up_value, down_value = self.part(up_idx), self.part(down_idx)
        if self.came is not None:
            up, down = [got.astype(F32) for got in self.came]
            if up_idx == down_idx:
                up_value = down_value = up_value + up + down
            else:
                up_value, down_value = up_value + up, down_value + down
        return [
            (up_value.astype(BF16), "stream", [(i, i + 1) for i in range(step + 1)]),
            (down_value.astype(BF16), "stream", [(i, i - 1) for i in range(n - 1 - step, n)]),
        ]

    def take(self, got):
        self.came = got
        self.step += 1

    def prepare(self):
        n, step = lax.axis_size("stream"), self.step
        for idx in {n - 1 - step, (1 + step) % n}:
            if idx not in self.parts:
                self.parts[idx] = self.block(idx, self.order.hold)
                self.order.did(self.parts[idx])

    def pieces(self):
        return self.part(0), *self.came

    def value(self):
        own, up, down = self.pieces()
        return own + up.astype(F32) + down.astype(F32)


class ProductScatter(LineScatter):
    def __init__(self, order, member, lhs, weight):
        super().__init__(order, None)
        self.args = (member, lhs, weight)

    def items(self):
        n, step = lax.axis_size("stream"), self.step
        up_turn, down_turn = n - 1 - step, 1 + step
        turns = (up_turn,) if up_turn == down_turn else (up_turn, down_turn)
        values = send_values(*self.args, turns, self.came)
        return [
            (values[0], "stream", [(i, i + 1) for i in range(step + 1)]),
            (values[-1], "stream", [(i, i - 1) for i in range(n - 1 - step, n)]),
        ]

    def own(self):
        member, lhs, weight = self.args
        (value,) = send_values(member, [self.order.hold(lhs[0]), *lhs[1:]], weight, (0,), None, F32)
        self.order.did(value)
        return value


class Butterfly:
    def __init__(self, value, axes=("stream",), merge=jnp.add):
        self.now, self.merge = value, merge
        self.turns = [(axis, 1 << i) for axis in axes for i in range(lax.axis_size(axis).bit_length() - 1)]
        assert all(lax.axis_size(axis) & (lax.axis_size(axis) - 1) == 0 for axis in axes)

    def items(self):
        axis, span = self.turns[0]
        return [(self.now, axis, [(i, i ^ span) for i in range(lax.axis_size(axis))])]

    def take(self, got):
        self.turns = self.turns[1:]
        self.now = self.merge(self.now, got[0])

    def value(self):
        assert not self.turns
        return self.now


def moments_merger(width, half):
    count = [width]

    def merge(mine, other):
        row = lax.broadcasted_iota(jnp.int32, mine.shape, 0)
        total = mine + other
        gap = jnp.roll(mine - other, half, axis=0)
        square = total + jnp.square(gap) * (0.5 * count[0])
        count[0] *= 2
        return jnp.where(row < half, 0.5 * total, square)

    return merge


def attend_forward_kernel(chunk, q_ref, *refs):
    k_refs, v_refs = refs[: chunk + 1], refs[chunk + 1 : 2 * chunk + 2]
    o_ref, lse_ref = refs[2 * chunk + 2 :]
    rows = q_ref.shape[0]
    keys = jnp.concatenate([ref[...] for ref in k_refs], axis=0)
    values = jnp.concatenate([ref[...] for ref in v_refs], axis=0)
    for sub in range(rows // SUB):
        count = chunk * rows + (sub + 1) * SUB
        span = pl.ds(sub * SUB, SUB)
        scores = times_transpose(keys[:count], q_ref[span, :]) * HEAD_DIM ** (-0.5)
        allowed = lax.broadcasted_iota(jnp.int32, (SUB, SUB), 0) <= lax.broadcasted_iota(
            jnp.int32, (SUB, SUB), 1
        )
        tail = jnp.where(allowed, scores[count - SUB :], -1e30)
        scores = jnp.concatenate([scores[: count - SUB], tail], axis=0) if count > SUB else tail
        top = jnp.max(scores, axis=0, keepdims=True)
        weights = jnp.exp(scores - top)
        total = jnp.sum(weights, axis=0, keepdims=True)
        probs = (weights * (1.0 / total)).astype(BF16)
        lse_ref[0, :, span] = top + jnp.log(total)
        out = contract_rows(values[:count], probs)
        o_ref[span, :] = out.T.astype(BF16)


def attend_forward(queries, keys, values):
    rows, width = queries.shape
    heads = width // HEAD_DIM
    chunk = len(keys) - 1
    spec = pl.BlockSpec((rows, HEAD_DIM), lambda h: (0, h))
    return pl.pallas_call(
        functools.partial(attend_forward_kernel, chunk),
        grid=(heads,),
        in_specs=[spec] * (2 * chunk + 3),
        out_specs=[spec, pl.BlockSpec((1, 1, rows), lambda h: (h, 0, 0))],
        out_shape=[
            jax.ShapeDtypeStruct((rows, width), BF16),
            jax.ShapeDtypeStruct((heads, 1, rows), F32),
        ],
        compiler_params=pltpu.CompilerParams(vmem_limit_bytes=48 * 2**20),
        name="attend_forward",
    )(queries, *keys, *values)


def attend_backward_kernel(chunk, q_ref, do_ref, lse_ref, *refs):
    n = chunk + 1
    k_refs, v_refs, refs = refs[:n], refs[n : 2 * n], refs[2 * n :]
    dk_in, dv_in, refs = refs[:chunk], refs[chunk : 2 * chunk], refs[2 * chunk :]
    dq_ref, dk_refs, dv_refs, (dk_acc, dv_acc) = refs[0], refs[1 : 1 + n], refs[1 + n : 1 + 2 * n], refs[1 + 2 * n :]
    rows = q_ref.shape[0]
    keys = jnp.concatenate([ref[...] for ref in k_refs], axis=0)
    values = jnp.concatenate([ref[...] for ref in v_refs], axis=0)
    for i in range(n):
        here = pl.ds(i * rows, rows)
        dk_acc[here, :] = dk_in[i][...] if i < chunk else jnp.zeros((rows, HEAD_DIM), F32)
        dv_acc[here, :] = dv_in[i][...] if i < chunk else jnp.zeros((rows, HEAD_DIM), F32)
    scale = HEAD_DIM ** (-0.5)
    for sub in range(rows // SUB):
        count = chunk * rows + (sub + 1) * SUB
        span = pl.ds(sub * SUB, SUB)
        query, grad = q_ref[span, :], do_ref[span, :]
        scores = times_transpose(keys[:count], query) * scale
        probs = jnp.exp(scores - lse_ref[0, :, span])
        allowed = lax.broadcasted_iota(jnp.int32, (SUB, SUB), 0) <= lax.broadcasted_iota(
            jnp.int32, (SUB, SUB), 1
        )
        tail = jnp.where(allowed, probs[count - SUB :], 0.0)
        probs = jnp.concatenate([probs[: count - SUB], tail], axis=0) if count > SUB else tail
        prob_grad = times_transpose(values[:count], grad)
        row_dot = jnp.sum(probs * prob_grad, axis=0, keepdims=True)
        score_grad = (probs * (prob_grad - row_dot)).astype(BF16)
        dq_ref[span, :] = (contract_rows(keys[:count], score_grad) * scale).T.astype(BF16)
        dk_acc[pl.ds(0, count), :] += jnp.dot(score_grad, query, preferred_element_type=F32) * scale
        dv_acc[pl.ds(0, count), :] += jnp.dot(
            probs.astype(BF16), grad, preferred_element_type=F32
        )
    for i in range(n):
        dk_refs[i][...] = dk_acc[pl.ds(i * rows, rows), :].astype(dk_refs[i].dtype)
        dv_refs[i][...] = dv_acc[pl.ds(i * rows, rows), :].astype(dv_refs[i].dtype)


def attend_backward(queries, grad, lse, keys, values, sums, final):
    rows, width = queries.shape
    heads = width // HEAD_DIM
    chunk = len(keys) - 1
    n = chunk + 1
    spec = pl.BlockSpec((rows, HEAD_DIM), lambda h: (0, h))
    dk_dv = [jax.ShapeDtypeStruct((rows, width), BF16 if final else F32)] * (2 * n)
    carried = [] if sums is None else [*sums[0], *sums[1]]
    outs = pl.pallas_call(
        functools.partial(attend_backward_kernel, chunk),
        grid=(heads,),
        in_specs=[spec, spec, pl.BlockSpec((1, 1, rows), lambda h: (h, 0, 0))]
        + [spec] * (2 * n + len(carried)),
        out_specs=[spec] * (1 + 2 * n),
        out_shape=[jax.ShapeDtypeStruct((rows, width), BF16), *dk_dv],
        scratch_shapes=[pltpu.VMEM((n * rows, HEAD_DIM), F32)] * 2,
        compiler_params=pltpu.CompilerParams(vmem_limit_bytes=48 * 2**20),
        name="attend_backward",
    )(queries, grad, lse, *keys, *values, *carried)
    return outs[0], outs[1 : 1 + n], outs[1 + n :]


GROUP = 128
VMEM_MOST = 60 * 2**20
TILE = 128
SLOT = 16
SCALE_ROW = 48
MEAN_ROW = 56
LANES = 128


def put_lane(acc, idx, column):
    lane = lax.broadcasted_iota(jnp.int32, acc.shape, 1)
    return jnp.where(lane == idx, column, acc)


def row_sum(values):
    return jnp.sum(values, axis=1, keepdims=True)


def spread(values, idx):
    return jnp.broadcast_to(values[:, idx : idx + 1], (values.shape[0], LANES))


def by_groups(tile, body):
    def step(i, carry):
        body(pl.ds(pl.multiple_of(i * GROUP, GROUP), GROUP))
        return carry

    lax.fori_loop(0, tile // GROUP, step, 0)


def mix_kernel(picked, hist_ref, coef_ref, *refs):
    out_refs, stat_ref, stat_acc = refs[: len(picked)], *(refs[len(picked) :] or (None, None))
    n_hist, tile, width = hist_ref.shape

    def group(span):
        coef = coef_ref[span, :]
        cols = {(s, j): spread(coef, s * n_hist + j) for s in picked for j in range(n_hist)}
        pivots, sums, squares = [], [], []
        for w in range(width // LANES):
            lanes = pl.ds(w * LANES, LANES)
            totals = [0.0] * len(picked)
            for j in range(n_hist):
                layer = hist_ref[j, span, lanes].astype(F32)
                for i, s in enumerate(picked):
                    totals[i] = totals[i] + cols[s, j] * layer
            for i, total in enumerate(totals):
                out_refs[i][span, lanes] = total
                if stat_ref is None:
                    continue
                if w == 0:
                    pivots.append(spread(total, 0))
                    sums.append(0.0)
                    squares.append(0.0)
                gap = total - pivots[i]
                sums[i] = sums[i] + gap
                squares[i] = squares[i] + jnp.square(gap)
        if stat_ref is not None:
            stats = jnp.zeros((GROUP, LANES), F32)
            for i in range(len(picked)):
                shift = row_sum(sums[i]) * (1.0 / width)
                stats = put_lane(stats, i, pivots[i] + shift)
                stats = put_lane(stats, len(picked) + i, row_sum(squares[i]) - shift * shift * width)
            stat_acc[span, :] = stats

    by_groups(tile, group)
    if stat_ref is not None:
        stat_ref[...] = stat_acc[...].T[: stat_ref.shape[0]]


def mix_streams(history, coef, chunk, picked, with_stats):
    n_hist, tokens, width = history.shape
    rows = tokens // CHUNKS
    base = chunk * rows // TILE
    wide = pl.BlockSpec((TILE, width), lambda i: (i, 0))
    n = len(picked)
    return pl.pallas_call(
        functools.partial(mix_kernel, picked),
        grid=(rows // TILE,),
        in_specs=[
            pl.BlockSpec((n_hist, TILE, width), lambda i: (0, base + i, 0)),
            pl.BlockSpec((TILE, 4 * n_hist), lambda i: (base + i, 0)),
        ],
        out_specs=[wide] * n + ([pl.BlockSpec((8, TILE), lambda i: (0, i))] if with_stats else []),
        out_shape=[jax.ShapeDtypeStruct((rows, width), F32)] * n
        + ([jax.ShapeDtypeStruct((8, rows), F32)] if with_stats else []),
        scratch_shapes=[pltpu.VMEM((TILE, LANES), F32)] if with_stats else [],
        compiler_params=pltpu.CompilerParams(vmem_limit_bytes=VMEM_MOST),
        name="mix_streams",
    )(history, coef)


def hat_of(stream, stat, s):
    return (stream - spread(stat, s)) * spread(stat, 3 + s)


def early_kernel(hist_ref, x0, x1, x2, stat_ref, sums_ref, acc_ref):
    n_hist, tile, width = hist_ref.shape

    def group(span):
        stat = stat_ref[span, :]
        sums = jnp.zeros((GROUP, LANES), F32)
        pieces = [pl.ds(w * LANES, LANES) for w in range(width // LANES)]
        others = [[hat_of(x[span, p], stat, s) for p in pieces] for s, x in enumerate((x0, x1, x2))]
        for j in range(n_hist):
            layer = [hist_ref[j, span, p].astype(F32) for p in pieces]
            sums = put_lane(sums, j, row_sum(sum(layer[1:], layer[0])))
            for s in range(3):
                terms = [x * y for x, y in zip(others[s], layer)]
                sums = put_lane(sums, (s + 1) * SLOT + j, row_sum(sum(terms[1:], terms[0])))
        acc_ref[span, :] = sums

    by_groups(tile, group)
    sums_ref[...] = acc_ref[...].T[: sums_ref.shape[0]]


def early_dots(history, streams, stat, chunk):
    n_hist, tokens, width = history.shape
    rows = stat.shape[0]
    base = chunk * rows // TILE
    wide = pl.BlockSpec((TILE, width), lambda i: (i, 0))
    return pl.pallas_call(
        early_kernel,
        grid=(rows // TILE,),
        in_specs=[
            pl.BlockSpec((n_hist, TILE, width), lambda i: (0, base + i, 0)),
            wide,
            wide,
            wide,
            pl.BlockSpec((TILE, LANES), lambda i: (i, 0)),
        ],
        out_specs=pl.BlockSpec((4 * SLOT, TILE), lambda i: (0, i)),
        out_shape=jax.ShapeDtypeStruct((4 * SLOT, rows), F32),
        scratch_shapes=[pltpu.VMEM((TILE, LANES), F32)],
        compiler_params=pltpu.CompilerParams(vmem_limit_bytes=VMEM_MOST),
        name="early_dots",
    )(history, *streams, stat)


def late_kernel(hist_ref, x0, x1, x2, stat_ref, gain_ref, resid_ref, own, up, down, g0, g1, g2, sums_ref, gain_grad_ref, acc_ref):
    grad_refs = (g0, g1, g2)
    n_hist, tile, width = hist_ref.shape

    @pl.when(pl.program_id(0) == 0)
    def _():
        gain_grad_ref[...] = jnp.zeros_like(gain_grad_ref)

    def group(span):
        stat = stat_ref[span, :]
        sums = jnp.zeros((GROUP, LANES), F32)
        pieces = [pl.ds(w * LANES, LANES) for w in range(width // LANES)]
        grads = []
        for s, x in enumerate((x0, x1, x2)):
            scaled, dots = [], []
            for p in pieces:
                d = own[s, span, p] + up[s, span, p].astype(F32) + down[s, span, p].astype(F32)
                product = d * hat_of(x[span, p], stat, s)
                gain = gain_ref[pl.ds(s, 1), p]
                gain_grad_ref[s, :, p] += jnp.sum(product.reshape(GROUP // 8, 8, LANES), axis=0)
                scaled.append(d * gain)
                dots.append(product * gain)
                grad_refs[s][span, p] = scaled[-1]
            sums = put_lane(sums, s * SLOT + n_hist, row_sum(sum(scaled[1:], scaled[0])))
            sums = put_lane(sums, s * SLOT + n_hist + 1, row_sum(sum(dots[1:], dots[0])))
            grads.append(scaled)
        grads.append([resid_ref[span, p] for p in pieces])
        for j in range(n_hist):
            layer = [hist_ref[j, span, p].astype(F32) for p in pieces]
            for s in range(4):
                terms = [x * y for x, y in zip(grads[s], layer)]
                sums = put_lane(sums, s * SLOT + j, row_sum(sum(terms[1:], terms[0])))
        acc_ref[span, :] = sums

    by_groups(tile, group)
    sums_ref[...] = acc_ref[...].T[: sums_ref.shape[0]]


def late_dots(history, streams, stat, gain, resid_grad, own, came, chunk):
    n_hist, tokens, width = history.shape
    rows = stat.shape[0]
    base = chunk * rows // TILE
    wide = pl.BlockSpec((TILE, width), lambda i: (i, 0))
    three = pl.BlockSpec((3, TILE, width), lambda i: (0, i, 0))
    return pl.pallas_call(
        late_kernel,
        grid=(rows // TILE,),
        in_specs=[
            pl.BlockSpec((n_hist, TILE, width), lambda i: (0, base + i, 0)),
            wide,
            wide,
            wide,
            pl.BlockSpec((TILE, LANES), lambda i: (i, 0)),
            pl.BlockSpec((3, width), lambda i: (0, 0)),
            wide,
            three,
            three,
            three,
        ],
        out_specs=[
            wide,
            wide,
            wide,
            pl.BlockSpec((4 * SLOT, TILE), lambda i: (0, i)),
            pl.BlockSpec((3, 8, width), lambda i: (0, 0, 0)),
        ],
        out_shape=[jax.ShapeDtypeStruct((rows, width), F32)] * 3
        + [
            jax.ShapeDtypeStruct((4 * SLOT, rows), F32),
            jax.ShapeDtypeStruct((3, 8, width), F32),
        ],
        scratch_shapes=[pltpu.VMEM((TILE, LANES), F32)],
        compiler_params=pltpu.CompilerParams(vmem_limit_bytes=VMEM_MOST),
        name="late_dots",
    )(history, *streams, stat, gain, resid_grad, own, *came)


def layers_kernel(coef_ref, x0, x1, x2, stat_ref, mean_ref, d0, d1, d2, resid_ref, extra_ref, *refs):
    out_ref = refs[-1]
    n_hist, tile, width = out_ref.shape

    def group(span):
        stat, coef, means = stat_ref[span, :], coef_ref[span, :], mean_ref[span, :]
        cols = [spread(coef, i) for i in range(4 * n_hist)]
        for w in range(width // LANES):
            p = pl.ds(w * LANES, LANES)
            grads = []
            for s, (x, d) in enumerate(((x0, d0), (x1, d1), (x2, d2))):
                hat = hat_of(x[span, p], stat, s)
                grads.append(
                    spread(stat, 3 + s) * (d[span, p] - spread(means, MEAN_ROW + s) - hat * spread(means, MEAN_ROW + 3 + s))
                )
            grads.append(resid_ref[span, p])
            for j in range(n_hist):
                total = extra_ref[span, p] if j == n_hist - 1 else 0.0
                for s in range(4):
                    total = total + cols[s * n_hist + j] * grads[s]
                out_ref[j, span, p] = total.astype(BF16)

    by_groups(tile, group)


def layer_grads(coef, streams, stat, means, scaled, resid_grad, extra, chunk, held, tokens, others):
    rows, width = resid_grad.shape
    n_hist = coef.shape[1] // 4
    base = chunk * rows // TILE
    wide = pl.BlockSpec((TILE, width), lambda i: (i, 0))
    narrow = pl.BlockSpec((TILE, LANES), lambda i: (i, 0))
    free = [*others] + ([] if held is None else [held])
    return pl.pallas_call(
        layers_kernel,
        grid=(rows // TILE,),
        in_specs=[
            pl.BlockSpec((TILE, 4 * n_hist), lambda i: (base + i, 0)),
            wide,
            wide,
            wide,
            narrow,
            narrow,
            wide,
            wide,
            wide,
            wide,
            wide,
        ]
        + [pl.BlockSpec(memory_space=pl.ANY)] * len(free),
        out_specs=pl.BlockSpec((n_hist, TILE, width), lambda i: (0, base + i, 0)),
        out_shape=jax.ShapeDtypeStruct((n_hist, tokens, width), BF16),
        input_output_aliases={} if held is None else {11 + len(others): 0},
        compiler_params=pltpu.CompilerParams(vmem_limit_bytes=32 * 2**20),
        name="layer_grads",
    )(coef, *streams, stat, means, *scaled, resid_grad, extra, *free)


def coef_kernel(full_width, n_hist, early, late, stat, act, slope, raw, scale, mix_out, mix_in, last, out_part, in_part, turned_ref, extra_ref, pack):
    rows = late.shape[1]
    mixh = act.shape[0]
    inside = lax.broadcasted_iota(jnp.int32, (SLOT, rows), 0) < n_hist
    pack[...] = jnp.zeros_like(pack)
    slots = []
    for s in range(3):
        mean = late[pl.ds(s * SLOT + n_hist, 1), :] * (1.0 / full_width)
        mean_hat = late[pl.ds(s * SLOT + n_hist + 1, 1), :] * (1.0 / full_width)
        pack[pl.ds(MEAN_ROW + s, 1), :] = mean
        pack[pl.ds(MEAN_ROW + 3 + s, 1), :] = mean_hat
        slot = inv_std(stat[pl.ds(3 + s, 1), :], full_width) * (
            late[pl.ds(s * SLOT, SLOT), :]
            - mean * early[pl.ds(0, SLOT), :]
            - mean_hat * early[pl.ds((s + 1) * SLOT, SLOT), :]
        )
        slots.append(jnp.where(inside, slot, 0.0))
    slots.append(jnp.where(inside, late[pl.ds(3 * SLOT, SLOT), :], 0.0))
    d_coef = jnp.concatenate(slots, axis=0)
    ones = jnp.ones((8, rows), F32)
    out_part[pl.ds(0, mixh), :] = dot_tt(act[...], d_coef, ((1,), (1,)), HIGH)
    out_part[pl.ds(SCALE_ROW, 8), :] = dot_tt(ones, d_coef, ((1,), (1,)), HIGH)
    d_pre = dot_tt(mix_out[...], d_coef, ((1,), (0,)), HIGH) * slope[...]
    d_raw = d_pre * scale[...]
    in_part[...] = dot_tt(d_raw, last[...].astype(F32), ((1,), (0,)), HIGH)
    pack[pl.ds(0, mixh), :] = d_raw
    pack[pl.ds(SCALE_ROW, 1), :] = (
        scale[...] * scale[...] * scale[...] * (1.0 / full_width)
        * jnp.sum(d_pre * raw[...], axis=0, keepdims=True)
    )
    turned = pack[...].T
    turned_ref[...] = turned
    back = dot_tt(turned, mix_in[...], ((1,), (1,)), HIGH)
    extra_ref[...] = back - turned[:, SCALE_ROW : SCALE_ROW + 1] * last[...].astype(F32)


def coef_grads(full_width, n_hist, early, late, stat, act, slope, raw, scale, mix_out, mix_in, last, chunk):
    width = last.shape[1]
    rows = late.shape[1]
    mixh = act.shape[0]

    def full(array):
        return pl.BlockSpec(array.shape, lambda i: (0,) * array.ndim)

    def part(array):
        return pl.BlockSpec((array.shape[0], rows), lambda i: (0, chunk))

    arrays = [early, late, stat, act, slope, raw, scale, mix_out, mix_in]
    outs = [
        jax.ShapeDtypeStruct((SCALE_ROW + 8, 4 * SLOT), F32),
        jax.ShapeDtypeStruct((mixh, width), F32),
        jax.ShapeDtypeStruct((rows, LANES), F32),
        jax.ShapeDtypeStruct((rows, width), F32),
    ]
    return pl.pallas_call(
        functools.partial(coef_kernel, full_width, n_hist),
        grid=(1,),
        in_specs=[part(early)]
        + [full(a) for a in arrays[1:3]]
        + [part(a) for a in arrays[3:7]]
        + [full(a) for a in arrays[7:]]
        + [pl.BlockSpec((rows, width), lambda i: (chunk, 0))],
        out_specs=[full(a) for a in outs],
        out_shape=outs,
        scratch_shapes=[pltpu.VMEM((LANES, rows), F32)],
        compiler_params=pltpu.CompilerParams(vmem_limit_bytes=32 * 2**20),
        name="coef_grads",
    )(*arrays, last)


def send_kernel(count, turns, has_came, member_ref, *refs):
    lhs, refs = refs[:count], refs[count:]
    weights, refs = refs[: len(turns)], refs[len(turns) :]
    came, outs = (refs[:2], refs[2:]) if has_came else ((), refs)
    for k in range(len(turns)):
        for s in range(count):
            value = times_transpose(lhs[s][...], weights[k][s])
            if has_came:
                for got in came if len(turns) == 1 else (came[k],):
                    value = value + got[s].astype(F32)
            outs[k][s] = value.astype(outs[k].dtype)


def send_values(member, lhs, weight, turns, came, kind=BF16):
    n = lax.axis_size("stream")
    count = len(lhs)
    rows, depth = lhs[0].shape
    width = weight.shape[1] // n
    tile = 256
    piece = pl.BlockSpec((count, tile, width), lambda i, m: (0, i, 0))

    def block(turn):
        return pl.BlockSpec((count, width, depth), lambda i, m: (0, lax.rem(m[0] + turn, n), 0))

    return pl.pallas_call(
        functools.partial(send_kernel, count, turns, came is not None),
        grid_spec=pltpu.PrefetchScalarGridSpec(
            num_scalar_prefetch=1,
            grid=(rows // tile,),
            in_specs=[pl.BlockSpec((tile, depth), lambda i, m: (i, 0))] * count
            + [block(turn) for turn in turns]
            + ([] if came is None else [piece] * 2),
            out_specs=[piece] * len(turns),
        ),
        out_shape=[jax.ShapeDtypeStruct((count, rows, width), kind)] * len(turns),
        compiler_params=pltpu.CompilerParams(vmem_limit_bytes=48 * 2**20),
        name="send_values",
    )(member, *lhs, *([weight] * len(turns)), *(came or ()))


def columns(rows_values):
    return jnp.concatenate([rows_values, jnp.zeros((TILE - 8, TILE), F32)], axis=0).T


def inv_std(squares, full_width):
    return lax.rsqrt(squares * (1.0 / full_width) + EPS_NORM)


def norm_kernel(full_width, x0, x1, x2, moment_ref, gain_ref, qk_ref, v_ref, stat_ref):
    row = lax.broadcasted_iota(jnp.int32, (8, TILE), 0)
    moments = moment_ref[...]
    stat = columns(jnp.where(row < 3, moments, inv_std(moments, full_width)))
    stat_ref[...] = stat
    for s, x in enumerate((x0, x1, x2)):
        hat = (x[...] - stat[:, s : s + 1]) * stat[:, 3 + s : 4 + s]
        value = (hat * gain_ref[pl.ds(s, 1), :]).astype(BF16)
        if s < 2:
            qk_ref[s] = value
        else:
            v_ref[...] = value


def norm_streams(full_width, streams, moments, gain):
    rows, width = streams[0].shape
    wide = pl.BlockSpec((TILE, width), lambda i: (i, 0))
    return pl.pallas_call(
        functools.partial(norm_kernel, full_width),
        grid=(rows // TILE,),
        in_specs=[
            wide,
            wide,
            wide,
            pl.BlockSpec((8, TILE), lambda i: (0, i)),
            pl.BlockSpec((3, width), lambda i: (0, 0)),
        ],
        out_specs=[
            pl.BlockSpec((2, TILE, width), lambda i: (0, i, 0)),
            wide,
            pl.BlockSpec((TILE, LANES), lambda i: (i, 0)),
        ],
        out_shape=[
            jax.ShapeDtypeStruct((2, rows, width), BF16),
            jax.ShapeDtypeStruct((rows, width), BF16),
            jax.ShapeDtypeStruct((rows, LANES), F32),
        ],
        compiler_params=pltpu.CompilerParams(vmem_limit_bytes=32 * 2**20),
        name="norm_streams",
    )(*streams, moments, gain)


def residual_kernel(member_ref, own, up, down, base, out_ref, low_ref, stat_ref):
    width = own.shape[1]
    value = base[...] + own[...] + up[...].astype(F32) + down[...].astype(F32)
    out_ref[...] = value
    pivot = value[:, :1]
    gap = value - pivot
    shift = row_sum(gap) * (1.0 / width)
    low_ref[...] = (gap - shift).astype(BF16)
    acc = put_lane(jnp.zeros((TILE, LANES), F32), member_ref[0], pivot + shift)
    square = row_sum(jnp.square(gap)) - shift * shift * width
    acc = put_lane(acc, 4 + member_ref[0], square)
    stat_ref[...] = acc.T[:8]


def residual_rows(member, own, up, down, base):
    rows, width = own.shape
    assert lax.axis_size("stream") == 4
    wide = pl.BlockSpec((TILE, width), lambda i, m: (i, 0))
    return pl.pallas_call(
        residual_kernel,
        grid_spec=pltpu.PrefetchScalarGridSpec(
            num_scalar_prefetch=1,
            grid=(rows // TILE,),
            in_specs=[wide] * 4,
            out_specs=[wide, wide, pl.BlockSpec((8, TILE), lambda i, m: (0, i))],
        ),
        out_shape=[
            jax.ShapeDtypeStruct((rows, width), F32),
            jax.ShapeDtypeStruct((rows, width), BF16),
            jax.ShapeDtypeStruct((8, rows), F32),
        ],
        compiler_params=pltpu.CompilerParams(vmem_limit_bytes=32 * 2**20),
        name="residual_rows",
    )(member, own, up, down, base)


def by_member(member_ref, pieces, store):
    n = (len(pieces) + 1) // 2
    low, high = (None, *pieces[1:n]), (None, *pieces[n:])
    for at in range(n):

        @pl.when(member_ref[0] == at)
        def _():
            for slot in range(n):
                if slot == at:
                    store(slot, pieces[0])
                elif slot < at:
                    store(slot, low[at - slot])
                else:
                    store(slot, high[slot - at])


def normed_kernel(full_width, member_ref, *refs):
    pieces, (stat_ref, gain_ref, out_ref, moment_ref) = refs[:-4], refs[-4:]
    n = (len(pieces) + 1) // 2
    width = pieces[0].shape[1]
    stat = stat_ref[...]
    mean = jnp.sum(stat[:n], axis=0, keepdims=True) * (1.0 / n)
    gaps = stat[:n] - mean
    square = jnp.sum(stat[n:], axis=0, keepdims=True) + width * jnp.sum(
        jnp.square(gaps), axis=0, keepdims=True
    )
    moment_ref[...] = jnp.concatenate([mean, square, jnp.zeros((6, TILE), F32)], axis=0)
    table = columns(
        jnp.concatenate([gaps, inv_std(square, full_width), jnp.zeros((3, TILE), F32)], axis=0)
    )

    def store(slot, ref):
        cols = pl.ds(slot * width, width)
        hat = (ref[...].astype(F32) + table[:, slot : slot + 1]) * table[:, n : n + 1]
        out_ref[:, cols] = (hat * gain_ref[:, cols]).astype(BF16)

    by_member(member_ref, pieces, store)


def normed_rows(full_width, member, chain, stat, gain):
    pieces = [chain.piece, *chain.low[1:], *chain.high[1:]]
    rows, width = chain.piece.shape
    wide = pl.BlockSpec((TILE, width), lambda i, m: (i, 0))
    narrow = pl.BlockSpec((8, TILE), lambda i, m: (0, i))
    return pl.pallas_call(
        functools.partial(normed_kernel, full_width),
        grid_spec=pltpu.PrefetchScalarGridSpec(
            num_scalar_prefetch=1,
            grid=(rows // TILE,),
            in_specs=[wide] * len(pieces)
            + [narrow, pl.BlockSpec((1, full_width), lambda i, m: (0, 0))],
            out_specs=[pl.BlockSpec((TILE, full_width), lambda i, m: (i, 0)), narrow],
        ),
        out_shape=[
            jax.ShapeDtypeStruct((rows, full_width), BF16),
            jax.ShapeDtypeStruct((8, rows), F32),
        ],
        compiler_params=pltpu.CompilerParams(vmem_limit_bytes=32 * 2**20),
        name="normed_rows",
    )(member, *pieces, stat, gain)


def branch_kernel(full_width, member_ref, *refs):
    pieces, (stat_ref, sums_ref, normed_ref, gain_ref, out_ref) = refs[:-5], refs[-5:]
    width = pieces[0].shape[1]
    inv = inv_std(columns(stat_ref[...])[:, 1:2], full_width)
    sums = columns(sums_ref[...]) * (1.0 / full_width)
    mean, slope = inv * sums[:, :1], inv * sums[:, 1:2]

    def store(slot, ref):
        cols = pl.ds(slot * width, width)
        hat = normed_ref[:, cols].astype(F32) / gain_ref[:, cols]
        out_ref[:, cols] = (ref[...].astype(F32) - mean - hat * slope).astype(BF16)

    by_member(member_ref, pieces, store)


def branch_rows(full_width, member, chain, stat, sums, normed, gain):
    pieces = [chain.piece, *chain.low[1:], *chain.high[1:]]
    rows, width = chain.piece.shape
    wide = pl.BlockSpec((TILE, width), lambda i, m: (i, 0))
    narrow = pl.BlockSpec((8, TILE), lambda i, m: (0, i))
    whole = pl.BlockSpec((TILE, full_width), lambda i, m: (i, 0))
    return pl.pallas_call(
        functools.partial(branch_kernel, full_width),
        grid_spec=pltpu.PrefetchScalarGridSpec(
            num_scalar_prefetch=1,
            grid=(rows // TILE,),
            in_specs=[wide] * len(pieces)
            + [narrow, narrow, whole, pl.BlockSpec((1, full_width), lambda i, m: (0, 0))],
            out_specs=whole,
        ),
        out_shape=jax.ShapeDtypeStruct((rows, full_width), BF16),
        compiler_params=pltpu.CompilerParams(vmem_limit_bytes=32 * 2**20),
        name="branch_rows",
    )(member, *pieces, stat, sums, normed, gain)


def mlp_back_kernel(full_width, own, up, down, x, stat_ref, gain_ref, cot, out_ref, low_ref, sums_ref, gain_grad_ref):
    @pl.when(pl.program_id(0) == 0)
    def _():
        gain_grad_ref[...] = jnp.zeros_like(gain_grad_ref)

    stat = columns(stat_ref[...])
    grad = own[...] + up[...].astype(F32) + down[...].astype(F32)
    out_ref[...] = grad
    inv = inv_std(stat[:, 1:2], full_width)
    product = grad * ((x[...] - stat[:, :1]) * inv)
    low_ref[...] = (cot[...] + inv * (grad * gain_ref[...])).astype(BF16)
    gain_grad_ref[...] += jnp.sum(product.reshape(TILE // 8, 8, -1), axis=0)
    acc = put_lane(jnp.zeros((TILE, LANES), F32), 0, row_sum(grad * gain_ref[...]))
    acc = put_lane(acc, 1, row_sum(product * gain_ref[...]))
    sums_ref[...] = acc.T[:8]


def mlp_back_rows(full_width, own, up, down, residual, stat, gain, cot):
    rows, width = residual.shape
    wide = pl.BlockSpec((TILE, width), lambda i: (i, 0))
    narrow = pl.BlockSpec((8, TILE), lambda i: (0, i))
    return pl.pallas_call(
        functools.partial(mlp_back_kernel, full_width),
        grid=(rows // TILE,),
        in_specs=[wide] * 4 + [narrow, pl.BlockSpec((1, width), lambda i: (0, 0)), wide],
        out_specs=[wide, wide, narrow, pl.BlockSpec((8, width), lambda i: (0, 0))],
        out_shape=[
            jax.ShapeDtypeStruct((rows, width), F32),
            jax.ShapeDtypeStruct((rows, width), BF16),
            jax.ShapeDtypeStruct((8, rows), F32),
            jax.ShapeDtypeStruct((8, width), F32),
        ],
        compiler_params=pltpu.CompilerParams(vmem_limit_bytes=32 * 2**20),
        name="mlp_back_rows",
    )(own, up, down, residual, stat, gain, cot)


def resid_grad_kernel(full_width, grad, x, stat_ref, sums_ref, gain_ref, cot, out_ref):
    stat = columns(stat_ref[...])
    sums = columns(sums_ref[...]) * (1.0 / full_width)
    inv = inv_std(stat[:, 1:2], full_width)
    hat = (x[...] - stat[:, :1]) * inv
    value = cot[...] + inv * (grad[...] * gain_ref[...] - sums[:, :1] - hat * sums[:, 1:2])
    out_ref[...] = value


def resid_grad_rows(full_width, grad, residual, stat, sums, gain, cot):
    rows, width = residual.shape
    wide = pl.BlockSpec((TILE, width), lambda i: (i, 0))
    narrow = pl.BlockSpec((8, TILE), lambda i: (0, i))
    return pl.pallas_call(
        functools.partial(resid_grad_kernel, full_width),
        grid=(rows // TILE,),
        in_specs=[wide, wide, narrow, narrow, pl.BlockSpec((1, width), lambda i: (0, 0)), wide],
        out_specs=wide,
        out_shape=jax.ShapeDtypeStruct((rows, width), F32),
        compiler_params=pltpu.CompilerParams(vmem_limit_bytes=32 * 2**20),
        name="resid_grad_rows",
    )(grad, residual, stat, sums, gain, cot)


def rows_product_kernel(n, *refs):
    former, latter, out_ref = refs[:n], refs[n : 2 * n], refs[-1]
    total = 0.0
    for c in range(n):
        total = total + contract_rows(former[c][...], latter[c][...])
    out_ref[...] = total.astype(BF16)


def rows_product(former, latter, out_cols, first, held, others=(), slot=None, half=None):
    n = len(former)
    rows, height = former[0].shape[-2:]
    width = latter[0].shape[1]
    skip = 0
    if half is not None:
        width //= 2
        out_cols //= 2
    tile_m, tile_n = min(512, height), min(2048, width)
    begin = first // tile_n
    if half:
        skip = width // tile_n
    free = [*others] + ([] if held is None else [held])
    return pl.pallas_call(
        functools.partial(rows_product_kernel, n),
        grid=(height // tile_m, width // tile_n),
        in_specs=[
            pl.BlockSpec((rows, tile_m), lambda i, j: (0, i))
            if slot is None
            else pl.BlockSpec((None, rows, tile_m), lambda i, j: (slot, 0, i))
        ]
        * n
        + [pl.BlockSpec((rows, tile_n), lambda i, j: (0, skip + j))] * n
        + [pl.BlockSpec(memory_space=pl.ANY)] * len(free),
        out_specs=pl.BlockSpec((tile_m, tile_n), lambda i, j: (i, begin + j)),
        out_shape=jax.ShapeDtypeStruct((height, out_cols), BF16),
        input_output_aliases={} if held is None else {2 * n + len(others): 0},
        compiler_params=pltpu.CompilerParams(vmem_limit_bytes=48 * 2**20),
        name="rows_product",
    )(*former, *latter, *free)


def local(
    history,
    mix_in,
    mix_out,
    mix_static,
    stream_gain,
    qkv_weight,
    out_weight,
    mlp_gain,
    up_weight,
    down_weight,
    out_grad,
    seq_group,
    group_weight,
):
    n_stream = lax.axis_size("stream")
    member = lax.axis_index("stream")
    n_hist, tokens, width = history.shape
    assert tokens == SEQ
    full_width = width * n_stream
    rows = tokens // CHUNKS
    both = range(CHUNKS)
    spans = [slice(c * rows, (c + 1) * rows) for c in both]
    first_col = member * width
    mixh = mix_in.shape[1]
    ff = up_weight.shape[1]
    order = Order()

    def rows_of(weight, idx):
        begin = lax.rem(member + idx, n_stream) * width
        return lax.dynamic_slice_in_dim(weight, begin, width, 0)

    def dp_sum(part):
        return lax.psum_scatter(part, "dp", scatter_dimension=0, tiled=True).astype(F32)

    mix_in_rows = lax.dynamic_slice_in_dim(mix_in, first_col, width, 0)
    mix_out_float = mix_out.astype(F32)

    last = history[n_hist - 1]
    square_part = jnp.sum(jnp.square(last.astype(F32)), axis=1)[None]
    raw_part = dot_tt(mix_in_rows, last, ((0,), (1,)))
    raw = Butterfly(jnp.concatenate([raw_part, square_part], axis=0))
    order.send(raw)

    here = member.astype(jnp.int32).reshape(1)
    qkv_rows = jnp.transpose(order.hold(qkv_weight), (1, 0, 2))
    order.did(qkv_rows)

    group_pick = (
        seq_group[:, None] == jnp.arange(group_weight.shape[0], dtype=jnp.int32)[None, :]
    ).astype(F32)
    seq_weight = jnp.sum(group_pick * group_weight.astype(F32)[None, :]) * COT_SCALE
    out_grad_held = order.hold(out_grad)
    cot_cols = [out_grad_held[spans[c]].astype(F32) * seq_weight for c in both]
    cot = [LineGather(cot_cols[c].astype(BF16), member) for c in both]
    order.did(cot[0].piece, cot[1].piece)
    order.send(raw)
    order.send(cot[0])

    sums = raw.value()
    raw_t = sums[:-1]
    scale_t = lax.rsqrt(sums[-1:] / full_width + EPS_MIX)
    act_t, slope_t = gelu_both(scale_t * raw_t)
    coef = (dot_tt(mix_out_float, act_t, ((0,), (0,)), HIGH) + mix_static.reshape(-1, 1)).T

    streams, moments = [None] * 2, [None] * 2
    stat, stat_rows, normed_chain = [None] * 2, [None] * 2, [None] * 2
    resid_streams, early_chain = [None] * 2, []

    def mix(c):
        *streams[c], sums = mix_streams(history, coef, c, (0, 1, 2), True)
        moments[c] = Butterfly(sums, merge=moments_merger(width, 3))

    def norm(c):
        stat_rows[c] = moments[c].value()
        pair, single, stat[c] = norm_streams(full_width, streams[c], stat_rows[c], stream_gain)
        normed_chain[c] = [LineGather(pair, member), LineGather(single, member)]

    def early(c):
        sums = early_dots(history, [order.hold(streams[c][0]), *streams[c][1:]], stat[c], c)
        order.did(sums)
        early_chain.append(Butterfly(sums))

    def mix_resid(c):
        (resid_streams[c],) = mix_streams(history, order.hold(coef), c, (3,), False)
        order.did(resid_streams[c])

    mix(0)
    mix(1)
    order.send(*moments)
    order.send(*moments)
    norm(0)
    order.send(normed_chain[0][0])
    order.send(normed_chain[0][1])
    norm(1)
    order.did(normed_chain[1][0].piece)
    mix_resid(0)
    order.send(normed_chain[0][0])
    order.send(normed_chain[0][1])
    early(0)
    order.send(normed_chain[0][0])
    order.send(normed_chain[0][1])
    mix_resid(1)
    order.send(normed_chain[1][0])
    order.send(normed_chain[1][1])

    normed, query, key, value, heads_out, lse = [], [], [], [], [], []
    branch = []

    def project(c):
        normed.append([chain.value() for chain in normed_chain[c]])
        for held, s, full in ((query, 0, normed[c][0][0]), (key, 1, normed[c][0][1]), (value, 2, normed[c][1])):
            held.append(jnp.dot(full, qkv_rows[s], preferred_element_type=F32).astype(BF16))

    def attend(c):
        out, out_lse = attend_forward(query[c], key[: c + 1], value[: c + 1])
        heads_out.append(out)
        lse.append(out_lse)
        branch.append(
            LineScatter(
                order, lambda idx, hold: times_transpose(hold(out), rows_of(out_weight, idx))
            )
        )

    residual, resid_moments = [], []
    mlp_gain_cols = lax.dynamic_slice_in_dim(mlp_gain, first_col, width, 0)[None, :]
    mlp_in, mlp_moments = [], []
    normed_mlp, hidden, d_hpre, mlp_back, mlp_out = [], [], [], [], []

    def end_branch(c):
        value, low, stats = residual_rows(here, *branch[c].pieces(), resid_streams[c])
        residual.append(value)
        resid_moments.append(Butterfly(stats))
        mlp_in.append(LineGather(low, member))

    cot_low, d_hidden = [], []

    def down_back(c):
        cot_low.append(cot[c].value())
        d_hidden.append(
            jnp.dot(order.hold(cot_low[c]), down_weight, preferred_element_type=F32)
        )
        order.did(d_hidden[c])

    def mlp(c):
        full, moments_all = normed_rows(
            full_width, here, mlp_in[c], resid_moments[c].value(), mlp_gain[None, :]
        )
        normed_mlp.append(full)
        mlp_moments.append(moments_all)
        hidden_pre = jnp.dot(normed_mlp[c], up_weight, preferred_element_type=F32)
        act, slope = gelu_both(hidden_pre)
        act = act.astype(BF16)
        d_pre = (d_hidden[c] * slope).astype(BF16)
        hidden.append(act)
        d_hpre.append(d_pre)
        mlp_back.append(
            LineScatter(
                order, lambda idx, hold: times_transpose(hold(d_pre), rows_of(up_weight, idx))
            )
        )
        mlp_out.append(
            LineScatter(
                order, lambda idx, hold: times_transpose(hold(act), rows_of(down_weight, idx))
            )
        )

    def weight_part(former, latter, out_cols, others):
        return rows_product(former, latter, out_cols, 0, None, others)

    d_normed_mlp, back_sums, mlp_gain_shares = [], [], []

    resid_grad, branch_grad = [], []

    def end_mlp_back(c):
        value, low, sums, share = mlp_back_rows(
            full_width, *mlp_back[c].pieces(), residual[c], mlp_moments[c], mlp_gain_cols,
            cot_cols[c],
        )
        d_normed_mlp.append(value)
        back_sums.append(Butterfly(sums))
        mlp_gain_shares.append(share)
        branch_grad.append(LineGather(low, member))

    d_branch, d_proj = [], []
    carried = [None]

    def attend_back(c):
        sums = back_sums[c].value()
        d_branch.append(
            branch_rows(
                full_width, here, branch_grad[c], mlp_moments[c], sums, normed_mlp[c],
                mlp_gain[None, :],
            )
        )
        resid_grad.append(
            resid_grad_rows(
                full_width, d_normed_mlp[c], residual[c], mlp_moments[c], sums, mlp_gain_cols,
                cot_cols[c],
            )
        )
        d_heads = jnp.dot(d_branch[c], out_weight, preferred_element_type=F32).astype(BF16)
        d_query, dk, dv = attend_backward(
            query[c], d_heads, lse[c], key[: c + 1], value[: c + 1], carried[0], c == CHUNKS - 1
        )
        carried[0] = (dk, dv)
        d_proj.append([d_query, None, None])
        if c == CHUNKS - 1:
            for i in both:
                d_proj[i][1:] = [dk[i], dv[i]]

    project(0)
    attend(0)
    order.send(branch[0])
    branch[0].prepare()
    order.send(normed_chain[1][0])
    order.send(branch[0])
    branch[0].prepare()
    order.send(normed_chain[1][1])
    early(1)
    order.send(branch[0])
    branch[0].prepare()
    order.send(normed_chain[1][0])
    order.send(normed_chain[1][1])
    end_branch(0)
    order.send(resid_moments[0], cot[0])
    project(1)
    order.send(resid_moments[0])
    order.send(cot[0])
    attend(1)
    order.send(branch[1], mlp_in[0])
    branch[1].prepare()
    down_back(0)
    order.send(branch[1], mlp_in[0])
    branch[1].prepare()
    order.send(branch[1], mlp_in[0])
    branch[1].prepare()
    order.send(cot[1])
    end_branch(1)
    order.send(mlp_in[1], resid_moments[1])
    mlp(0)
    order.send(cot[1])
    order.send(mlp_in[1], mlp_back[0], resid_moments[1])
    mlp_back[0].prepare()
    order.send(cot[1])
    order.send(mlp_in[1], mlp_back[0])
    mlp_back[0].prepare()
    down_back(1)
    order.send(mlp_back[0])
    mlp_back[0].prepare()
    mlp(1)
    end_mlp_back(0)
    order.send(mlp_back[1], branch_grad[0])
    mlp_back[1].prepare()
    order.send(mlp_back[1], branch_grad[0], back_sums[0])
    mlp_back[1].prepare()
    order.send(mlp_back[1], branch_grad[0], back_sums[0])
    mlp_back[1].prepare()
    end_mlp_back(1)
    mlp_out[0].prepare()
    order.send(branch_grad[1], mlp_out[0])
    mlp_out[0].prepare()
    attend_back(0)
    order.send(branch_grad[1], mlp_out[0], back_sums[1])
    chain = branch_grad[1]
    chain.low[-1], chain.high[-1], d_proj[0][0] = lax.optimization_barrier(
        (chain.low[-1], chain.high[-1], d_proj[0][0])
    )
    mlp_out[0].prepare()
    order.send(branch_grad[1], mlp_out[0], back_sums[1])
    mlp_out[0].prepare()
    mlp_out[1].prepare()
    attend_back(1)
    order.send(mlp_out[1])
    mlp_out[1].prepare()

    grads = [ProductScatter(order, here, d_proj[c], qkv_rows) for c in both]
    own = [None] * 2
    early_one = Butterfly(jnp.concatenate([chain.now for chain in early_chain], axis=1))
    order.send(*grads, early_one)
    out_part = weight_part(d_branch, heads_out, width, grads[0].came)
    down_part = weight_part(cot_low, hidden, ff, grads[1].came)
    order.send(*grads, early_one)
    up_part = weight_part(normed_mlp, d_hpre, ff, grads[0].came)
    qkv_part = None
    for s in range(3):
        qkv_part = rows_product(
            [normed[c][s // 2] for c in both], [d_proj[c][s] for c in both], 3 * width, s * width,
            qkv_part, grads[1].came, s if s < 2 else None,
        )
    order.send(*grads)
    down_grad = dp_sum(down_part)
    own = [grads[c].own() for c in both]
    up_grad, out_weight_grad = [dp_sum(part) for part in (up_part, out_part)]
    qkv_sum = lax.psum_scatter(qkv_part, "dp", scatter_dimension=0, tiled=True)
    qkv_grad = jnp.stack(
        [qkv_sum[:, s * width : (s + 1) * width] for s in range(3)], axis=1
    ).astype(F32)
    gain_part = jnp.sum(mlp_gain_shares[0] + mlp_gain_shares[1], axis=0)
    gain_chain = Butterfly(
        jnp.where(
            jnp.arange(n_stream)[:, None] == member,
            gain_part[None, :],
            jnp.zeros((n_stream, width), F32),
        )
    )

    mix_out_wide = jnp.pad(
        mix_out_float.reshape(-1, 4, n_hist), ((0, 0), (0, 0), (0, SLOT - n_hist))
    ).reshape(-1, 4 * SLOT)
    mix_in_wide = jnp.pad(mix_in_rows.astype(F32), ((0, 0), (0, LANES - mixh)))
    d_normed, late, gain_shares, shares = [], [], [], []
    history_grad = [None]

    def late_sums(c):
        *scaled, sums, gain_share = late_dots(
            history, streams[c], stat[c], stream_gain, resid_grad[c], own[c], grads[c].came, c
        )
        d_normed.append(scaled)
        late.append(Butterfly(sums))
        gain_shares.append(gain_share)

    def coefs(c):
        shares.append(
            coef_grads(
                full_width, n_hist, early_one.value(), late[c].value(), stat_rows[c], act_t,
                slope_t, raw_t, scale_t, mix_out_wide, mix_in_wide, last, c,
            )
        )

    def layers(c, others):
        _, _, turned, extra = shares[c]
        history_grad[0] = layer_grads(
            coef, streams[c], stat[c], turned, d_normed[c], resid_grad[c], extra, c,
            history_grad[0], tokens, others,
        )
        order.did(history_grad[0])

    late_sums(0)
    order.did(qkv_part)
    order.send(late[0], gain_chain)
    order.send(mlp_out[1])
    mlp_out[1].prepare()
    late_sums(1)
    order.send(late[0], late[1], gain_chain)
    coefs(0)
    order.send(late[1])
    coefs(1)
    out_share, in_share = [shares[0][i] + shares[1][i] for i in range(2)]
    gain_share = jnp.sum(gain_shares[0] + gain_shares[1], axis=1)
    out_share = jnp.pad(out_share, ((0, 0), (0, width - 4 * SLOT)))
    small = Butterfly(
        jnp.concatenate([out_share, in_share, gain_share, gain_chain.value()], axis=0), ("dp",)
    )
    layers(0, (small.now,))
    order.send(small)
    order.send(mlp_out[1])
    layers(1, ())
    while small.turns:
        order.send(small)
    output_cols = jnp.concatenate(
        [(residual[c] + mlp_out[c].value()).astype(BF16) for c in both], axis=0
    )
    small = small.value()
    top = out_share.shape[0]
    by_slot = small[:top, : 4 * SLOT].reshape(-1, 4, SLOT)[:, :, :n_hist]
    return (
        output_cols,
        history_grad[0],
        small[top : top + mixh].T,
        by_slot[:mixh].reshape(mixh, 4 * n_hist),
        by_slot[SCALE_ROW],
        small[top + mixh : top + mixh + 3],
        qkv_grad,
        out_weight_grad,
        small[top + mixh + 3 :].reshape(full_width),
        up_grad,
        down_grad,
    )


def solution(mesh):
    in_specs = (
        P(None, "dp", "stream"),
        P(),
        P(),
        P(),
        P(None, "stream"),
        P(None, None, "stream"),
        P(None, "stream"),
        P(),
        P(None, "stream"),
        P(None, "stream"),
        P("dp", "stream"),
        P("dp"),
        P(),
    )
    out_specs = (
        P("dp", "stream"),
        P(None, "dp", "stream"),
        P("stream", None),
        P(),
        P(),
        P(None, "stream"),
        P("dp", None, "stream"),
        P("dp", "stream"),
        P(),
        P("dp", "stream"),
        P("dp", "stream"),
    )
    return jax.shard_map(local, mesh=mesh, in_specs=in_specs, out_specs=out_specs, check_vma=False)
```

```python
import functools
import math

import jax
import jax.numpy as jnp
from jax import lax
from jax.experimental import pallas as pl
from jax.experimental.pallas import tpu as pltpu
from jax.sharding import PartitionSpec as P

HEAD_DIM = 128
SEQ = 1024
CHUNKS = 2
SUB = 512

HIGH = lax.Precision.HIGHEST
EPS_NORM = 1e-05
EPS_MIX = 1e-06
COT_SCALE = 0.4
F32 = jnp.float32
BF16 = jnp.bfloat16


def gelu_both(values):
    cdf = 0.5 * (1.0 + lax.erf(values * math.sqrt(0.5)))
    density = jnp.exp(-0.5 * jnp.square(values)) * (1.0 / math.sqrt(2.0 * math.pi))
    return values * cdf, cdf + values * density


def dot_tt(former, latter, dims, precision=None):
    return lax.dot_general(
        former, latter, (dims, ((), ())), precision=precision, preferred_element_type=F32
    )


def contract_rows(former, latter):
    return dot_tt(former, latter, ((0,), (0,)))


def times_transpose(former, latter):
    return dot_tt(former, latter, ((1,), (1,)))


def after(value, *others):
    return lax.optimization_barrier((value, *others))[0]


class Order:
    def __init__(self):
        self.tick = ()

    def hold(self, value):
        return after(value, *self.tick) if self.tick else value

    def did(self, *outs):
        self.tick = (*self.tick, *outs)

    def send(self, *chains):
        items = [chain.items() for chain in chains]
        flat = [value for chain_items in items for value, _, _ in chain_items]
        held = lax.optimization_barrier((*flat, *self.tick))[: len(flat)]
        self.tick = tuple(held)
        at = 0
        for chain, chain_items in zip(chains, items):
            got = []
            for _, axis, perm in chain_items:
                got.append(lax.ppermute(held[at], axis, perm))
                at += 1
            chain.take(got)


class LineGather:
    def __init__(self, piece, member):
        self.piece, self.member = piece, member
        self.low, self.high = [piece], [piece]

    def items(self):
        n, step = lax.axis_size("stream"), len(self.low)
        return [
            (self.low[-1], "stream", [(i, i + 1) for i in range(step - 1, n - 1)]),
            (self.high[-1], "stream", [(i, i - 1) for i in range(1, n - step + 1)]),
        ]

    def take(self, got):
        self.low.append(got[0])
        self.high.append(got[1])

    def value(self):
        n, member = lax.axis_size("stream"), self.member
        slots = []
        for slot in range(n):
            value = self.piece
            for at in range(n):
                if at > slot:
                    value = jnp.where(member == at, self.low[at - slot], value)
                elif at < slot:
                    value = jnp.where(member == at, self.high[slot - at], value)
            slots.append(value)
        return jnp.concatenate(slots, axis=-1)


class LineScatter:
    def __init__(self, order, block):
        self.order, self.block = order, block
        self.parts, self.came, self.step = {}, None, 0

    def part(self, idx):
        if idx not in self.parts:
            self.parts[idx] = self.block(idx, lambda value: value)
        return self.parts[idx]

    def items(self):
        n, step = lax.axis_size("stream"), self.step
        up_idx, down_idx = n - 1 - step, 1 + step
        up_value, down_value = self.part(up_idx), self.part(down_idx)
        if self.came is not None:
            up, down = [got.astype(F32) for got in self.came]
            if up_idx == down_idx:
                up_value = down_value = up_value + up + down
            else:
                up_value, down_value = up_value + up, down_value + down
        return [
            (up_value.astype(BF16), "stream", [(i, i + 1) for i in range(step + 1)]),
            (down_value.astype(BF16), "stream", [(i, i - 1) for i in range(n - 1 - step, n)]),
        ]

    def take(self, got):
        self.came = got
        self.step += 1

    def prepare(self):
        n, step = lax.axis_size("stream"), self.step
        for idx in {n - 1 - step, (1 + step) % n}:
            if idx not in self.parts:
                self.parts[idx] = self.block(idx, self.order.hold)
                self.order.did(self.parts[idx])

    def pieces(self):
        return self.part(0), *self.came

    def value(self):
        own, up, down = self.pieces()
        return own + up.astype(F32) + down.astype(F32)


class ProductScatter(LineScatter):
    def __init__(self, order, member, lhs, weight):
        super().__init__(order, None)
        self.args = (member, lhs, weight)

    def items(self):
        n, step = lax.axis_size("stream"), self.step
        up_turn, down_turn = n - 1 - step, 1 + step
        turns = (up_turn,) if up_turn == down_turn else (up_turn, down_turn)
        values = send_values(*self.args, turns, self.came)
        return [
            (values[0], "stream", [(i, i + 1) for i in range(step + 1)]),
            (values[-1], "stream", [(i, i - 1) for i in range(n - 1 - step, n)]),
        ]

    def own(self):
        member, lhs, weight = self.args
        (value,) = send_values(member, [self.order.hold(lhs[0]), *lhs[1:]], weight, (0,), None, F32)
        self.order.did(value)
        return value


class Butterfly:
    def __init__(self, value, axes=("stream",), merge=jnp.add):
        self.now, self.merge = value, merge
        self.turns = [(axis, 1 << i) for axis in axes for i in range(lax.axis_size(axis).bit_length() - 1)]
        assert all(lax.axis_size(axis) & (lax.axis_size(axis) - 1) == 0 for axis in axes)

    def items(self):
        axis, span = self.turns[0]
        return [(self.now, axis, [(i, i ^ span) for i in range(lax.axis_size(axis))])]

    def take(self, got):
        self.turns = self.turns[1:]
        self.now = self.merge(self.now, got[0])

    def value(self):
        assert not self.turns
        return self.now


def moments_merger(width, half):
    count = [width]

    def merge(mine, other):
        row = lax.broadcasted_iota(jnp.int32, mine.shape, 0)
        total = mine + other
        gap = jnp.roll(mine - other, half, axis=0)
        square = total + jnp.square(gap) * (0.5 * count[0])
        count[0] *= 2
        return jnp.where(row < half, 0.5 * total, square)

    return merge


def attend_forward_kernel(chunk, q_ref, *refs):
    k_refs, v_refs = refs[: chunk + 1], refs[chunk + 1 : 2 * chunk + 2]
    o_ref, lse_ref = refs[2 * chunk + 2 :]
    rows = q_ref.shape[0]
    keys = jnp.concatenate([ref[...] for ref in k_refs], axis=0)
    values = jnp.concatenate([ref[...] for ref in v_refs], axis=0)
    for sub in range(rows // SUB):
        count = chunk * rows + (sub + 1) * SUB
        span = pl.ds(sub * SUB, SUB)
        scores = times_transpose(keys[:count], q_ref[span, :]) * HEAD_DIM ** (-0.5)
        allowed = lax.broadcasted_iota(jnp.int32, (SUB, SUB), 0) <= lax.broadcasted_iota(
            jnp.int32, (SUB, SUB), 1
        )
        tail = jnp.where(allowed, scores[count - SUB :], -1e30)
        scores = jnp.concatenate([scores[: count - SUB], tail], axis=0) if count > SUB else tail
        top = jnp.max(scores, axis=0, keepdims=True)
        weights = jnp.exp(scores - top)
        total = jnp.sum(weights, axis=0, keepdims=True)
        probs = (weights * (1.0 / total)).astype(BF16)
        lse_ref[0, :, span] = top + jnp.log(total)
        out = contract_rows(values[:count], probs)
        o_ref[span, :] = out.T.astype(BF16)


def attend_forward(queries, keys, values):
    rows, width = queries.shape
    heads = width // HEAD_DIM
    chunk = len(keys) - 1
    spec = pl.BlockSpec((rows, HEAD_DIM), lambda h: (0, h))
    return pl.pallas_call(
        functools.partial(attend_forward_kernel, chunk),
        grid=(heads,),
        in_specs=[spec] * (2 * chunk + 3),
        out_specs=[spec, pl.BlockSpec((1, 1, rows), lambda h: (h, 0, 0))],
        out_shape=[
            jax.ShapeDtypeStruct((rows, width), BF16),
            jax.ShapeDtypeStruct((heads, 1, rows), F32),
        ],
        compiler_params=pltpu.CompilerParams(vmem_limit_bytes=48 * 2**20),
        name="attend_forward",
    )(queries, *keys, *values)


def attend_backward_kernel(chunk, q_ref, do_ref, lse_ref, *refs):
    n = chunk + 1
    k_refs, v_refs, refs = refs[:n], refs[n : 2 * n], refs[2 * n :]
    dk_in, dv_in, refs = refs[:chunk], refs[chunk : 2 * chunk], refs[2 * chunk :]
    dq_ref, dk_refs, dv_refs, (dk_acc, dv_acc) = refs[0], refs[1 : 1 + n], refs[1 + n : 1 + 2 * n], refs[1 + 2 * n :]
    rows = q_ref.shape[0]
    keys = jnp.concatenate([ref[...] for ref in k_refs], axis=0)
    values = jnp.concatenate([ref[...] for ref in v_refs], axis=0)
    for i in range(n):
        here = pl.ds(i * rows, rows)
        dk_acc[here, :] = dk_in[i][...] if i < chunk else jnp.zeros((rows, HEAD_DIM), F32)
        dv_acc[here, :] = dv_in[i][...] if i < chunk else jnp.zeros((rows, HEAD_DIM), F32)
    scale = HEAD_DIM ** (-0.5)
    for sub in range(rows // SUB):
        count = chunk * rows + (sub + 1) * SUB
        span = pl.ds(sub * SUB, SUB)
        query, grad = q_ref[span, :], do_ref[span, :]
        scores = times_transpose(keys[:count], query) * scale
        probs = jnp.exp(scores - lse_ref[0, :, span])
        allowed = lax.broadcasted_iota(jnp.int32, (SUB, SUB), 0) <= lax.broadcasted_iota(
            jnp.int32, (SUB, SUB), 1
        )
        tail = jnp.where(allowed, probs[count - SUB :], 0.0)
        probs = jnp.concatenate([probs[: count - SUB], tail], axis=0) if count > SUB else tail
        prob_grad = times_transpose(values[:count], grad)
        row_dot = jnp.sum(probs * prob_grad, axis=0, keepdims=True)
        score_grad = (probs * (prob_grad - row_dot)).astype(BF16)
        dq_ref[span, :] = (contract_rows(keys[:count], score_grad) * scale).T.astype(BF16)
        dk_acc[pl.ds(0, count), :] += jnp.dot(score_grad, query, preferred_element_type=F32) * scale
        dv_acc[pl.ds(0, count), :] += jnp.dot(
            probs.astype(BF16), grad, preferred_element_type=F32
        )
    for i in range(n):
        dk_refs[i][...] = dk_acc[pl.ds(i * rows, rows), :].astype(dk_refs[i].dtype)
        dv_refs[i][...] = dv_acc[pl.ds(i * rows, rows), :].astype(dv_refs[i].dtype)


def attend_backward(queries, grad, lse, keys, values, sums, final):
    rows, width = queries.shape
    heads = width // HEAD_DIM
    chunk = len(keys) - 1
    n = chunk + 1
    spec = pl.BlockSpec((rows, HEAD_DIM), lambda h: (0, h))
    dk_dv = [jax.ShapeDtypeStruct((rows, width), BF16 if final else F32)] * (2 * n)
    carried = [] if sums is None else [*sums[0], *sums[1]]
    outs = pl.pallas_call(
        functools.partial(attend_backward_kernel, chunk),
        grid=(heads,),
        in_specs=[spec, spec, pl.BlockSpec((1, 1, rows), lambda h: (h, 0, 0))]
        + [spec] * (2 * n + len(carried)),
        out_specs=[spec] * (1 + 2 * n),
        out_shape=[jax.ShapeDtypeStruct((rows, width), BF16), *dk_dv],
        scratch_shapes=[pltpu.VMEM((n * rows, HEAD_DIM), F32)] * 2,
        compiler_params=pltpu.CompilerParams(vmem_limit_bytes=48 * 2**20),
        name="attend_backward",
    )(queries, grad, lse, *keys, *values, *carried)
    return outs[0], outs[1 : 1 + n], outs[1 + n :]


GROUP = 128
VMEM_MOST = 60 * 2**20
TILE = 128
SLOT = 16
SCALE_ROW = 48
MEAN_ROW = 56
LANES = 128


def put_lane(acc, idx, column):
    lane = lax.broadcasted_iota(jnp.int32, acc.shape, 1)
    return jnp.where(lane == idx, column, acc)


def row_sum(values):
    return jnp.sum(values, axis=1, keepdims=True)


def spread(values, idx):
    return jnp.broadcast_to(values[:, idx : idx + 1], (values.shape[0], LANES))


def by_groups(tile, body):
    def step(i, carry):
        body(pl.ds(pl.multiple_of(i * GROUP, GROUP), GROUP))
        return carry

    lax.fori_loop(0, tile // GROUP, step, 0)


def mix_kernel(picked, hist_ref, coef_ref, *refs):
    out_refs, stat_ref, stat_acc = refs[: len(picked)], *(refs[len(picked) :] or (None, None))
    n_hist, tile, width = hist_ref.shape

    def group(span):
        coef = coef_ref[span, :]
        cols = {(s, j): spread(coef, s * n_hist + j) for s in picked for j in range(n_hist)}
        pivots, sums, squares = [], [], []
        for w in range(width // LANES):
            lanes = pl.ds(w * LANES, LANES)
            totals = [0.0] * len(picked)
            for j in range(n_hist):
                layer = hist_ref[j, span, lanes].astype(F32)
                for i, s in enumerate(picked):
                    totals[i] = totals[i] + cols[s, j] * layer
            for i, total in enumerate(totals):
                out_refs[i][span, lanes] = total
                if stat_ref is None:
                    continue
                if w == 0:
                    pivots.append(spread(total, 0))
                    sums.append(0.0)
                    squares.append(0.0)
                gap = total - pivots[i]
                sums[i] = sums[i] + gap
                squares[i] = squares[i] + jnp.square(gap)
        if stat_ref is not None:
            stats = jnp.zeros((GROUP, LANES), F32)
            for i in range(len(picked)):
                shift = row_sum(sums[i]) * (1.0 / width)
                stats = put_lane(stats, i, pivots[i] + shift)
                stats = put_lane(stats, len(picked) + i, row_sum(squares[i]) - shift * shift * width)
            stat_acc[span, :] = stats

    by_groups(tile, group)
    if stat_ref is not None:
        stat_ref[...] = stat_acc[...].T[: stat_ref.shape[0]]


def mix_streams(history, coef, chunk, picked, with_stats):
    n_hist, tokens, width = history.shape
    rows = tokens // CHUNKS
    base = chunk * rows // TILE
    wide = pl.BlockSpec((TILE, width), lambda i: (i, 0))
    n = len(picked)
    return pl.pallas_call(
        functools.partial(mix_kernel, picked),
        grid=(rows // TILE,),
        in_specs=[
            pl.BlockSpec((n_hist, TILE, width), lambda i: (0, base + i, 0)),
            pl.BlockSpec((TILE, 4 * n_hist), lambda i: (base + i, 0)),
        ],
        out_specs=[wide] * n + ([pl.BlockSpec((8, TILE), lambda i: (0, i))] if with_stats else []),
        out_shape=[jax.ShapeDtypeStruct((rows, width), F32)] * n
        + ([jax.ShapeDtypeStruct((8, rows), F32)] if with_stats else []),
        scratch_shapes=[pltpu.VMEM((TILE, LANES), F32)] if with_stats else [],
        compiler_params=pltpu.CompilerParams(vmem_limit_bytes=VMEM_MOST),
        name="mix_streams",
    )(history, coef)


def hat_of(stream, stat, s):
    return (stream - spread(stat, s)) * spread(stat, 3 + s)


def early_kernel(hist_ref, x0, x1, x2, stat_ref, sums_ref, acc_ref):
    n_hist, tile, width = hist_ref.shape

    def group(span):
        stat = stat_ref[span, :]
        sums = jnp.zeros((GROUP, LANES), F32)
        pieces = [pl.ds(w * LANES, LANES) for w in range(width // LANES)]
        others = [[hat_of(x[span, p], stat, s) for p in pieces] for s, x in enumerate((x0, x1, x2))]
        for j in range(n_hist):
            layer = [hist_ref[j, span, p].astype(F32) for p in pieces]
            sums = put_lane(sums, j, row_sum(sum(layer[1:], layer[0])))
            for s in range(3):
                terms = [x * y for x, y in zip(others[s], layer)]
                sums = put_lane(sums, (s + 1) * SLOT + j, row_sum(sum(terms[1:], terms[0])))
        acc_ref[span, :] = sums

    by_groups(tile, group)
    sums_ref[...] = acc_ref[...].T[: sums_ref.shape[0]]


def early_dots(history, streams, stat, chunk):
    n_hist, tokens, width = history.shape
    rows = stat.shape[0]
    base = chunk * rows // TILE
    wide = pl.BlockSpec((TILE, width), lambda i: (i, 0))
    return pl.pallas_call(
        early_kernel,
        grid=(rows // TILE,),
        in_specs=[
            pl.BlockSpec((n_hist, TILE, width), lambda i: (0, base + i, 0)),
            wide,
            wide,
            wide,
            pl.BlockSpec((TILE, LANES), lambda i: (i, 0)),
        ],
        out_specs=pl.BlockSpec((4 * SLOT, TILE), lambda i: (0, i)),
        out_shape=jax.ShapeDtypeStruct((4 * SLOT, rows), F32),
        scratch_shapes=[pltpu.VMEM((TILE, LANES), F32)],
        compiler_params=pltpu.CompilerParams(vmem_limit_bytes=VMEM_MOST),
        name="early_dots",
    )(history, *streams, stat)


def late_kernel(hist_ref, x0, x1, x2, stat_ref, gain_ref, resid_ref, own, up, down, g0, g1, g2, sums_ref, gain_grad_ref, acc_ref):
    grad_refs = (g0, g1, g2)
    n_hist, tile, width = hist_ref.shape

    @pl.when(pl.program_id(0) == 0)
    def _():
        gain_grad_ref[...] = jnp.zeros_like(gain_grad_ref)

    def group(span):
        stat = stat_ref[span, :]
        sums = jnp.zeros((GROUP, LANES), F32)
        pieces = [pl.ds(w * LANES, LANES) for w in range(width // LANES)]
        grads = []
        for s, x in enumerate((x0, x1, x2)):
            scaled, dots = [], []
            for p in pieces:
                d = own[s, span, p] + up[s, span, p].astype(F32) + down[s, span, p].astype(F32)
                product = d * hat_of(x[span, p], stat, s)
                gain = gain_ref[pl.ds(s, 1), p]
                gain_grad_ref[s, :, p] += jnp.sum(product.reshape(GROUP // 8, 8, LANES), axis=0)
                scaled.append(d * gain)
                dots.append(product * gain)
                grad_refs[s][span, p] = scaled[-1]
            sums = put_lane(sums, s * SLOT + n_hist, row_sum(sum(scaled[1:], scaled[0])))
            sums = put_lane(sums, s * SLOT + n_hist + 1, row_sum(sum(dots[1:], dots[0])))
            grads.append(scaled)
        grads.append([resid_ref[span, p] for p in pieces])
        for j in range(n_hist):
            layer = [hist_ref[j, span, p].astype(F32) for p in pieces]
            for s in range(4):
                terms = [x * y for x, y in zip(grads[s], layer)]
                sums = put_lane(sums, s * SLOT + j, row_sum(sum(terms[1:], terms[0])))
        acc_ref[span, :] = sums

    by_groups(tile, group)
    sums_ref[...] = acc_ref[...].T[: sums_ref.shape[0]]


def late_dots(history, streams, stat, gain, resid_grad, own, came, chunk):
    n_hist, tokens, width = history.shape
    rows = stat.shape[0]
    base = chunk * rows // TILE
    wide = pl.BlockSpec((TILE, width), lambda i: (i, 0))
    three = pl.BlockSpec((3, TILE, width), lambda i: (0, i, 0))
    return pl.pallas_call(
        late_kernel,
        grid=(rows // TILE,),
        in_specs=[
            pl.BlockSpec((n_hist, TILE, width), lambda i: (0, base + i, 0)),
            wide,
            wide,
            wide,
            pl.BlockSpec((TILE, LANES), lambda i: (i, 0)),
            pl.BlockSpec((3, width), lambda i: (0, 0)),
            wide,
            three,
            three,
            three,
        ],
        out_specs=[
            wide,
            wide,
            wide,
            pl.BlockSpec((4 * SLOT, TILE), lambda i: (0, i)),
            pl.BlockSpec((3, 8, width), lambda i: (0, 0, 0)),
        ],
        out_shape=[jax.ShapeDtypeStruct((rows, width), F32)] * 3
        + [
            jax.ShapeDtypeStruct((4 * SLOT, rows), F32),
            jax.ShapeDtypeStruct((3, 8, width), F32),
        ],
        scratch_shapes=[pltpu.VMEM((TILE, LANES), F32)],
        compiler_params=pltpu.CompilerParams(vmem_limit_bytes=VMEM_MOST),
        name="late_dots",
    )(history, *streams, stat, gain, resid_grad, own, *came)


def layers_kernel(coef_ref, x0, x1, x2, stat_ref, mean_ref, d0, d1, d2, resid_ref, extra_ref, *refs):
    out_ref = refs[-1]
    n_hist, tile, width = out_ref.shape

    def group(span):
        stat, coef, means = stat_ref[span, :], coef_ref[span, :], mean_ref[span, :]
        cols = [spread(coef, i) for i in range(4 * n_hist)]
        for w in range(width // LANES):
            p = pl.ds(w * LANES, LANES)
            grads = []
            for s, (x, d) in enumerate(((x0, d0), (x1, d1), (x2, d2))):
                hat = hat_of(x[span, p], stat, s)
                grads.append(
                    spread(stat, 3 + s) * (d[span, p] - spread(means, MEAN_ROW + s) - hat * spread(means, MEAN_ROW + 3 + s))
                )
            grads.append(resid_ref[span, p])
            for j in range(n_hist):
                total = extra_ref[span, p] if j == n_hist - 1 else 0.0
                for s in range(4):
                    total = total + cols[s * n_hist + j] * grads[s]
                out_ref[j, span, p] = total.astype(BF16)

    by_groups(tile, group)


def layer_grads(coef, streams, stat, means, scaled, resid_grad, extra, chunk, held, tokens, others):
    rows, width = resid_grad.shape
    n_hist = coef.shape[1] // 4
    base = chunk * rows // TILE
    wide = pl.BlockSpec((TILE, width), lambda i: (i, 0))
    narrow = pl.BlockSpec((TILE, LANES), lambda i: (i, 0))
    free = [*others] + ([] if held is None else [held])
    return pl.pallas_call(
        layers_kernel,
        grid=(rows // TILE,),
        in_specs=[
            pl.BlockSpec((TILE, 4 * n_hist), lambda i: (base + i, 0)),
            wide,
            wide,
            wide,
            narrow,
            narrow,
            wide,
            wide,
            wide,
            wide,
            wide,
        ]
        + [pl.BlockSpec(memory_space=pl.ANY)] * len(free),
        out_specs=pl.BlockSpec((n_hist, TILE, width), lambda i: (0, base + i, 0)),
        out_shape=jax.ShapeDtypeStruct((n_hist, tokens, width), BF16),
        input_output_aliases={} if held is None else {11 + len(others): 0},
        compiler_params=pltpu.CompilerParams(vmem_limit_bytes=32 * 2**20),
        name="layer_grads",
    )(coef, *streams, stat, means, *scaled, resid_grad, extra, *free)


def coef_kernel(full_width, n_hist, early, late, stat, act, slope, raw, scale, mix_out, mix_in, last, out_part, in_part, turned_ref, extra_ref, pack):
    rows = late.shape[1]
    mixh = act.shape[0]
    inside = lax.broadcasted_iota(jnp.int32, (SLOT, rows), 0) < n_hist
    pack[...] = jnp.zeros_like(pack)
    slots = []
    for s in range(3):
        mean = late[pl.ds(s * SLOT + n_hist, 1), :] * (1.0 / full_width)
        mean_hat = late[pl.ds(s * SLOT + n_hist + 1, 1), :] * (1.0 / full_width)
        pack[pl.ds(MEAN_ROW + s, 1), :] = mean
        pack[pl.ds(MEAN_ROW + 3 + s, 1), :] = mean_hat
        slot = inv_std(stat[pl.ds(3 + s, 1), :], full_width) * (
            late[pl.ds(s * SLOT, SLOT), :]
            - mean * early[pl.ds(0, SLOT), :]
            - mean_hat * early[pl.ds((s + 1) * SLOT, SLOT), :]
        )
        slots.append(jnp.where(inside, slot, 0.0))
    slots.append(jnp.where(inside, late[pl.ds(3 * SLOT, SLOT), :], 0.0))
    d_coef = jnp.concatenate(slots, axis=0)
    ones = jnp.ones((8, rows), F32)
    out_part[pl.ds(0, mixh), :] = dot_tt(act[...], d_coef, ((1,), (1,)), HIGH)
    out_part[pl.ds(SCALE_ROW, 8), :] = dot_tt(ones, d_coef, ((1,), (1,)), HIGH)
    d_pre = dot_tt(mix_out[...], d_coef, ((1,), (0,)), HIGH) * slope[...]
    d_raw = d_pre * scale[...]
    in_part[...] = dot_tt(d_raw, last[...].astype(F32), ((1,), (0,)), HIGH)
    pack[pl.ds(0, mixh), :] = d_raw
    pack[pl.ds(SCALE_ROW, 1), :] = (
        scale[...] * scale[...] * scale[...] * (1.0 / full_width)
        * jnp.sum(d_pre * raw[...], axis=0, keepdims=True)
    )
    turned = pack[...].T
    turned_ref[...] = turned
    back = dot_tt(turned, mix_in[...], ((1,), (1,)), HIGH)
    extra_ref[...] = back - turned[:, SCALE_ROW : SCALE_ROW + 1] * last[...].astype(F32)


def coef_grads(full_width, n_hist, early, late, stat, act, slope, raw, scale, mix_out, mix_in, last, chunk):
    width = last.shape[1]
    rows = late.shape[1]
    mixh = act.shape[0]

    def full(array):
        return pl.BlockSpec(array.shape, lambda i: (0,) * array.ndim)

    def part(array):
        return pl.BlockSpec((array.shape[0], rows), lambda i: (0, chunk))

    arrays = [early, late, stat, act, slope, raw, scale, mix_out, mix_in]
    outs = [
        jax.ShapeDtypeStruct((SCALE_ROW + 8, 4 * SLOT), F32),
        jax.ShapeDtypeStruct((mixh, width), F32),
        jax.ShapeDtypeStruct((rows, LANES), F32),
        jax.ShapeDtypeStruct((rows, width), F32),
    ]
    return pl.pallas_call(
        functools.partial(coef_kernel, full_width, n_hist),
        grid=(1,),
        in_specs=[part(early)]
        + [full(a) for a in arrays[1:3]]
        + [part(a) for a in arrays[3:7]]
        + [full(a) for a in arrays[7:]]
        + [pl.BlockSpec((rows, width), lambda i: (chunk, 0))],
        out_specs=[full(a) for a in outs],
        out_shape=outs,
        scratch_shapes=[pltpu.VMEM((LANES, rows), F32)],
        compiler_params=pltpu.CompilerParams(vmem_limit_bytes=32 * 2**20),
        name="coef_grads",
    )(*arrays, last)


def send_kernel(count, turns, has_came, member_ref, *refs):
    lhs, refs = refs[:count], refs[count:]
    weights, refs = refs[: len(turns)], refs[len(turns) :]
    came, outs = (refs[:2], refs[2:]) if has_came else ((), refs)
    for k in range(len(turns)):
        for s in range(count):
            value = times_transpose(lhs[s][...], weights[k][s])
            if has_came:
                for got in came if len(turns) == 1 else (came[k],):
                    value = value + got[s].astype(F32)
            outs[k][s] = value.astype(outs[k].dtype)


def send_values(member, lhs, weight, turns, came, kind=BF16):
    n = lax.axis_size("stream")
    count = len(lhs)
    rows, depth = lhs[0].shape
    width = weight.shape[1] // n
    tile = 256
    piece = pl.BlockSpec((count, tile, width), lambda i, m: (0, i, 0))

    def block(turn):
        return pl.BlockSpec((count, width, depth), lambda i, m: (0, lax.rem(m[0] + turn, n), 0))

    return pl.pallas_call(
        functools.partial(send_kernel, count, turns, came is not None),
        grid_spec=pltpu.PrefetchScalarGridSpec(
            num_scalar_prefetch=1,
            grid=(rows // tile,),
            in_specs=[pl.BlockSpec((tile, depth), lambda i, m: (i, 0))] * count
            + [block(turn) for turn in turns]
            + ([] if came is None else [piece] * 2),
            out_specs=[piece] * len(turns),
        ),
        out_shape=[jax.ShapeDtypeStruct((count, rows, width), kind)] * len(turns),
        compiler_params=pltpu.CompilerParams(vmem_limit_bytes=48 * 2**20),
        name="send_values",
    )(member, *lhs, *([weight] * len(turns)), *(came or ()))


def columns(rows_values):
    return jnp.concatenate([rows_values, jnp.zeros((TILE - 8, TILE), F32)], axis=0).T


def inv_std(squares, full_width):
    return lax.rsqrt(squares * (1.0 / full_width) + EPS_NORM)


def norm_kernel(full_width, x0, x1, x2, moment_ref, gain_ref, qk_ref, v_ref, stat_ref):
    row = lax.broadcasted_iota(jnp.int32, (8, TILE), 0)
    moments = moment_ref[...]
    stat = columns(jnp.where(row < 3, moments, inv_std(moments, full_width)))
    stat_ref[...] = stat
    for s, x in enumerate((x0, x1, x2)):
        hat = (x[...] - stat[:, s : s + 1]) * stat[:, 3 + s : 4 + s]
        value = (hat * gain_ref[pl.ds(s, 1), :]).astype(BF16)
        if s < 2:
            qk_ref[s] = value
        else:
            v_ref[...] = value


def norm_streams(full_width, streams, moments, gain):
    rows, width = streams[0].shape
    wide = pl.BlockSpec((TILE, width), lambda i: (i, 0))
    return pl.pallas_call(
        functools.partial(norm_kernel, full_width),
        grid=(rows // TILE,),
        in_specs=[
            wide,
            wide,
            wide,
            pl.BlockSpec((8, TILE), lambda i: (0, i)),
            pl.BlockSpec((3, width), lambda i: (0, 0)),
        ],
        out_specs=[
            pl.BlockSpec((2, TILE, width), lambda i: (0, i, 0)),
            wide,
            pl.BlockSpec((TILE, LANES), lambda i: (i, 0)),
        ],
        out_shape=[
            jax.ShapeDtypeStruct((2, rows, width), BF16),
            jax.ShapeDtypeStruct((rows, width), BF16),
            jax.ShapeDtypeStruct((rows, LANES), F32),
        ],
        compiler_params=pltpu.CompilerParams(vmem_limit_bytes=32 * 2**20),
        name="norm_streams",
    )(*streams, moments, gain)


def residual_kernel(member_ref, own, up, down, base, out_ref, low_ref, stat_ref):
    width = own.shape[1]
    value = base[...] + own[...] + up[...].astype(F32) + down[...].astype(F32)
    out_ref[...] = value
    pivot = value[:, :1]
    gap = value - pivot
    shift = row_sum(gap) * (1.0 / width)
    low_ref[...] = (gap - shift).astype(BF16)
    acc = put_lane(jnp.zeros((TILE, LANES), F32), member_ref[0], pivot + shift)
    square = row_sum(jnp.square(gap)) - shift * shift * width
    acc = put_lane(acc, 4 + member_ref[0], square)
    stat_ref[...] = acc.T[:8]


def residual_rows(member, own, up, down, base):
    rows, width = own.shape
    assert lax.axis_size("stream") == 4
    wide = pl.BlockSpec((TILE, width), lambda i, m: (i, 0))
    return pl.pallas_call(
        residual_kernel,
        grid_spec=pltpu.PrefetchScalarGridSpec(
            num_scalar_prefetch=1,
            grid=(rows // TILE,),
            in_specs=[wide] * 4,
            out_specs=[wide, wide, pl.BlockSpec((8, TILE), lambda i, m: (0, i))],
        ),
        out_shape=[
            jax.ShapeDtypeStruct((rows, width), F32),
            jax.ShapeDtypeStruct((rows, width), BF16),
            jax.ShapeDtypeStruct((8, rows), F32),
        ],
        compiler_params=pltpu.CompilerParams(vmem_limit_bytes=32 * 2**20),
        name="residual_rows",
    )(member, own, up, down, base)


def by_member(member_ref, pieces, store):
    n = (len(pieces) + 1) // 2
    low, high = (None, *pieces[1:n]), (None, *pieces[n:])
    for at in range(n):

        @pl.when(member_ref[0] == at)
        def _():
            for slot in range(n):
                if slot == at:
                    store(slot, pieces[0])
                elif slot < at:
                    store(slot, low[at - slot])
                else:
                    store(slot, high[slot - at])


def normed_kernel(full_width, member_ref, *refs):
    pieces, (stat_ref, gain_ref, out_ref, moment_ref) = refs[:-4], refs[-4:]
    n = (len(pieces) + 1) // 2
    width = pieces[0].shape[1]
    stat = stat_ref[...]
    mean = jnp.sum(stat[:n], axis=0, keepdims=True) * (1.0 / n)
    gaps = stat[:n] - mean
    square = jnp.sum(stat[n:], axis=0, keepdims=True) + width * jnp.sum(
        jnp.square(gaps), axis=0, keepdims=True
    )
    moment_ref[...] = jnp.concatenate([mean, square, jnp.zeros((6, TILE), F32)], axis=0)
    table = columns(
        jnp.concatenate([gaps, inv_std(square, full_width), jnp.zeros((3, TILE), F32)], axis=0)
    )

    def store(slot, ref):
        cols = pl.ds(slot * width, width)
        hat = (ref[...].astype(F32) + table[:, slot : slot + 1]) * table[:, n : n + 1]
        out_ref[:, cols] = (hat * gain_ref[:, cols]).astype(BF16)

    by_member(member_ref, pieces, store)


def normed_rows(full_width, member, chain, stat, gain):
    pieces = [chain.piece, *chain.low[1:], *chain.high[1:]]
    rows, width = chain.piece.shape
    wide = pl.BlockSpec((TILE, width), lambda i, m: (i, 0))
    narrow = pl.BlockSpec((8, TILE), lambda i, m: (0, i))
    return pl.pallas_call(
        functools.partial(normed_kernel, full_width),
        grid_spec=pltpu.PrefetchScalarGridSpec(
            num_scalar_prefetch=1,
            grid=(rows // TILE,),
            in_specs=[wide] * len(pieces)
            + [narrow, pl.BlockSpec((1, full_width), lambda i, m: (0, 0))],
            out_specs=[pl.BlockSpec((TILE, full_width), lambda i, m: (i, 0)), narrow],
        ),
        out_shape=[
            jax.ShapeDtypeStruct((rows, full_width), BF16),
            jax.ShapeDtypeStruct((8, rows), F32),
        ],
        compiler_params=pltpu.CompilerParams(vmem_limit_bytes=32 * 2**20),
        name="normed_rows",
    )(member, *pieces, stat, gain)


def branch_kernel(full_width, member_ref, *refs):
    pieces, (stat_ref, sums_ref, normed_ref, gain_ref, out_ref) = refs[:-5], refs[-5:]
    width = pieces[0].shape[1]
    inv = inv_std(columns(stat_ref[...])[:, 1:2], full_width)
    sums = columns(sums_ref[...]) * (1.0 / full_width)
    mean, slope = inv * sums[:, :1], inv * sums[:, 1:2]

    def store(slot, ref):
        cols = pl.ds(slot * width, width)
        hat = normed_ref[:, cols].astype(F32) / gain_ref[:, cols]
        out_ref[:, cols] = (ref[...].astype(F32) - mean - hat * slope).astype(BF16)

    by_member(member_ref, pieces, store)


def branch_rows(full_width, member, chain, stat, sums, normed, gain):
    pieces = [chain.piece, *chain.low[1:], *chain.high[1:]]
    rows, width = chain.piece.shape
    wide = pl.BlockSpec((TILE, width), lambda i, m: (i, 0))
    narrow = pl.BlockSpec((8, TILE), lambda i, m: (0, i))
    whole = pl.BlockSpec((TILE, full_width), lambda i, m: (i, 0))
    return pl.pallas_call(
        functools.partial(branch_kernel, full_width),
        grid_spec=pltpu.PrefetchScalarGridSpec(
            num_scalar_prefetch=1,
            grid=(rows // TILE,),
            in_specs=[wide] * len(pieces)
            + [narrow, narrow, whole, pl.BlockSpec((1, full_width), lambda i, m: (0, 0))],
            out_specs=whole,
        ),
        out_shape=jax.ShapeDtypeStruct((rows, full_width), BF16),
        compiler_params=pltpu.CompilerParams(vmem_limit_bytes=32 * 2**20),
        name="branch_rows",
    )(member, *pieces, stat, sums, normed, gain)


def mlp_back_kernel(full_width, own, up, down, x, stat_ref, gain_ref, cot, out_ref, low_ref, sums_ref, gain_grad_ref):
    @pl.when(pl.program_id(0) == 0)
    def _():
        gain_grad_ref[...] = jnp.zeros_like(gain_grad_ref)

    stat = columns(stat_ref[...])
    grad = own[...] + up[...].astype(F32) + down[...].astype(F32)
    out_ref[...] = grad
    inv = inv_std(stat[:, 1:2], full_width)
    product = grad * ((x[...] - stat[:, :1]) * inv)
    low_ref[...] = (cot[...] + inv * (grad * gain_ref[...])).astype(BF16)
    gain_grad_ref[...] += jnp.sum(product.reshape(TILE // 8, 8, -1), axis=0)
    acc = put_lane(jnp.zeros((TILE, LANES), F32), 0, row_sum(grad * gain_ref[...]))
    acc = put_lane(acc, 1, row_sum(product * gain_ref[...]))
    sums_ref[...] = acc.T[:8]


def mlp_back_rows(full_width, own, up, down, residual, stat, gain, cot):
    rows, width = residual.shape
    wide = pl.BlockSpec((TILE, width), lambda i: (i, 0))
    narrow = pl.BlockSpec((8, TILE), lambda i: (0, i))
    return pl.pallas_call(
        functools.partial(mlp_back_kernel, full_width),
        grid=(rows // TILE,),
        in_specs=[wide] * 4 + [narrow, pl.BlockSpec((1, width), lambda i: (0, 0)), wide],
        out_specs=[wide, wide, narrow, pl.BlockSpec((8, width), lambda i: (0, 0))],
        out_shape=[
            jax.ShapeDtypeStruct((rows, width), F32),
            jax.ShapeDtypeStruct((rows, width), BF16),
            jax.ShapeDtypeStruct((8, rows), F32),
            jax.ShapeDtypeStruct((8, width), F32),
        ],
        compiler_params=pltpu.CompilerParams(vmem_limit_bytes=32 * 2**20),
        name="mlp_back_rows",
    )(own, up, down, residual, stat, gain, cot)


def resid_grad_kernel(full_width, grad, x, stat_ref, sums_ref, gain_ref, cot, out_ref):
    stat = columns(stat_ref[...])
    sums = columns(sums_ref[...]) * (1.0 / full_width)
    inv = inv_std(stat[:, 1:2], full_width)
    hat = (x[...] - stat[:, :1]) * inv
    value = cot[...] + inv * (grad[...] * gain_ref[...] - sums[:, :1] - hat * sums[:, 1:2])
    out_ref[...] = value


def resid_grad_rows(full_width, grad, residual, stat, sums, gain, cot):
    rows, width = residual.shape
    wide = pl.BlockSpec((TILE, width), lambda i: (i, 0))
    narrow = pl.BlockSpec((8, TILE), lambda i: (0, i))
    return pl.pallas_call(
        functools.partial(resid_grad_kernel, full_width),
        grid=(rows // TILE,),
        in_specs=[wide, wide, narrow, narrow, pl.BlockSpec((1, width), lambda i: (0, 0)), wide],
        out_specs=wide,
        out_shape=jax.ShapeDtypeStruct((rows, width), F32),
        compiler_params=pltpu.CompilerParams(vmem_limit_bytes=32 * 2**20),
        name="resid_grad_rows",
    )(grad, residual, stat, sums, gain, cot)


def rows_product_kernel(n, *refs):
    former, latter, out_ref = refs[:n], refs[n : 2 * n], refs[-1]
    total = 0.0
    for c in range(n):
        total = total + contract_rows(former[c][...], latter[c][...])
    out_ref[...] = total.astype(BF16)


def rows_product(former, latter, out_cols, first, held, others=(), slot=None, half=None):
    n = len(former)
    rows, height = former[0].shape[-2:]
    width = latter[0].shape[1]
    skip = 0
    if half is not None:
        width //= 2
        out_cols //= 2
    tile_m, tile_n = min(512 if width > 512 else 1024, height), min(2048, width)
    begin = first // tile_n
    if half:
        skip = width // tile_n
    free = [*others] + ([] if held is None else [held])
    return pl.pallas_call(
        functools.partial(rows_product_kernel, n),
        grid=(height // tile_m, width // tile_n),
        in_specs=[
            pl.BlockSpec((rows, tile_m), lambda i, j: (0, i))
            if slot is None
            else pl.BlockSpec((None, rows, tile_m), lambda i, j: (slot, 0, i))
        ]
        * n
        + [pl.BlockSpec((rows, tile_n), lambda i, j: (0, skip + j))] * n
        + [pl.BlockSpec(memory_space=pl.ANY)] * len(free),
        out_specs=pl.BlockSpec((tile_m, tile_n), lambda i, j: (i, begin + j)),
        out_shape=jax.ShapeDtypeStruct((height, out_cols), BF16),
        input_output_aliases={} if held is None else {2 * n + len(others): 0},
        compiler_params=pltpu.CompilerParams(vmem_limit_bytes=48 * 2**20),
        name="rows_product",
    )(*former, *latter, *free)


def local(
    history,
    mix_in,
    mix_out,
    mix_static,
    stream_gain,
    qkv_weight,
    out_weight,
    mlp_gain,
    up_weight,
    down_weight,
    out_grad,
    seq_group,
    group_weight,
):
    n_stream = lax.axis_size("stream")
    member = lax.axis_index("stream")
    n_hist, tokens, width = history.shape
    assert tokens == SEQ
    full_width = width * n_stream
    rows = tokens // CHUNKS
    both = range(CHUNKS)
    spans = [slice(c * rows, (c + 1) * rows) for c in both]
    first_col = member * width
    mixh = mix_in.shape[1]
    ff = up_weight.shape[1]
    order = Order()

    def rows_of(weight, idx):
        begin = lax.rem(member + idx, n_stream) * width
        return lax.dynamic_slice_in_dim(weight, begin, width, 0)

    def dp_sum(part):
        return lax.psum_scatter(part, "dp", scatter_dimension=0, tiled=True).astype(F32)

    mix_in_rows = lax.dynamic_slice_in_dim(mix_in, first_col, width, 0)
    mix_out_float = mix_out.astype(F32)

    last = history[n_hist - 1]
    square_part = jnp.sum(jnp.square(last.astype(F32)), axis=1)[None]
    raw_part = dot_tt(mix_in_rows, last, ((0,), (1,)))
    raw = Butterfly(jnp.concatenate([raw_part, square_part], axis=0))
    order.send(raw)

    here = member.astype(jnp.int32).reshape(1)
    qkv_rows = jnp.transpose(order.hold(qkv_weight), (1, 0, 2))
    order.did(qkv_rows)

    group_pick = (
        seq_group[:, None] == jnp.arange(group_weight.shape[0], dtype=jnp.int32)[None, :]
    ).astype(F32)
    seq_weight = jnp.sum(group_pick * group_weight.astype(F32)[None, :]) * COT_SCALE
    out_grad_held = order.hold(out_grad)
    cot_cols = [out_grad_held[spans[c]].astype(F32) * seq_weight for c in both]
    cot = [LineGather(cot_cols[c].astype(BF16), member) for c in both]
    order.did(cot[0].piece, cot[1].piece)
    order.send(raw)
    order.send(cot[0])

    sums = raw.value()
    raw_t = sums[:-1]
    scale_t = lax.rsqrt(sums[-1:] / full_width + EPS_MIX)
    act_t, slope_t = gelu_both(scale_t * raw_t)
    coef = (dot_tt(mix_out_float, act_t, ((0,), (0,)), HIGH) + mix_static.reshape(-1, 1)).T

    streams, moments = [None] * 2, [None] * 2
    stat, stat_rows, normed_chain = [None] * 2, [None] * 2, [None] * 2
    resid_streams, early_chain = [None] * 2, []

    def mix(c):
        *streams[c], sums = mix_streams(history, coef, c, (0, 1, 2), True)
        moments[c] = Butterfly(sums, merge=moments_merger(width, 3))

    def norm(c):
        stat_rows[c] = moments[c].value()
        pair, single, stat[c] = norm_streams(full_width, streams[c], stat_rows[c], stream_gain)
        normed_chain[c] = [LineGather(pair, member), LineGather(single, member)]

    def early(c):
        sums = early_dots(history, [order.hold(streams[c][0]), *streams[c][1:]], stat[c], c)
        order.did(sums)
        early_chain.append(Butterfly(sums))

    def mix_resid(c):
        (resid_streams[c],) = mix_streams(history, order.hold(coef), c, (3,), False)
        order.did(resid_streams[c])

    mix(0)
    mix(1)
    order.send(*moments)
    order.send(*moments)
    norm(0)
    order.send(normed_chain[0][0])
    order.send(normed_chain[0][1])
    norm(1)
    order.did(normed_chain[1][0].piece)
    mix_resid(0)
    order.send(normed_chain[0][0])
    order.send(normed_chain[0][1])
    early(0)
    order.send(normed_chain[0][0])
    order.send(normed_chain[0][1])
    mix_resid(1)
    order.send(normed_chain[1][0])
    order.send(normed_chain[1][1])

    normed, query, key, value, heads_out, lse = [], [], [], [], [], []
    branch = []

    def project(c):
        normed.append([chain.value() for chain in normed_chain[c]])
        for held, s, full in ((query, 0, normed[c][0][0]), (key, 1, normed[c][0][1]), (value, 2, normed[c][1])):
            held.append(jnp.dot(full, qkv_rows[s], preferred_element_type=F32).astype(BF16))

    def attend(c):
        out, out_lse = attend_forward(query[c], key[: c + 1], value[: c + 1])
        heads_out.append(out)
        lse.append(out_lse)
        branch.append(
            LineScatter(
                order, lambda idx, hold: times_transpose(hold(out), rows_of(out_weight, idx))
            )
        )

    residual, resid_moments = [], []
    mlp_gain_cols = lax.dynamic_slice_in_dim(mlp_gain, first_col, width, 0)[None, :]
    mlp_in, mlp_moments = [], []
    normed_mlp, hidden, d_hpre, mlp_back, mlp_out = [], [], [], [], []

    def end_branch(c):
        value, low, stats = residual_rows(here, *branch[c].pieces(), resid_streams[c])
        residual.append(value)
        resid_moments.append(Butterfly(stats))
        mlp_in.append(LineGather(low, member))

    cot_low, d_hidden = [], []

    def down_back(c):
        cot_low.append(cot[c].value())
        d_hidden.append(
            jnp.dot(order.hold(cot_low[c]), down_weight, preferred_element_type=F32)
        )
        order.did(d_hidden[c])

    def mlp(c):
        full, moments_all = normed_rows(
            full_width, here, mlp_in[c], resid_moments[c].value(), mlp_gain[None, :]
        )
        normed_mlp.append(full)
        mlp_moments.append(moments_all)
        hidden_pre = jnp.dot(normed_mlp[c], up_weight, preferred_element_type=F32)
        act, slope = gelu_both(hidden_pre)
        act = act.astype(BF16)
        d_pre = (d_hidden[c] * slope).astype(BF16)
        hidden.append(act)
        d_hpre.append(d_pre)
        mlp_back.append(
            LineScatter(
                order, lambda idx, hold: times_transpose(hold(d_pre), rows_of(up_weight, idx))
            )
        )
        mlp_out.append(
            LineScatter(
                order, lambda idx, hold: times_transpose(hold(act), rows_of(down_weight, idx))
            )
        )

    def weight_part(former, latter, out_cols, others):
        return rows_product(former, latter, out_cols, 0, None, others)

    d_normed_mlp, back_sums, mlp_gain_shares = [], [], []

    resid_grad, branch_grad = [], []

    def end_mlp_back(c):
        value, low, sums, share = mlp_back_rows(
            full_width, *mlp_back[c].pieces(), residual[c], mlp_moments[c], mlp_gain_cols,
            cot_cols[c],
        )
        d_normed_mlp.append(value)
        back_sums.append(Butterfly(sums))
        mlp_gain_shares.append(share)
        branch_grad.append(LineGather(low, member))

    d_branch, d_proj = [], []
    carried = [None]

    def attend_back(c):
        sums = back_sums[c].value()
        d_branch.append(
            branch_rows(
                full_width, here, branch_grad[c], mlp_moments[c], sums, normed_mlp[c],
                mlp_gain[None, :],
            )
        )
        resid_grad.append(
            resid_grad_rows(
                full_width, d_normed_mlp[c], residual[c], mlp_moments[c], sums, mlp_gain_cols,
                cot_cols[c],
            )
        )
        d_heads = jnp.dot(d_branch[c], out_weight, preferred_element_type=F32).astype(BF16)
        d_query, dk, dv = attend_backward(
            query[c], d_heads, lse[c], key[: c + 1], value[: c + 1], carried[0], c == CHUNKS - 1
        )
        carried[0] = (dk, dv)
        d_proj.append([d_query, None, None])
        if c == CHUNKS - 1:
            for i in both:
                d_proj[i][1:] = [dk[i], dv[i]]

    project(0)
    attend(0)
    order.send(branch[0])
    branch[0].prepare()
    order.send(normed_chain[1][0])
    order.send(branch[0])
    branch[0].prepare()
    order.send(normed_chain[1][1])
    early(1)
    order.send(branch[0])
    branch[0].prepare()
    order.send(normed_chain[1][0])
    order.send(normed_chain[1][1])
    end_branch(0)
    order.send(resid_moments[0], cot[0])
    project(1)
    order.send(resid_moments[0])
    order.send(cot[0])
    attend(1)
    order.send(branch[1], mlp_in[0])
    branch[1].prepare()
    down_back(0)
    order.send(branch[1], mlp_in[0])
    branch[1].prepare()
    order.send(branch[1], mlp_in[0])
    branch[1].prepare()
    order.send(cot[1])
    end_branch(1)
    order.send(mlp_in[1], resid_moments[1])
    mlp(0)
    order.send(cot[1])
    order.send(mlp_in[1], mlp_back[0], resid_moments[1])
    mlp_back[0].prepare()
    order.send(cot[1])
    order.send(mlp_in[1], mlp_back[0])
    mlp_back[0].prepare()
    down_back(1)
    order.send(mlp_back[0])
    mlp_back[0].prepare()
    mlp(1)
    end_mlp_back(0)
    order.send(mlp_back[1], branch_grad[0])
    mlp_back[1].prepare()
    down_part = weight_part(cot_low, hidden, ff, mlp_back[1].came)
    order.send(mlp_back[1], branch_grad[0], back_sums[0])
    up_came, down_came = mlp_back[1].came
    up_came, down_part = lax.optimization_barrier((up_came, down_part))
    mlp_back[1].came = [up_came, down_came]
    down_sum = lax.psum_scatter(down_part, "dp", scatter_dimension=0, tiled=True)
    mlp_back[1].prepare()
    order.send(mlp_back[1], branch_grad[0], back_sums[0])
    mlp_back[1].prepare()
    end_mlp_back(1)
    mlp_out[0].prepare()
    order.send(branch_grad[1], mlp_out[0])
    mlp_out[0].prepare()
    attend_back(0)
    order.send(branch_grad[1], mlp_out[0], back_sums[1])
    chain = branch_grad[1]
    chain.low[-1], chain.high[-1], d_proj[0][0] = lax.optimization_barrier(
        (chain.low[-1], chain.high[-1], d_proj[0][0])
    )
    mlp_out[0].prepare()
    order.send(branch_grad[1], mlp_out[0], back_sums[1])
    mlp_out[0].prepare()
    mlp_out[1].prepare()
    attend_back(1)
    order.send(mlp_out[1])
    mlp_out[1].prepare()

    grads = [ProductScatter(order, here, d_proj[c], qkv_rows) for c in both]
    own = [None] * 2
    early_one = Butterfly(jnp.concatenate([chain.now for chain in early_chain], axis=1))
    order.send(*grads, early_one)
    out_part = weight_part(d_branch, heads_out, width, (*grads[0].came, down_sum))
    order.send(*grads, early_one)
    up_part = weight_part(normed_mlp, d_hpre, ff, grads[0].came)
    qkv_part = None
    for s in range(3):
        qkv_part = rows_product(
            [normed[c][s // 2] for c in both], [d_proj[c][s] for c in both], 3 * width, s * width,
            qkv_part, grads[1].came, s if s < 2 else None,
        )
    order.send(*grads)
    down_grad = down_sum.astype(F32)
    own = [grads[c].own() for c in both]
    up_grad, out_weight_grad = [dp_sum(part) for part in (up_part, out_part)]
    qkv_sum = lax.psum_scatter(qkv_part, "dp", scatter_dimension=0, tiled=True)
    qkv_grad = jnp.stack(
        [qkv_sum[:, s * width : (s + 1) * width] for s in range(3)], axis=1
    ).astype(F32)
    gain_part = jnp.sum(mlp_gain_shares[0] + mlp_gain_shares[1], axis=0)
    gain_chain = Butterfly(
        jnp.where(
            jnp.arange(n_stream)[:, None] == member,
            gain_part[None, :],
            jnp.zeros((n_stream, width), F32),
        )
    )

    mix_out_wide = jnp.pad(
        mix_out_float.reshape(-1, 4, n_hist), ((0, 0), (0, 0), (0, SLOT - n_hist))
    ).reshape(-1, 4 * SLOT)
    mix_in_wide = jnp.pad(mix_in_rows.astype(F32), ((0, 0), (0, LANES - mixh)))
    d_normed, late, gain_shares, shares = [], [], [], []
    history_grad = [None]

    def late_sums(c):
        *scaled, sums, gain_share = late_dots(
            history, streams[c], stat[c], stream_gain, resid_grad[c], own[c], grads[c].came, c
        )
        d_normed.append(scaled)
        late.append(Butterfly(sums))
        gain_shares.append(gain_share)

    def coefs(c):
        shares.append(
            coef_grads(
                full_width, n_hist, early_one.value(), late[c].value(), stat_rows[c], act_t,
                slope_t, raw_t, scale_t, mix_out_wide, mix_in_wide, last, c,
            )
        )

    def layers(c, others):
        _, _, turned, extra = shares[c]
        history_grad[0] = layer_grads(
            coef, streams[c], stat[c], turned, d_normed[c], resid_grad[c], extra, c,
            history_grad[0], tokens, others,
        )
        order.did(history_grad[0])

    late_sums(0)
    order.did(qkv_part)
    order.send(late[0], gain_chain)
    order.send(mlp_out[1])
    mlp_out[1].prepare()
    late_sums(1)
    order.send(late[0], late[1], gain_chain)
    coefs(0)
    order.send(late[1])
    coefs(1)
    out_share, in_share = [shares[0][i] + shares[1][i] for i in range(2)]
    gain_share = jnp.sum(gain_shares[0] + gain_shares[1], axis=1)
    out_share = jnp.pad(out_share, ((0, 0), (0, width - 4 * SLOT)))
    small = Butterfly(
        jnp.concatenate([out_share, in_share, gain_share, gain_chain.value()], axis=0), ("dp",)
    )
    order.send(small)
    order.send(mlp_out[1])
    layers(0, (small.now,))
    layers(1, ())
    while small.turns:
        order.send(small)
    output_cols = jnp.concatenate(
        [(residual[c] + mlp_out[c].value()).astype(BF16) for c in both], axis=0
    )
    small = small.value()
    top = out_share.shape[0]
    by_slot = small[:top, : 4 * SLOT].reshape(-1, 4, SLOT)[:, :, :n_hist]
    return (
        output_cols,
        history_grad[0],
        small[top : top + mixh].T,
        by_slot[:mixh].reshape(mixh, 4 * n_hist),
        by_slot[SCALE_ROW],
        small[top + mixh : top + mixh + 3],
        qkv_grad,
        out_weight_grad,
        small[top + mixh + 3 :].reshape(full_width),
        up_grad,
        down_grad,
    )


def solution(mesh):
    in_specs = (
        P(None, "dp", "stream"),
        P(),
        P(),
        P(),
        P(None, "stream"),
        P(None, None, "stream"),
        P(None, "stream"),
        P(),
        P(None, "stream"),
        P(None, "stream"),
        P("dp", "stream"),
        P("dp"),
        P(),
    )
    out_specs = (
        P("dp", "stream"),
        P(None, "dp", "stream"),
        P("stream", None),
        P(),
        P(),
        P(None, "stream"),
        P("dp", None, "stream"),
        P("dp", "stream"),
        P(),
        P("dp", "stream"),
        P("dp", "stream"),
    )
    return jax.shard_map(local, mesh=mesh, in_specs=in_specs, out_specs=out_specs, check_vma=False)
```

```python
import functools
import math

import jax
import jax.numpy as jnp
from jax import lax
from jax.experimental import pallas as pl
from jax.experimental.pallas import tpu as pltpu
from jax.sharding import PartitionSpec as P

HEAD_DIM = 128
SEQ = 1024
CHUNKS = 2
SUB = 512

HIGH = lax.Precision.HIGHEST
EPS_NORM = 1e-05
EPS_MIX = 1e-06
COT_SCALE = 0.4
F32 = jnp.float32
BF16 = jnp.bfloat16


def gelu_both(values):
    cdf = 0.5 * (1.0 + lax.erf(values * math.sqrt(0.5)))
    density = jnp.exp(-0.5 * jnp.square(values)) * (1.0 / math.sqrt(2.0 * math.pi))
    return values * cdf, cdf + values * density


def dot_tt(former, latter, dims, precision=None):
    return lax.dot_general(
        former, latter, (dims, ((), ())), precision=precision, preferred_element_type=F32
    )


def contract_rows(former, latter):
    return dot_tt(former, latter, ((0,), (0,)))


def times_transpose(former, latter):
    return dot_tt(former, latter, ((1,), (1,)))


def after(value, *others):
    return lax.optimization_barrier((value, *others))[0]


class Order:
    def __init__(self):
        self.tick = ()

    def hold(self, value):
        return after(value, *self.tick) if self.tick else value

    def did(self, *outs):
        self.tick = (*self.tick, *outs)

    def send(self, *chains):
        items = [chain.items() for chain in chains]
        flat = [value for chain_items in items for value, _, _ in chain_items]
        held = lax.optimization_barrier((*flat, *self.tick))[: len(flat)]
        self.tick = tuple(held)
        at = 0
        for chain, chain_items in zip(chains, items):
            got = []
            for _, axis, perm in chain_items:
                got.append(lax.ppermute(held[at], axis, perm))
                at += 1
            chain.take(got)


class LineGather:
    def __init__(self, piece, member):
        self.piece, self.member = piece, member
        self.low, self.high = [piece], [piece]

    def items(self):
        n, step = lax.axis_size("stream"), len(self.low)
        return [
            (self.low[-1], "stream", [(i, i + 1) for i in range(step - 1, n - 1)]),
            (self.high[-1], "stream", [(i, i - 1) for i in range(1, n - step + 1)]),
        ]

    def take(self, got):
        self.low.append(got[0])
        self.high.append(got[1])

    def value(self):
        n, member = lax.axis_size("stream"), self.member
        slots = []
        for slot in range(n):
            value = self.piece
            for at in range(n):
                if at > slot:
                    value = jnp.where(member == at, self.low[at - slot], value)
                elif at < slot:
                    value = jnp.where(member == at, self.high[slot - at], value)
            slots.append(value)
        return jnp.concatenate(slots, axis=-1)


class LineScatter:
    def __init__(self, order, block):
        self.order, self.block = order, block
        self.parts, self.came, self.step = {}, None, 0

    def part(self, idx):
        if idx not in self.parts:
            self.parts[idx] = self.block(idx, lambda value: value)
        return self.parts[idx]

    def items(self):
        n, step = lax.axis_size("stream"), self.step
        up_idx, down_idx = n - 1 - step, 1 + step
        up_value, down_value = self.part(up_idx), self.part(down_idx)
        if self.came is not None:
            up, down = [got.astype(F32) for got in self.came]
            if up_idx == down_idx:
                up_value = down_value = up_value + up + down
            else:
                up_value, down_value = up_value + up, down_value + down
        return [
            (up_value.astype(BF16), "stream", [(i, i + 1) for i in range(step + 1)]),
            (down_value.astype(BF16), "stream", [(i, i - 1) for i in range(n - 1 - step, n)]),
        ]

    def take(self, got):
        self.came = got
        self.step += 1

    def prepare(self):
        n, step = lax.axis_size("stream"), self.step
        for idx in {n - 1 - step, (1 + step) % n}:
            if idx not in self.parts:
                self.parts[idx] = self.block(idx, self.order.hold)
                self.order.did(self.parts[idx])

    def pieces(self):
        return self.part(0), *self.came

    def value(self):
        own, up, down = self.pieces()
        return own + up.astype(F32) + down.astype(F32)


class ProductScatter(LineScatter):
    def __init__(self, order, member, lhs, weight):
        super().__init__(order, None)
        self.args = (member, lhs, weight)

    def items(self):
        n, step = lax.axis_size("stream"), self.step
        up_turn, down_turn = n - 1 - step, 1 + step
        turns = (up_turn,) if up_turn == down_turn else (up_turn, down_turn)
        values = send_values(*self.args, turns, self.came)
        return [
            (values[0], "stream", [(i, i + 1) for i in range(step + 1)]),
            (values[-1], "stream", [(i, i - 1) for i in range(n - 1 - step, n)]),
        ]

    def own(self):
        member, lhs, weight = self.args
        (value,) = send_values(member, [self.order.hold(lhs[0]), *lhs[1:]], weight, (0,), None, F32)
        self.order.did(value)
        return value


class Butterfly:
    def __init__(self, value, axes=("stream",), merge=jnp.add):
        self.now, self.merge = value, merge
        self.turns = [(axis, 1 << i) for axis in axes for i in range(lax.axis_size(axis).bit_length() - 1)]
        assert all(lax.axis_size(axis) & (lax.axis_size(axis) - 1) == 0 for axis in axes)

    def items(self):
        axis, span = self.turns[0]
        return [(self.now, axis, [(i, i ^ span) for i in range(lax.axis_size(axis))])]

    def take(self, got):
        self.turns = self.turns[1:]
        self.now = self.merge(self.now, got[0])

    def value(self):
        assert not self.turns
        return self.now


def moments_merger(width, half):
    count = [width]

    def merge(mine, other):
        row = lax.broadcasted_iota(jnp.int32, mine.shape, 0)
        total = mine + other
        gap = jnp.roll(mine - other, half, axis=0)
        square = total + jnp.square(gap) * (0.5 * count[0])
        count[0] *= 2
        return jnp.where(row < half, 0.5 * total, square)

    return merge


def attend_forward_kernel(chunk, q_ref, *refs):
    k_refs, v_refs = refs[: chunk + 1], refs[chunk + 1 : 2 * chunk + 2]
    o_ref, lse_ref = refs[2 * chunk + 2 :]
    rows = q_ref.shape[0]
    keys = jnp.concatenate([ref[...] for ref in k_refs], axis=0)
    values = jnp.concatenate([ref[...] for ref in v_refs], axis=0)
    for sub in range(rows // SUB):
        count = chunk * rows + (sub + 1) * SUB
        span = pl.ds(sub * SUB, SUB)
        scores = times_transpose(keys[:count], q_ref[span, :]) * HEAD_DIM ** (-0.5)
        allowed = lax.broadcasted_iota(jnp.int32, (SUB, SUB), 0) <= lax.broadcasted_iota(
            jnp.int32, (SUB, SUB), 1
        )
        tail = jnp.where(allowed, scores[count - SUB :], -1e30)
        scores = jnp.concatenate([scores[: count - SUB], tail], axis=0) if count > SUB else tail
        top = jnp.max(scores, axis=0, keepdims=True)
        weights = jnp.exp(scores - top)
        total = jnp.sum(weights, axis=0, keepdims=True)
        probs = (weights * (1.0 / total)).astype(BF16)
        lse_ref[0, :, span] = top + jnp.log(total)
        out = contract_rows(values[:count], probs)
        o_ref[span, :] = out.T.astype(BF16)


def attend_forward(queries, keys, values):
    rows, width = queries.shape
    heads = width // HEAD_DIM
    chunk = len(keys) - 1
    spec = pl.BlockSpec((rows, HEAD_DIM), lambda h: (0, h))
    return pl.pallas_call(
        functools.partial(attend_forward_kernel, chunk),
        grid=(heads,),
        in_specs=[spec] * (2 * chunk + 3),
        out_specs=[spec, pl.BlockSpec((1, 1, rows), lambda h: (h, 0, 0))],
        out_shape=[
            jax.ShapeDtypeStruct((rows, width), BF16),
            jax.ShapeDtypeStruct((heads, 1, rows), F32),
        ],
        compiler_params=pltpu.CompilerParams(vmem_limit_bytes=48 * 2**20),
        name="attend_forward",
    )(queries, *keys, *values)


def attend_backward_kernel(chunk, q_ref, do_ref, lse_ref, *refs):
    n = chunk + 1
    k_refs, v_refs, refs = refs[:n], refs[n : 2 * n], refs[2 * n :]
    dk_in, dv_in, refs = refs[:chunk], refs[chunk : 2 * chunk], refs[2 * chunk :]
    dq_ref, dk_refs, dv_refs, (dk_acc, dv_acc) = refs[0], refs[1 : 1 + n], refs[1 + n : 1 + 2 * n], refs[1 + 2 * n :]
    rows = q_ref.shape[0]
    keys = jnp.concatenate([ref[...] for ref in k_refs], axis=0)
    values = jnp.concatenate([ref[...] for ref in v_refs], axis=0)
    for i in range(n):
        here = pl.ds(i * rows, rows)
        dk_acc[here, :] = dk_in[i][...] if i < chunk else jnp.zeros((rows, HEAD_DIM), F32)
        dv_acc[here, :] = dv_in[i][...] if i < chunk else jnp.zeros((rows, HEAD_DIM), F32)
    scale = HEAD_DIM ** (-0.5)
    for sub in range(rows // SUB):
        count = chunk * rows + (sub + 1) * SUB
        span = pl.ds(sub * SUB, SUB)
        query, grad = q_ref[span, :], do_ref[span, :]
        scores = times_transpose(keys[:count], query) * scale
        probs = jnp.exp(scores - lse_ref[0, :, span])
        allowed = lax.broadcasted_iota(jnp.int32, (SUB, SUB), 0) <= lax.broadcasted_iota(
            jnp.int32, (SUB, SUB), 1
        )
        tail = jnp.where(allowed, probs[count - SUB :], 0.0)
        probs = jnp.concatenate([probs[: count - SUB], tail], axis=0) if count > SUB else tail
        prob_grad = times_transpose(values[:count], grad)
        row_dot = jnp.sum(probs * prob_grad, axis=0, keepdims=True)
        score_grad = (probs * (prob_grad - row_dot)).astype(BF16)
        dq_ref[span, :] = (contract_rows(keys[:count], score_grad) * scale).T.astype(BF16)
        dk_acc[pl.ds(0, count), :] += jnp.dot(score_grad, query, preferred_element_type=F32) * scale
        dv_acc[pl.ds(0, count), :] += jnp.dot(
            probs.astype(BF16), grad, preferred_element_type=F32
        )
    for i in range(n):
        dk_refs[i][...] = dk_acc[pl.ds(i * rows, rows), :].astype(dk_refs[i].dtype)
        dv_refs[i][...] = dv_acc[pl.ds(i * rows, rows), :].astype(dv_refs[i].dtype)


def attend_backward(queries, grad, lse, keys, values, sums, final):
    rows, width = queries.shape
    heads = width // HEAD_DIM
    chunk = len(keys) - 1
    n = chunk + 1
    spec = pl.BlockSpec((rows, HEAD_DIM), lambda h: (0, h))
    dk_dv = [jax.ShapeDtypeStruct((rows, width), BF16 if final else F32)] * (2 * n)
    carried = [] if sums is None else [*sums[0], *sums[1]]
    outs = pl.pallas_call(
        functools.partial(attend_backward_kernel, chunk),
        grid=(heads,),
        in_specs=[spec, spec, pl.BlockSpec((1, 1, rows), lambda h: (h, 0, 0))]
        + [spec] * (2 * n + len(carried)),
        out_specs=[spec] * (1 + 2 * n),
        out_shape=[jax.ShapeDtypeStruct((rows, width), BF16), *dk_dv],
        scratch_shapes=[pltpu.VMEM((n * rows, HEAD_DIM), F32)] * 2,
        compiler_params=pltpu.CompilerParams(vmem_limit_bytes=48 * 2**20),
        name="attend_backward",
    )(queries, grad, lse, *keys, *values, *carried)
    return outs[0], outs[1 : 1 + n], outs[1 + n :]


GROUP = 128
VMEM_MOST = 60 * 2**20
TILE = 128
SLOT = 16
SCALE_ROW = 48
MEAN_ROW = 56
LANES = 128


def put_lane(acc, idx, column):
    lane = lax.broadcasted_iota(jnp.int32, acc.shape, 1)
    return jnp.where(lane == idx, column, acc)


def row_sum(values):
    return jnp.sum(values, axis=1, keepdims=True)


def spread(values, idx):
    return jnp.broadcast_to(values[:, idx : idx + 1], (values.shape[0], LANES))


def by_groups(tile, body):
    def step(i, carry):
        body(pl.ds(pl.multiple_of(i * GROUP, GROUP), GROUP))
        return carry

    lax.fori_loop(0, tile // GROUP, step, 0)


def mix_kernel(picked, hist_ref, coef_ref, *refs):
    out_refs, stat_ref, stat_acc = refs[: len(picked)], *(refs[len(picked) :] or (None, None))
    n_hist, tile, width = hist_ref.shape

    def group(span):
        coef = coef_ref[span, :]
        cols = {(s, j): spread(coef, s * n_hist + j) for s in picked for j in range(n_hist)}
        pivots, sums, squares = [], [], []
        for w in range(width // LANES):
            lanes = pl.ds(w * LANES, LANES)
            totals = [0.0] * len(picked)
            for j in range(n_hist):
                layer = hist_ref[j, span, lanes].astype(F32)
                for i, s in enumerate(picked):
                    totals[i] = totals[i] + cols[s, j] * layer
            for i, total in enumerate(totals):
                out_refs[i][span, lanes] = total
                if stat_ref is None:
                    continue
                if w == 0:
                    pivots.append(spread(total, 0))
                    sums.append(0.0)
                    squares.append(0.0)
                gap = total - pivots[i]
                sums[i] = sums[i] + gap
                squares[i] = squares[i] + jnp.square(gap)
        if stat_ref is not None:
            stats = jnp.zeros((GROUP, LANES), F32)
            for i in range(len(picked)):
                shift = row_sum(sums[i]) * (1.0 / width)
                stats = put_lane(stats, i, pivots[i] + shift)
                stats = put_lane(stats, len(picked) + i, row_sum(squares[i]) - shift * shift * width)
            stat_acc[span, :] = stats

    by_groups(tile, group)
    if stat_ref is not None:
        stat_ref[...] = stat_acc[...].T[: stat_ref.shape[0]]


def mix_streams(history, coef, chunk, picked, with_stats):
    n_hist, tokens, width = history.shape
    rows = tokens // CHUNKS
    base = chunk * rows // TILE
    wide = pl.BlockSpec((TILE, width), lambda i: (i, 0))
    n = len(picked)
    return pl.pallas_call(
        functools.partial(mix_kernel, picked),
        grid=(rows // TILE,),
        in_specs=[
            pl.BlockSpec((n_hist, TILE, width), lambda i: (0, base + i, 0)),
            pl.BlockSpec((TILE, 4 * n_hist), lambda i: (base + i, 0)),
        ],
        out_specs=[wide] * n + ([pl.BlockSpec((8, TILE), lambda i: (0, i))] if with_stats else []),
        out_shape=[jax.ShapeDtypeStruct((rows, width), F32)] * n
        + ([jax.ShapeDtypeStruct((8, rows), F32)] if with_stats else []),
        scratch_shapes=[pltpu.VMEM((TILE, LANES), F32)] if with_stats else [],
        compiler_params=pltpu.CompilerParams(vmem_limit_bytes=VMEM_MOST),
        name="mix_streams",
    )(history, coef)


def hat_of(stream, stat, s):
    return (stream - spread(stat, s)) * spread(stat, 3 + s)


def early_kernel(hist_ref, x0, x1, x2, stat_ref, sums_ref, acc_ref):
    n_hist, tile, width = hist_ref.shape

    def group(span):
        stat = stat_ref[span, :]
        sums = jnp.zeros((GROUP, LANES), F32)
        pieces = [pl.ds(w * LANES, LANES) for w in range(width // LANES)]
        others = [[hat_of(x[span, p], stat, s) for p in pieces] for s, x in enumerate((x0, x1, x2))]
        for j in range(n_hist):
            layer = [hist_ref[j, span, p].astype(F32) for p in pieces]
            sums = put_lane(sums, j, row_sum(sum(layer[1:], layer[0])))
            for s in range(3):
                terms = [x * y for x, y in zip(others[s], layer)]
                sums = put_lane(sums, (s + 1) * SLOT + j, row_sum(sum(terms[1:], terms[0])))
        acc_ref[span, :] = sums

    by_groups(tile, group)
    sums_ref[...] = acc_ref[...].T[: sums_ref.shape[0]]


def early_dots(history, streams, stat, chunk):
    n_hist, tokens, width = history.shape
    rows = stat.shape[0]
    base = chunk * rows // TILE
    wide = pl.BlockSpec((TILE, width), lambda i: (i, 0))
    return pl.pallas_call(
        early_kernel,
        grid=(rows // TILE,),
        in_specs=[
            pl.BlockSpec((n_hist, TILE, width), lambda i: (0, base + i, 0)),
            wide,
            wide,
            wide,
            pl.BlockSpec((TILE, LANES), lambda i: (i, 0)),
        ],
        out_specs=pl.BlockSpec((4 * SLOT, TILE), lambda i: (0, i)),
        out_shape=jax.ShapeDtypeStruct((4 * SLOT, rows), F32),
        scratch_shapes=[pltpu.VMEM((TILE, LANES), F32)],
        compiler_params=pltpu.CompilerParams(vmem_limit_bytes=VMEM_MOST),
        name="early_dots",
    )(history, *streams, stat)


def late_kernel(hist_ref, x0, x1, x2, stat_ref, gain_ref, resid_ref, own, up, down, g0, g1, g2, sums_ref, gain_grad_ref, acc_ref):
    grad_refs = (g0, g1, g2)
    n_hist, tile, width = hist_ref.shape

    @pl.when(pl.program_id(0) == 0)
    def _():
        gain_grad_ref[...] = jnp.zeros_like(gain_grad_ref)

    def group(span):
        stat = stat_ref[span, :]
        sums = jnp.zeros((GROUP, LANES), F32)
        pieces = [pl.ds(w * LANES, LANES) for w in range(width // LANES)]
        grads = []
        for s, x in enumerate((x0, x1, x2)):
            scaled, dots = [], []
            for p in pieces:
                d = own[s, span, p] + up[s, span, p].astype(F32) + down[s, span, p].astype(F32)
                product = d * hat_of(x[span, p], stat, s)
                gain = gain_ref[pl.ds(s, 1), p]
                gain_grad_ref[s, :, p] += jnp.sum(product.reshape(GROUP // 8, 8, LANES), axis=0)
                scaled.append(d * gain)
                dots.append(product * gain)
                grad_refs[s][span, p] = scaled[-1]
            sums = put_lane(sums, s * SLOT + n_hist, row_sum(sum(scaled[1:], scaled[0])))
            sums = put_lane(sums, s * SLOT + n_hist + 1, row_sum(sum(dots[1:], dots[0])))
            grads.append(scaled)
        grads.append([resid_ref[span, p] for p in pieces])
        for j in range(n_hist):
            layer = [hist_ref[j, span, p].astype(F32) for p in pieces]
            for s in range(4):
                terms = [x * y for x, y in zip(grads[s], layer)]
                sums = put_lane(sums, s * SLOT + j, row_sum(sum(terms[1:], terms[0])))
        acc_ref[span, :] = sums

    by_groups(tile, group)
    sums_ref[...] = acc_ref[...].T[: sums_ref.shape[0]]


def late_dots(history, streams, stat, gain, resid_grad, own, came, chunk):
    n_hist, tokens, width = history.shape
    rows = stat.shape[0]
    base = chunk * rows // TILE
    wide = pl.BlockSpec((TILE, width), lambda i: (i, 0))
    three = pl.BlockSpec((3, TILE, width), lambda i: (0, i, 0))
    return pl.pallas_call(
        late_kernel,
        grid=(rows // TILE,),
        in_specs=[
            pl.BlockSpec((n_hist, TILE, width), lambda i: (0, base + i, 0)),
            wide,
            wide,
            wide,
            pl.BlockSpec((TILE, LANES), lambda i: (i, 0)),
            pl.BlockSpec((3, width), lambda i: (0, 0)),
            wide,
            three,
            three,
            three,
        ],
        out_specs=[
            wide,
            wide,
            wide,
            pl.BlockSpec((4 * SLOT, TILE), lambda i: (0, i)),
            pl.BlockSpec((3, 8, width), lambda i: (0, 0, 0)),
        ],
        out_shape=[jax.ShapeDtypeStruct((rows, width), F32)] * 3
        + [
            jax.ShapeDtypeStruct((4 * SLOT, rows), F32),
            jax.ShapeDtypeStruct((3, 8, width), F32),
        ],
        scratch_shapes=[pltpu.VMEM((TILE, LANES), F32)],
        compiler_params=pltpu.CompilerParams(vmem_limit_bytes=VMEM_MOST),
        name="late_dots",
    )(history, *streams, stat, gain, resid_grad, own, *came)


def layers_kernel(coef_ref, x0, x1, x2, stat_ref, mean_ref, d0, d1, d2, resid_ref, extra_ref, *refs):
    out_ref = refs[-1]
    n_hist, tile, width = out_ref.shape

    def group(span):
        stat, coef, means = stat_ref[span, :], coef_ref[span, :], mean_ref[span, :]
        cols = [spread(coef, i) for i in range(4 * n_hist)]
        for w in range(width // LANES):
            p = pl.ds(w * LANES, LANES)
            grads = []
            for s, (x, d) in enumerate(((x0, d0), (x1, d1), (x2, d2))):
                hat = hat_of(x[span, p], stat, s)
                grads.append(
                    spread(stat, 3 + s) * (d[span, p] - spread(means, MEAN_ROW + s) - hat * spread(means, MEAN_ROW + 3 + s))
                )
            grads.append(resid_ref[span, p])
            for j in range(n_hist):
                total = extra_ref[span, p] if j == n_hist - 1 else 0.0
                for s in range(4):
                    total = total + cols[s * n_hist + j] * grads[s]
                out_ref[j, span, p] = total.astype(BF16)

    by_groups(tile, group)


def layer_grads(coef, streams, stat, means, scaled, resid_grad, extra, chunk, held, tokens, others):
    rows, width = resid_grad.shape
    n_hist = coef.shape[1] // 4
    base = chunk * rows // TILE
    wide = pl.BlockSpec((TILE, width), lambda i: (i, 0))
    narrow = pl.BlockSpec((TILE, LANES), lambda i: (i, 0))
    free = [*others] + ([] if held is None else [held])
    return pl.pallas_call(
        layers_kernel,
        grid=(rows // TILE,),
        in_specs=[
            pl.BlockSpec((TILE, 4 * n_hist), lambda i: (base + i, 0)),
            wide,
            wide,
            wide,
            narrow,
            narrow,
            wide,
            wide,
            wide,
            wide,
            wide,
        ]
        + [pl.BlockSpec(memory_space=pl.ANY)] * len(free),
        out_specs=pl.BlockSpec((n_hist, TILE, width), lambda i: (0, base + i, 0)),
        out_shape=jax.ShapeDtypeStruct((n_hist, tokens, width), BF16),
        input_output_aliases={} if held is None else {11 + len(others): 0},
        compiler_params=pltpu.CompilerParams(vmem_limit_bytes=32 * 2**20),
        name="layer_grads",
    )(coef, *streams, stat, means, *scaled, resid_grad, extra, *free)


def coef_kernel(full_width, n_hist, early, late, stat, act, slope, raw, scale, mix_out, mix_in, last, out_part, in_part, turned_ref, extra_ref, pack):
    rows = late.shape[1]
    mixh = act.shape[0]
    inside = lax.broadcasted_iota(jnp.int32, (SLOT, rows), 0) < n_hist
    pack[...] = jnp.zeros_like(pack)
    slots = []
    for s in range(3):
        mean = late[pl.ds(s * SLOT + n_hist, 1), :] * (1.0 / full_width)
        mean_hat = late[pl.ds(s * SLOT + n_hist + 1, 1), :] * (1.0 / full_width)
        pack[pl.ds(MEAN_ROW + s, 1), :] = mean
        pack[pl.ds(MEAN_ROW + 3 + s, 1), :] = mean_hat
        slot = inv_std(stat[pl.ds(3 + s, 1), :], full_width) * (
            late[pl.ds(s * SLOT, SLOT), :]
            - mean * early[pl.ds(0, SLOT), :]
            - mean_hat * early[pl.ds((s + 1) * SLOT, SLOT), :]
        )
        slots.append(jnp.where(inside, slot, 0.0))
    slots.append(jnp.where(inside, late[pl.ds(3 * SLOT, SLOT), :], 0.0))
    d_coef = jnp.concatenate(slots, axis=0)
    ones = jnp.ones((8, rows), F32)
    out_part[pl.ds(0, mixh), :] = dot_tt(act[...], d_coef, ((1,), (1,)), HIGH)
    out_part[pl.ds(SCALE_ROW, 8), :] = dot_tt(ones, d_coef, ((1,), (1,)), HIGH)
    d_pre = dot_tt(mix_out[...], d_coef, ((1,), (0,)), HIGH) * slope[...]
    d_raw = d_pre * scale[...]
    in_part[...] = dot_tt(d_raw, last[...].astype(F32), ((1,), (0,)), HIGH)
    pack[pl.ds(0, mixh), :] = d_raw
    pack[pl.ds(SCALE_ROW, 1), :] = (
        scale[...] * scale[...] * scale[...] * (1.0 / full_width)
        * jnp.sum(d_pre * raw[...], axis=0, keepdims=True)
    )
    turned = pack[...].T
    turned_ref[...] = turned
    back = dot_tt(turned, mix_in[...], ((1,), (1,)), HIGH)
    extra_ref[...] = back - turned[:, SCALE_ROW : SCALE_ROW + 1] * last[...].astype(F32)


def coef_grads(full_width, n_hist, early, late, stat, act, slope, raw, scale, mix_out, mix_in, last, chunk):
    width = last.shape[1]
    rows = late.shape[1]
    mixh = act.shape[0]

    def full(array):
        return pl.BlockSpec(array.shape, lambda i: (0,) * array.ndim)

    def part(array):
        return pl.BlockSpec((array.shape[0], rows), lambda i: (0, chunk))

    arrays = [early, late, stat, act, slope, raw, scale, mix_out, mix_in]
    outs = [
        jax.ShapeDtypeStruct((SCALE_ROW + 8, 4 * SLOT), F32),
        jax.ShapeDtypeStruct((mixh, width), F32),
        jax.ShapeDtypeStruct((rows, LANES), F32),
        jax.ShapeDtypeStruct((rows, width), F32),
    ]
    return pl.pallas_call(
        functools.partial(coef_kernel, full_width, n_hist),
        grid=(1,),
        in_specs=[part(early)]
        + [full(a) for a in arrays[1:3]]
        + [part(a) for a in arrays[3:7]]
        + [full(a) for a in arrays[7:]]
        + [pl.BlockSpec((rows, width), lambda i: (chunk, 0))],
        out_specs=[full(a) for a in outs],
        out_shape=outs,
        scratch_shapes=[pltpu.VMEM((LANES, rows), F32)],
        compiler_params=pltpu.CompilerParams(vmem_limit_bytes=32 * 2**20),
        name="coef_grads",
    )(*arrays, last)


def send_kernel(count, turns, has_came, member_ref, *refs):
    lhs, refs = refs[:count], refs[count:]
    weights, refs = refs[: len(turns)], refs[len(turns) :]
    came, outs = (refs[:2], refs[2:]) if has_came else ((), refs)
    for k in range(len(turns)):
        for s in range(count):
            value = times_transpose(lhs[s][...], weights[k][s])
            if has_came:
                for got in came if len(turns) == 1 else (came[k],):
                    value = value + got[s].astype(F32)
            outs[k][s] = value.astype(outs[k].dtype)


def send_values(member, lhs, weight, turns, came, kind=BF16):
    n = lax.axis_size("stream")
    count = len(lhs)
    rows, depth = lhs[0].shape
    width = weight.shape[1] // n
    tile = 256
    piece = pl.BlockSpec((count, tile, width), lambda i, m: (0, i, 0))

    def block(turn):
        return pl.BlockSpec((count, width, depth), lambda i, m: (0, lax.rem(m[0] + turn, n), 0))

    return pl.pallas_call(
        functools.partial(send_kernel, count, turns, came is not None),
        grid_spec=pltpu.PrefetchScalarGridSpec(
            num_scalar_prefetch=1,
            grid=(rows // tile,),
            in_specs=[pl.BlockSpec((tile, depth), lambda i, m: (i, 0))] * count
            + [block(turn) for turn in turns]
            + ([] if came is None else [piece] * 2),
            out_specs=[piece] * len(turns),
        ),
        out_shape=[jax.ShapeDtypeStruct((count, rows, width), kind)] * len(turns),
        compiler_params=pltpu.CompilerParams(vmem_limit_bytes=48 * 2**20),
        name="send_values",
    )(member, *lhs, *([weight] * len(turns)), *(came or ()))


def columns(rows_values):
    return jnp.concatenate([rows_values, jnp.zeros((TILE - 8, TILE), F32)], axis=0).T


def inv_std(squares, full_width):
    return lax.rsqrt(squares * (1.0 / full_width) + EPS_NORM)


def norm_kernel(full_width, x0, x1, x2, moment_ref, gain_ref, qk_ref, v_ref, stat_ref):
    row = lax.broadcasted_iota(jnp.int32, (8, TILE), 0)
    moments = moment_ref[...]
    stat = columns(jnp.where(row < 3, moments, inv_std(moments, full_width)))
    stat_ref[...] = stat
    for s, x in enumerate((x0, x1, x2)):
        hat = (x[...] - stat[:, s : s + 1]) * stat[:, 3 + s : 4 + s]
        value = (hat * gain_ref[pl.ds(s, 1), :]).astype(BF16)
        if s < 2:
            qk_ref[s] = value
        else:
            v_ref[...] = value


def norm_streams(full_width, streams, moments, gain):
    rows, width = streams[0].shape
    wide = pl.BlockSpec((TILE, width), lambda i: (i, 0))
    return pl.pallas_call(
        functools.partial(norm_kernel, full_width),
        grid=(rows // TILE,),
        in_specs=[
            wide,
            wide,
            wide,
            pl.BlockSpec((8, TILE), lambda i: (0, i)),
            pl.BlockSpec((3, width), lambda i: (0, 0)),
        ],
        out_specs=[
            pl.BlockSpec((2, TILE, width), lambda i: (0, i, 0)),
            wide,
            pl.BlockSpec((TILE, LANES), lambda i: (i, 0)),
        ],
        out_shape=[
            jax.ShapeDtypeStruct((2, rows, width), BF16),
            jax.ShapeDtypeStruct((rows, width), BF16),
            jax.ShapeDtypeStruct((rows, LANES), F32),
        ],
        compiler_params=pltpu.CompilerParams(vmem_limit_bytes=32 * 2**20),
        name="norm_streams",
    )(*streams, moments, gain)


def residual_kernel(member_ref, own, up, down, base, out_ref, low_ref, stat_ref):
    width = own.shape[1]
    value = base[...] + own[...] + up[...].astype(F32) + down[...].astype(F32)
    out_ref[...] = value
    pivot = value[:, :1]
    gap = value - pivot
    shift = row_sum(gap) * (1.0 / width)
    low_ref[...] = (gap - shift).astype(BF16)
    acc = put_lane(jnp.zeros((TILE, LANES), F32), member_ref[0], pivot + shift)
    square = row_sum(jnp.square(gap)) - shift * shift * width
    acc = put_lane(acc, 4 + member_ref[0], square)
    stat_ref[...] = acc.T[:8]


def residual_rows(member, own, up, down, base):
    rows, width = own.shape
    assert lax.axis_size("stream") == 4
    wide = pl.BlockSpec((TILE, width), lambda i, m: (i, 0))
    return pl.pallas_call(
        residual_kernel,
        grid_spec=pltpu.PrefetchScalarGridSpec(
            num_scalar_prefetch=1,
            grid=(rows // TILE,),
            in_specs=[wide] * 4,
            out_specs=[wide, wide, pl.BlockSpec((8, TILE), lambda i, m: (0, i))],
        ),
        out_shape=[
            jax.ShapeDtypeStruct((rows, width), F32),
            jax.ShapeDtypeStruct((rows, width), BF16),
            jax.ShapeDtypeStruct((8, rows), F32),
        ],
        compiler_params=pltpu.CompilerParams(vmem_limit_bytes=32 * 2**20),
        name="residual_rows",
    )(member, own, up, down, base)


def by_member(member_ref, pieces, store):
    n = (len(pieces) + 1) // 2
    low, high = (None, *pieces[1:n]), (None, *pieces[n:])
    for at in range(n):

        @pl.when(member_ref[0] == at)
        def _():
            for slot in range(n):
                if slot == at:
                    store(slot, pieces[0])
                elif slot < at:
                    store(slot, low[at - slot])
                else:
                    store(slot, high[slot - at])


def normed_kernel(full_width, member_ref, *refs):
    pieces, (stat_ref, gain_ref, out_ref, moment_ref) = refs[:-4], refs[-4:]
    n = (len(pieces) + 1) // 2
    width = pieces[0].shape[1]
    stat = stat_ref[...]
    mean = jnp.sum(stat[:n], axis=0, keepdims=True) * (1.0 / n)
    gaps = stat[:n] - mean
    square = jnp.sum(stat[n:], axis=0, keepdims=True) + width * jnp.sum(
        jnp.square(gaps), axis=0, keepdims=True
    )
    moment_ref[...] = jnp.concatenate([mean, square, jnp.zeros((6, TILE), F32)], axis=0)
    table = columns(
        jnp.concatenate([gaps, inv_std(square, full_width), jnp.zeros((3, TILE), F32)], axis=0)
    )

    def store(slot, ref):
        cols = pl.ds(slot * width, width)
        hat = (ref[...].astype(F32) + table[:, slot : slot + 1]) * table[:, n : n + 1]
        out_ref[:, cols] = (hat * gain_ref[:, cols]).astype(BF16)

    by_member(member_ref, pieces, store)


def normed_rows(full_width, member, chain, stat, gain):
    pieces = [chain.piece, *chain.low[1:], *chain.high[1:]]
    rows, width = chain.piece.shape
    wide = pl.BlockSpec((TILE, width), lambda i, m: (i, 0))
    narrow = pl.BlockSpec((8, TILE), lambda i, m: (0, i))
    return pl.pallas_call(
        functools.partial(normed_kernel, full_width),
        grid_spec=pltpu.PrefetchScalarGridSpec(
            num_scalar_prefetch=1,
            grid=(rows // TILE,),
            in_specs=[wide] * len(pieces)
            + [narrow, pl.BlockSpec((1, full_width), lambda i, m: (0, 0))],
            out_specs=[pl.BlockSpec((TILE, full_width), lambda i, m: (i, 0)), narrow],
        ),
        out_shape=[
            jax.ShapeDtypeStruct((rows, full_width), BF16),
            jax.ShapeDtypeStruct((8, rows), F32),
        ],
        compiler_params=pltpu.CompilerParams(vmem_limit_bytes=32 * 2**20),
        name="normed_rows",
    )(member, *pieces, stat, gain)


def branch_kernel(full_width, member_ref, *refs):
    pieces, (stat_ref, sums_ref, normed_ref, gain_ref, out_ref) = refs[:-5], refs[-5:]
    width = pieces[0].shape[1]
    inv = inv_std(columns(stat_ref[...])[:, 1:2], full_width)
    sums = columns(sums_ref[...]) * (1.0 / full_width)
    mean, slope = inv * sums[:, :1], inv * sums[:, 1:2]

    def store(slot, ref):
        cols = pl.ds(slot * width, width)
        hat = normed_ref[:, cols].astype(F32) / gain_ref[:, cols]
        out_ref[:, cols] = (ref[...].astype(F32) - mean - hat * slope).astype(BF16)

    by_member(member_ref, pieces, store)


def branch_rows(full_width, member, chain, stat, sums, normed, gain):
    pieces = [chain.piece, *chain.low[1:], *chain.high[1:]]
    rows, width = chain.piece.shape
    wide = pl.BlockSpec((TILE, width), lambda i, m: (i, 0))
    narrow = pl.BlockSpec((8, TILE), lambda i, m: (0, i))
    whole = pl.BlockSpec((TILE, full_width), lambda i, m: (i, 0))
    return pl.pallas_call(
        functools.partial(branch_kernel, full_width),
        grid_spec=pltpu.PrefetchScalarGridSpec(
            num_scalar_prefetch=1,
            grid=(rows // TILE,),
            in_specs=[wide] * len(pieces)
            + [narrow, narrow, whole, pl.BlockSpec((1, full_width), lambda i, m: (0, 0))],
            out_specs=whole,
        ),
        out_shape=jax.ShapeDtypeStruct((rows, full_width), BF16),
        compiler_params=pltpu.CompilerParams(vmem_limit_bytes=32 * 2**20),
        name="branch_rows",
    )(member, *pieces, stat, sums, normed, gain)


def mlp_back_kernel(full_width, own, up, down, x, stat_ref, gain_ref, cot, out_ref, low_ref, sums_ref, gain_grad_ref):
    @pl.when(pl.program_id(0) == 0)
    def _():
        gain_grad_ref[...] = jnp.zeros_like(gain_grad_ref)

    stat = columns(stat_ref[...])
    grad = own[...] + up[...].astype(F32) + down[...].astype(F32)
    out_ref[...] = grad
    inv = inv_std(stat[:, 1:2], full_width)
    product = grad * ((x[...] - stat[:, :1]) * inv)
    low_ref[...] = (cot[...] + inv * (grad * gain_ref[...])).astype(BF16)
    gain_grad_ref[...] += jnp.sum(product.reshape(TILE // 8, 8, -1), axis=0)
    acc = put_lane(jnp.zeros((TILE, LANES), F32), 0, row_sum(grad * gain_ref[...]))
    acc = put_lane(acc, 1, row_sum(product * gain_ref[...]))
    sums_ref[...] = acc.T[:8]


def mlp_back_rows(full_width, own, up, down, residual, stat, gain, cot):
    rows, width = residual.shape
    wide = pl.BlockSpec((TILE, width), lambda i: (i, 0))
    narrow = pl.BlockSpec((8, TILE), lambda i: (0, i))
    return pl.pallas_call(
        functools.partial(mlp_back_kernel, full_width),
        grid=(rows // TILE,),
        in_specs=[wide] * 4 + [narrow, pl.BlockSpec((1, width), lambda i: (0, 0)), wide],
        out_specs=[wide, wide, narrow, pl.BlockSpec((8, width), lambda i: (0, 0))],
        out_shape=[
            jax.ShapeDtypeStruct((rows, width), F32),
            jax.ShapeDtypeStruct((rows, width), BF16),
            jax.ShapeDtypeStruct((8, rows), F32),
            jax.ShapeDtypeStruct((8, width), F32),
        ],
        compiler_params=pltpu.CompilerParams(vmem_limit_bytes=32 * 2**20),
        name="mlp_back_rows",
    )(own, up, down, residual, stat, gain, cot)


def resid_grad_kernel(full_width, grad, x, stat_ref, sums_ref, gain_ref, cot, out_ref):
    stat = columns(stat_ref[...])
    sums = columns(sums_ref[...]) * (1.0 / full_width)
    inv = inv_std(stat[:, 1:2], full_width)
    hat = (x[...] - stat[:, :1]) * inv
    value = cot[...] + inv * (grad[...] * gain_ref[...] - sums[:, :1] - hat * sums[:, 1:2])
    out_ref[...] = value


def resid_grad_rows(full_width, grad, residual, stat, sums, gain, cot):
    rows, width = residual.shape
    wide = pl.BlockSpec((TILE, width), lambda i: (i, 0))
    narrow = pl.BlockSpec((8, TILE), lambda i: (0, i))
    return pl.pallas_call(
        functools.partial(resid_grad_kernel, full_width),
        grid=(rows // TILE,),
        in_specs=[wide, wide, narrow, narrow, pl.BlockSpec((1, width), lambda i: (0, 0)), wide],
        out_specs=wide,
        out_shape=jax.ShapeDtypeStruct((rows, width), F32),
        compiler_params=pltpu.CompilerParams(vmem_limit_bytes=32 * 2**20),
        name="resid_grad_rows",
    )(grad, residual, stat, sums, gain, cot)


def rows_product_kernel(n, *refs):
    former, latter, out_ref = refs[:n], refs[n : 2 * n], refs[-1]
    total = 0.0
    for c in range(n):
        total = total + contract_rows(former[c][...], latter[c][...])
    out_ref[...] = total.astype(BF16)


def rows_product(former, latter, out_cols, first, held, others=(), slot=None, half=None):
    n = len(former)
    rows, height = former[0].shape[-2:]
    width = latter[0].shape[1]
    skip = 0
    if half is not None:
        width //= 2
        out_cols //= 2
    tile_m, tile_n = min(512 if width > 512 else 1024, height), min(2048, width)
    begin = first // tile_n
    if half:
        skip = width // tile_n
    free = [*others] + ([] if held is None else [held])
    return pl.pallas_call(
        functools.partial(rows_product_kernel, n),
        grid=(height // tile_m, width // tile_n),
        in_specs=[
            pl.BlockSpec((rows, tile_m), lambda i, j: (0, i))
            if slot is None
            else pl.BlockSpec((None, rows, tile_m), lambda i, j: (slot, 0, i))
        ]
        * n
        + [pl.BlockSpec((rows, tile_n), lambda i, j: (0, skip + j))] * n
        + [pl.BlockSpec(memory_space=pl.ANY)] * len(free),
        out_specs=pl.BlockSpec((tile_m, tile_n), lambda i, j: (i, begin + j)),
        out_shape=jax.ShapeDtypeStruct((height, out_cols), BF16),
        input_output_aliases={} if held is None else {2 * n + len(others): 0},
        compiler_params=pltpu.CompilerParams(vmem_limit_bytes=48 * 2**20),
        name="rows_product",
    )(*former, *latter, *free)


def local(
    history,
    mix_in,
    mix_out,
    mix_static,
    stream_gain,
    qkv_weight,
    out_weight,
    mlp_gain,
    up_weight,
    down_weight,
    out_grad,
    seq_group,
    group_weight,
):
    n_stream = lax.axis_size("stream")
    member = lax.axis_index("stream")
    n_hist, tokens, width = history.shape
    assert tokens == SEQ
    full_width = width * n_stream
    rows = tokens // CHUNKS
    both = range(CHUNKS)
    spans = [slice(c * rows, (c + 1) * rows) for c in both]
    first_col = member * width
    mixh = mix_in.shape[1]
    ff = up_weight.shape[1]
    order = Order()

    def rows_of(weight, idx):
        begin = lax.rem(member + idx, n_stream) * width
        return lax.dynamic_slice_in_dim(weight, begin, width, 0)

    def dp_sum(part):
        return lax.psum_scatter(part, "dp", scatter_dimension=0, tiled=True).astype(F32)

    mix_in_rows = lax.dynamic_slice_in_dim(mix_in, first_col, width, 0)
    mix_out_float = mix_out.astype(F32)

    last = history[n_hist - 1]
    square_part = jnp.sum(jnp.square(last.astype(F32)), axis=1)[None]
    raw_part = dot_tt(mix_in_rows, last, ((0,), (1,)))
    raw = Butterfly(jnp.concatenate([raw_part, square_part], axis=0))
    order.send(raw)

    here = member.astype(jnp.int32).reshape(1)
    qkv_rows = jnp.transpose(order.hold(qkv_weight), (1, 0, 2))
    order.did(qkv_rows)

    group_pick = (
        seq_group[:, None] == jnp.arange(group_weight.shape[0], dtype=jnp.int32)[None, :]
    ).astype(F32)
    seq_weight = jnp.sum(group_pick * group_weight.astype(F32)[None, :]) * COT_SCALE
    out_grad_held = order.hold(out_grad)
    cot_cols = [out_grad_held[spans[c]].astype(F32) * seq_weight for c in both]
    cot = [LineGather(cot_cols[c].astype(BF16), member) for c in both]
    order.did(cot[0].piece, cot[1].piece)
    order.send(raw)
    order.send(cot[0])

    sums = raw.value()
    raw_t = sums[:-1]
    scale_t = lax.rsqrt(sums[-1:] / full_width + EPS_MIX)
    act_t, slope_t = gelu_both(scale_t * raw_t)
    coef = (dot_tt(mix_out_float, act_t, ((0,), (0,)), HIGH) + mix_static.reshape(-1, 1)).T

    streams, moments = [None] * 2, [None] * 2
    stat, stat_rows, normed_chain = [None] * 2, [None] * 2, [None] * 2
    resid_streams, early_chain = [None] * 2, []

    def mix(c):
        *streams[c], sums = mix_streams(history, coef, c, (0, 1, 2), True)
        moments[c] = Butterfly(sums, merge=moments_merger(width, 3))

    def norm(c):
        stat_rows[c] = moments[c].value()
        pair, single, stat[c] = norm_streams(full_width, streams[c], stat_rows[c], stream_gain)
        normed_chain[c] = [LineGather(pair, member), LineGather(single, member)]

    def early(c):
        sums = early_dots(history, [order.hold(streams[c][0]), *streams[c][1:]], stat[c], c)
        order.did(sums)
        early_chain.append(Butterfly(sums))

    def mix_resid(c):
        (resid_streams[c],) = mix_streams(history, order.hold(coef), c, (3,), False)
        order.did(resid_streams[c])

    mix(0)
    mix(1)
    order.send(*moments)
    order.send(*moments)
    norm(0)
    order.send(normed_chain[0][0])
    order.send(normed_chain[0][1])
    norm(1)
    order.did(normed_chain[1][0].piece)
    mix_resid(0)
    order.send(normed_chain[0][0])
    order.send(normed_chain[0][1])
    early(0)
    order.send(normed_chain[0][0])
    order.send(normed_chain[0][1])
    mix_resid(1)
    order.send(normed_chain[1][0])
    order.send(normed_chain[1][1])

    normed, query, key, value, heads_out, lse = [], [], [], [], [], []
    branch = []

    def project(c):
        normed.append([chain.value() for chain in normed_chain[c]])
        for held, s, full in ((query, 0, normed[c][0][0]), (key, 1, normed[c][0][1]), (value, 2, normed[c][1])):
            held.append(jnp.dot(full, qkv_rows[s], preferred_element_type=F32).astype(BF16))

    def attend(c):
        out, out_lse = attend_forward(query[c], key[: c + 1], value[: c + 1])
        heads_out.append(out)
        lse.append(out_lse)
        branch.append(
            LineScatter(
                order, lambda idx, hold: times_transpose(hold(out), rows_of(out_weight, idx))
            )
        )

    residual, resid_moments = [], []
    mlp_gain_cols = lax.dynamic_slice_in_dim(mlp_gain, first_col, width, 0)[None, :]
    mlp_in, mlp_moments = [], []
    normed_mlp, hidden, d_hpre, mlp_back, mlp_out = [], [], [], [], []

    def end_branch(c):
        value, low, stats = residual_rows(here, *branch[c].pieces(), resid_streams[c])
        residual.append(value)
        resid_moments.append(Butterfly(stats))
        mlp_in.append(LineGather(low, member))

    cot_low, d_hidden = [], []

    def down_back(c):
        cot_low.append(cot[c].value())
        d_hidden.append(
            jnp.dot(order.hold(cot_low[c]), down_weight, preferred_element_type=F32)
        )
        order.did(d_hidden[c])

    def mlp(c):
        full, moments_all = normed_rows(
            full_width, here, mlp_in[c], resid_moments[c].value(), mlp_gain[None, :]
        )
        normed_mlp.append(full)
        mlp_moments.append(moments_all)
        hidden_pre = jnp.dot(normed_mlp[c], up_weight, preferred_element_type=F32)
        act, slope = gelu_both(hidden_pre)
        act = act.astype(BF16)
        d_pre = (d_hidden[c] * slope).astype(BF16)
        hidden.append(act)
        d_hpre.append(d_pre)
        mlp_back.append(
            LineScatter(
                order, lambda idx, hold: times_transpose(hold(d_pre), rows_of(up_weight, idx))
            )
        )
        mlp_out.append(
            LineScatter(
                order, lambda idx, hold: times_transpose(hold(act), rows_of(down_weight, idx))
            )
        )

    def weight_part(former, latter, out_cols, others):
        return rows_product(former, latter, out_cols, 0, None, others)

    d_normed_mlp, back_sums, mlp_gain_shares = [], [], []

    resid_grad, branch_grad = [], []

    def end_mlp_back(c):
        value, low, sums, share = mlp_back_rows(
            full_width, *mlp_back[c].pieces(), residual[c], mlp_moments[c], mlp_gain_cols,
            cot_cols[c],
        )
        d_normed_mlp.append(value)
        back_sums.append(Butterfly(sums))
        mlp_gain_shares.append(share)
        branch_grad.append(LineGather(low, member))

    d_branch, d_proj = [], []
    carried = [None]

    def attend_back(c):
        sums = back_sums[c].value()
        d_branch.append(
            branch_rows(
                full_width, here, branch_grad[c], mlp_moments[c], sums, normed_mlp[c],
                mlp_gain[None, :],
            )
        )
        resid_grad.append(
            resid_grad_rows(
                full_width, d_normed_mlp[c], residual[c], mlp_moments[c], sums, mlp_gain_cols,
                cot_cols[c],
            )
        )
        d_heads = jnp.dot(d_branch[c], out_weight, preferred_element_type=F32).astype(BF16)
        d_query, dk, dv = attend_backward(
            query[c], d_heads, lse[c], key[: c + 1], value[: c + 1], carried[0], c == CHUNKS - 1
        )
        carried[0] = (dk, dv)
        d_proj.append([d_query, None, None])
        if c == CHUNKS - 1:
            for i in both:
                d_proj[i][1:] = [dk[i], dv[i]]

    project(0)
    attend(0)
    order.send(branch[0])
    branch[0].prepare()
    order.send(normed_chain[1][0])
    order.send(branch[0])
    branch[0].prepare()
    order.send(normed_chain[1][1])
    early(1)
    order.send(branch[0])
    branch[0].prepare()
    order.send(normed_chain[1][0])
    order.send(normed_chain[1][1])
    end_branch(0)
    order.send(resid_moments[0], cot[0])
    project(1)
    order.send(resid_moments[0])
    order.send(cot[0])
    attend(1)
    order.send(branch[1], mlp_in[0])
    branch[1].prepare()
    down_back(0)
    order.send(branch[1], mlp_in[0])
    branch[1].prepare()
    order.send(branch[1], mlp_in[0])
    branch[1].prepare()
    order.send(cot[1])
    end_branch(1)
    order.send(mlp_in[1], resid_moments[1])
    mlp(0)
    order.send(cot[1])
    order.send(mlp_in[1], mlp_back[0], resid_moments[1])
    mlp_back[0].prepare()
    order.send(cot[1])
    order.send(mlp_in[1], mlp_back[0])
    mlp_back[0].prepare()
    down_back(1)
    order.send(mlp_back[0])
    mlp_back[0].prepare()
    mlp(1)
    end_mlp_back(0)
    order.send(mlp_back[1], branch_grad[0])
    mlp_back[1].prepare()
    down_part = weight_part(cot_low, hidden, ff, mlp_back[1].came)
    order.send(mlp_back[1], branch_grad[0], back_sums[0])
    up_came, down_came = mlp_back[1].came
    up_came, down_part = lax.optimization_barrier((up_came, down_part))
    mlp_back[1].came = [up_came, down_came]
    down_sum = lax.psum_scatter(down_part, "dp", scatter_dimension=0, tiled=True)
    mlp_back[1].prepare()
    order.send(mlp_back[1], branch_grad[0], back_sums[0])
    mlp_back[1].prepare()
    end_mlp_back(1)
    mlp_out[0].prepare()
    order.send(branch_grad[1], mlp_out[0])
    mlp_out[0].prepare()
    attend_back(0)
    order.send(branch_grad[1], mlp_out[0], back_sums[1])
    chain = branch_grad[1]
    chain.low[-1], chain.high[-1], d_proj[0][0] = lax.optimization_barrier(
        (chain.low[-1], chain.high[-1], d_proj[0][0])
    )
    mlp_out[0].prepare()
    order.send(branch_grad[1], mlp_out[0], back_sums[1])
    mlp_out[0].prepare()
    mlp_out[1].prepare()
    attend_back(1)
    order.send(mlp_out[1])
    mlp_out[1].prepare()

    grads = [ProductScatter(order, here, d_proj[c], qkv_rows) for c in both]
    own = [None] * 2
    early_one = Butterfly(jnp.concatenate([chain.now for chain in early_chain], axis=1))
    order.send(*grads, early_one)
    out_part = weight_part(d_branch, heads_out, width, (*grads[0].came, down_sum))
    up_part = weight_part(normed_mlp, d_hpre, ff, grads[0].came)
    order.send(*grads, early_one)
    qkv_part = None
    for s in range(3):
        qkv_part = rows_product(
            [normed[c][s // 2] for c in both], [d_proj[c][s] for c in both], 3 * width, s * width,
            qkv_part, grads[1].came, s if s < 2 else None,
        )
    order.send(*grads)
    down_grad = down_sum.astype(F32)
    own = [grads[c].own() for c in both]
    up_grad, out_weight_grad = [dp_sum(part) for part in (up_part, out_part)]
    qkv_sum = lax.psum_scatter(qkv_part, "dp", scatter_dimension=0, tiled=True)
    qkv_grad = jnp.stack(
        [qkv_sum[:, s * width : (s + 1) * width] for s in range(3)], axis=1
    ).astype(F32)
    gain_part = jnp.sum(mlp_gain_shares[0] + mlp_gain_shares[1], axis=0)
    gain_chain = Butterfly(
        jnp.where(
            jnp.arange(n_stream)[:, None] == member,
            gain_part[None, :],
            jnp.zeros((n_stream, width), F32),
        )
    )

    mix_out_wide = jnp.pad(
        mix_out_float.reshape(-1, 4, n_hist), ((0, 0), (0, 0), (0, SLOT - n_hist))
    ).reshape(-1, 4 * SLOT)
    mix_in_wide = jnp.pad(mix_in_rows.astype(F32), ((0, 0), (0, LANES - mixh)))
    d_normed, late, gain_shares, shares = [], [], [], []
    history_grad = [None]

    def late_sums(c):
        *scaled, sums, gain_share = late_dots(
            history, streams[c], stat[c], stream_gain, resid_grad[c], own[c], grads[c].came, c
        )
        d_normed.append(scaled)
        late.append(Butterfly(sums))
        gain_shares.append(gain_share)

    def coefs(c):
        shares.append(
            coef_grads(
                full_width, n_hist, early_one.value(), late[c].value(), stat_rows[c], act_t,
                slope_t, raw_t, scale_t, mix_out_wide, mix_in_wide, last, c,
            )
        )

    def layers(c, others):
        _, _, turned, extra = shares[c]
        history_grad[0] = layer_grads(
            coef, streams[c], stat[c], turned, d_normed[c], resid_grad[c], extra, c,
            history_grad[0], tokens, others,
        )
        order.did(history_grad[0])

    late_sums(0)
    order.did(qkv_part)
    order.send(late[0], gain_chain)
    order.send(mlp_out[1])
    mlp_out[1].prepare()
    late_sums(1)
    order.send(late[0], late[1], gain_chain)
    coefs(0)
    order.send(late[1])
    coefs(1)
    out_share, in_share = [shares[0][i] + shares[1][i] for i in range(2)]
    gain_share = jnp.sum(gain_shares[0] + gain_shares[1], axis=1)
    out_share = jnp.pad(out_share, ((0, 0), (0, width - 4 * SLOT)))
    small = Butterfly(
        jnp.concatenate([out_share, in_share, gain_share, gain_chain.value()], axis=0), ("dp",)
    )
    order.send(small)
    order.send(mlp_out[1])
    layers(0, (small.now,))
    layers(1, ())
    while small.turns:
        order.send(small)
    output_cols = jnp.concatenate(
        [(residual[c] + mlp_out[c].value()).astype(BF16) for c in both], axis=0
    )
    small = small.value()
    top = out_share.shape[0]
    by_slot = small[:top, : 4 * SLOT].reshape(-1, 4, SLOT)[:, :, :n_hist]
    return (
        output_cols,
        history_grad[0],
        small[top : top + mixh].T,
        by_slot[:mixh].reshape(mixh, 4 * n_hist),
        by_slot[SCALE_ROW],
        small[top + mixh : top + mixh + 3],
        qkv_grad,
        out_weight_grad,
        small[top + mixh + 3 :].reshape(full_width),
        up_grad,
        down_grad,
    )


def solution(mesh):
    in_specs = (
        P(None, "dp", "stream"),
        P(),
        P(),
        P(),
        P(None, "stream"),
        P(None, None, "stream"),
        P(None, "stream"),
        P(),
        P(None, "stream"),
        P(None, "stream"),
        P("dp", "stream"),
        P("dp"),
        P(),
    )
    out_specs = (
        P("dp", "stream"),
        P(None, "dp", "stream"),
        P("stream", None),
        P(),
        P(),
        P(None, "stream"),
        P("dp", None, "stream"),
        P("dp", "stream"),
        P(),
        P("dp", "stream"),
        P("dp", "stream"),
    )
    return jax.shard_map(local, mesh=mesh, in_specs=in_specs, out_specs=out_specs, check_vma=False)
```
